256 devices in a mesh: src: 64 (over x, y, z_lo, core), tgt: 4 (over z_hi).
Axes of the slice: x: 4, y: 4, z: 8 (z_hi: 4, z_lo: 2; z = z_hi * 2 + z_lo), core: 2. Of those that a mesh axis runs over, the one named last changes fastest.
Arguments:
- src_emb: bfloat16 [64, 65536], P(None, 'src'), may hold values from -6 to 6
- src_pos: float32 [2, 65536], P(None, 'src'), may hold values from 0 to 12
- src_logw: float32 [65536], P('src'), may hold values from -1 to 1
- tgt_emb: bfloat16 [64, 16384], P(None, ('src', 'tgt')), may hold values from -6 to 6
- tgt_pos: bfloat16 [2, 16384], P(None, ('src', 'tgt')), may hold values from 0 to 12
- tgt_logw: bfloat16 [16384], P(('src', 'tgt')), may hold values from -1 to 1
Outputs:
- src_potential: float32 [65536], P('src')
- tgt_potential: float32 [16384], P(('src', 'tgt'))
- feature_grad: float32 [64, 65536], P(None, 'src')
The draws below stay inside these ranges and needn't reach their ends.
All inputs are finite; a program needn't handle non-finite values.
Results may differ from the reference program's by a relative error of at most 0.0053.
Values may be sent and summed in bfloat16 or wider, within the bound.
No kernel may reach another device: no remote copies, remote signals or barrier semaphores. Data moves between devices by JAX's collectives and lax.ppermute only.
A program may use at most 64 MiB of HBM per device.

```python
import math
import jax
import jax.numpy as jnp
from jax import lax

EMB = 64
ITERS = 3
NS = 65536
NT = 16384


def source_layout(key):
    first, second, third = jax.random.split(jax.random.fold_in(key, 21), 3)
    base_x = jax.random.uniform(first, (NS,), jnp.float32, 0.0, 10.0)
    base_y = jax.random.uniform(second, (NS,), jnp.float32, 0.0, 3.0)
    order = jax.random.permutation(third, NS)
    remote = (order < NS // 16).astype(jnp.float32)
    return (base_x, base_y, remote)


def source_features(key):
    raw = jax.random.normal(jax.random.fold_in(key, 33), (EMB, NS), jnp.float32)
    return jnp.clip(2.0 * raw, -6.0, 6.0)


def partner_index():
    return jnp.arange(NT, dtype=jnp.int32) * 9973 % NS


def draw_src_emb(key, part):
    return source_features(key).astype(jnp.bfloat16)


def draw_tgt_emb(key, part):
    features = source_features(key)
    partner = partner_index()
    key = jax.random.fold_in(key, 13)
    noise = jax.random.normal(key, (EMB, NT), jnp.float32)
    return jnp.clip(features[:, partner] + 0.5 * noise, -6.0, 6.0).astype(jnp.bfloat16)


def draw_src_pos(key, part):
    base_x, base_y, remote = source_layout(key)
    key = jax.random.fold_in(key, 5)
    first, second = jax.random.split(key)
    lowest = 10.0
    far_x = jax.random.uniform(first, (NS,), jnp.float32, 0.0, 4.0)
    far_y = jax.random.uniform(second, (NS,), jnp.float32, lowest, 12.0)
    pos_x = base_x * (1.0 - remote) + far_x * remote
    pos_y = base_y * (1.0 - remote) + far_y * remote
    return jnp.stack([pos_x, pos_y], 0)


def draw_tgt_pos(key, part):
    base_x, base_y, remote_src = source_layout(key)
    partner = partner_index()
    key = jax.random.fold_in(key, 9)
    first, second, third = jax.random.split(key, 3)
    lowest = 10.0
    drift = jax.random.uniform(first, (2,), jnp.float32, 1.25, 1.5)
    order = jax.random.permutation(second, NT)
    remote = (order < NT // 16).astype(jnp.float32)
    far = jax.random.uniform(third, (2, NT), jnp.float32, lowest, 12.0)
    near = jnp.stack([base_x[partner] + drift[0], base_y[partner] + drift[1]], 0)
    field = near * (1.0 - remote[None, :]) + far * remote[None, :]
    return field.astype(jnp.bfloat16)


def block_scale(rng, shape, cuts, low, high):
    level, own = 1.0, jax.random.fold_in(rng, 6)
    for axis_at, shards_of in cuts:
        draws = jnp.exp(jax.random.uniform(jax.random.fold_in(own, axis_at), (shards_of,), jnp.float32, low / len(cuts), high / len(cuts)))
        level = level * jnp.repeat(draws, shape[axis_at] // shards_of).reshape([-1 if axis == axis_at else 1 for axis in range(len(shape))])
    return level


def setup_inputs(seed: int = 0) -> dict:
    keys = jax.random.split(jax.random.key(seed), 7)
    return {
        "src_emb": draw_src_emb(jax.random.fold_in(keys[6], 71), 0),
        "src_pos": draw_src_pos(jax.random.fold_in(keys[6], 71), 0),
        "src_logw": jnp.clip(jax.random.uniform(keys[2], (NS,), jnp.float32, -1.0, 1.0) * block_scale(keys[2], (NS,), ((0, 64),), -0.4, 0.0), -1.0, 1.0),
        "tgt_emb": draw_tgt_emb(jax.random.fold_in(keys[6], 71), 0),
        "tgt_pos": draw_tgt_pos(jax.random.fold_in(keys[6], 71), 0),
        "tgt_logw": jnp.clip(jax.random.uniform(keys[5], (NT,), jnp.float32, -1.0, 1.0) * block_scale(keys[5], (NT,), ((0, 256),), -0.4, 0.0), -1.0, 1.0).astype(jnp.bfloat16),
    }


eps_reg = 0.25
rho_reg = 2.0
damping = rho_reg / (rho_reg + eps_reg)


def cost_tile(src_emb, src_sq, src_pos, cols_emb, cols_pos):
    inner = lax.dot_general(src_emb, cols_emb, (((0,), (0,)), ((), ())), preferred_element_type=jnp.float32)
    cols_sq = jnp.sum(jnp.square(cols_emb.astype(jnp.float32)), axis=0)
    pos_f = cols_pos.astype(jnp.float32)
    delta_x = src_pos[0][:, None] - pos_f[0][None, :]
    delta_y = src_pos[1][:, None] - pos_f[1][None, :]
    return (src_sq[:, None] + cols_sq[None, :] - 2.0 * inner) / cols_emb.shape[0] + delta_x * delta_x + delta_y * delta_y


def reference(src_emb, src_pos, src_logw, tgt_emb, tgt_pos, tgt_logw):
    src_sq = jnp.sum(jnp.square(src_emb.astype(jnp.float32)), axis=0)
    width = math.gcd(NT, 1024)
    steps = NT // width
    logb = tgt_logw.astype(jnp.float32)

    def columns(index):
        begin = index * width
        return (lax.dynamic_slice_in_dim(tgt_emb, begin, width, 1), lax.dynamic_slice_in_dim(tgt_pos, begin, width, 1), lax.dynamic_slice_in_dim(logb, begin, width, 0))

    potential_g = jnp.zeros((NT,), jnp.float32)
    potential_f = jnp.zeros((NS,), jnp.float32)
    for step in range(ITERS):
        def row_step(state, index):
            cols_emb, cols_pos, cols_logb = columns(index)
            g_cols = lax.dynamic_slice_in_dim(potential_g, index * width, width, 0)
            cost = cost_tile(src_emb, src_sq, src_pos, cols_emb, cols_pos)
            score = cols_logb[None, :] + (g_cols[None, :] - cost) / eps_reg
            block_max = jnp.max(score, axis=1)
            top = jnp.maximum(state[0], block_max)
            total = state[1] * jnp.exp(state[0] - top) + jnp.sum(jnp.exp(score - top[:, None]), axis=1)
            return (top, total), None

        init = (jnp.full((NS,), -jnp.inf, jnp.float32), jnp.zeros((NS,), jnp.float32))
        (row_max, row_sum), unused = lax.scan(row_step, init, jnp.arange(steps, dtype=jnp.int32))
        potential_f = -damping * eps_reg * (row_max + jnp.log(row_sum))

        def col_block(index):
            cols_emb, cols_pos, cols_logb = columns(index)
            cost = cost_tile(src_emb, src_sq, src_pos, cols_emb, cols_pos)
            score = src_logw[:, None] + (potential_f[:, None] - cost) / eps_reg
            block_max = jnp.max(score, axis=0)
            return block_max + jnp.log(jnp.sum(jnp.exp(score - block_max[None, :]), axis=0))

        col_lse = lax.map(col_block, jnp.arange(steps, dtype=jnp.int32)).reshape(NT)
        potential_g = -damping * eps_reg * col_lse

    def plan_step(state, index):
        cols_emb, cols_pos, cols_logb = columns(index)
        g_cols = lax.dynamic_slice_in_dim(potential_g, index * width, width, 0)
        cost = cost_tile(src_emb, src_sq, src_pos, cols_emb, cols_pos)
        plan = jnp.exp(src_logw[:, None] + cols_logb[None, :] + (potential_f[:, None] + g_cols[None, :] - cost) / eps_reg)
        mass = state[0] + jnp.sum(plan, axis=1)
        pull = state[1] + lax.dot_general(cols_emb, plan.astype(jnp.bfloat16), (((1,), (1,)), ((), ())), preferred_element_type=jnp.float32)
        return (mass, pull), None

    init = (jnp.zeros((NS,), jnp.float32), jnp.zeros((EMB, NS), jnp.float32))
    (mass, pull), unused = lax.scan(plan_step, init, jnp.arange(steps, dtype=jnp.int32))
    feature_grad = mass[None, :] * src_emb.astype(jnp.float32) - pull
    return potential_f, potential_g, feature_grad
```

```python
import functools

import jax
import jax.numpy as jnp
from jax import lax
from jax.experimental import pallas as pl
from jax.experimental.pallas import tpu as pltpu
from jax.sharding import PartitionSpec as P

ITERS = 3
EPS = 0.25
RHO = 2.0
LAM = RHO / (RHO + EPS)
EMB = 64
DEPTH = 128
PACK = 80
MIB = 1 << 20
LOW, HIGH = 1e-25, 1e30


def pieces(value):
    high = value.astype(jnp.bfloat16).astype(jnp.float32)
    rest = value - high
    mid = rest.astype(jnp.bfloat16).astype(jnp.float32)
    low = (rest - mid).astype(jnp.bfloat16).astype(jnp.float32)
    return high, mid, low


def stacked(rows, height, width):
    index = lax.broadcasted_iota(jnp.int32, (height, width), 0)
    block = jnp.zeros((height, width), jnp.float32)
    for at, row in enumerate(rows):
        if row is not None:
            block = jnp.where(index == at, row, block)
    return block


def source_static(emb_ref, pos_ref, out_ref):
    width = emb_ref.shape[1]
    pos = pos_ref[...]
    emb = emb_ref[...].astype(jnp.float32)
    sq = jnp.sum(emb * emb, axis=0, keepdims=True)
    shift = -(sq * (1.0 / EMB) + pos[0:1] * pos[0:1] + pos[1:2] * pos[1:2]) * (1.0 / EPS)
    pos = pos * (2.0 / EPS)
    zero, one = jnp.zeros((1, width), jnp.float32), jnp.ones((1, width), jnp.float32)
    rows = [*pieces(pos[0:1]), *pieces(pos[1:2]), zero, zero, zero, one, one, one]
    extra = stacked(rows, 16, width)
    emb = emb * (2.0 / (EMB * EPS))
    pad = jnp.zeros((DEPTH - PACK, 128), jnp.float32)
    for at in range(0, width, 128):
        block = jnp.concatenate([emb[:, at : at + 128], extra[:, at : at + 128], pad], axis=0)
        out_ref[at : at + 128, :] = block.T.astype(jnp.bfloat16)
    return shift


def target_static(pack_ref, at, out_ref):
    width = pack_ref.shape[1]
    pack = pack_ref[...].astype(jnp.float32)
    emb, geo = pack[0:EMB], pack[EMB : EMB + 4]
    sq = jnp.sum(emb * emb, axis=0, keepdims=True)
    x, y = geo[0:1], geo[1:2]
    shift = -(sq * (1.0 / EMB) + x * x + y * y) * (1.0 / EPS)
    one = jnp.ones((1, width), jnp.float32)
    cut = slice(at, at + width)
    out_ref[0:EMB, cut] = pack_ref[0:EMB, :]
    out_ref[EMB:PACK, cut] = stacked([x, x, x, y, y, y, one, one, one], 16, width).astype(jnp.bfloat16)
    out_ref[PACK:DEPTH, cut] = jnp.zeros((DEPTH - PACK, width), jnp.bfloat16)
    return shift, geo[2:3]


def set_source(a_ref, shift, a_s):
    block = stacked([None] * 6 + [*pieces(shift)], 16, a_ref.shape[0])
    above = jnp.zeros((EMB, 128), jnp.float32)
    below = jnp.zeros((DEPTH - PACK, 128), jnp.float32)
    for at in range(0, a_ref.shape[0], 128):
        part = jnp.concatenate([above, block[:, at : at + 128], below], axis=0).T
        a_s[at : at + 128, :] = a_ref[at : at + 128, :] + part.astype(jnp.bfloat16)


def set_target(b_ref, shift, b_s):
    block = stacked([None] * 9 + [*pieces(shift)], 16, b_ref.shape[1])
    b_s[EMB:PACK, :] = (b_ref[EMB:PACK, :].astype(jnp.float32) + block).astype(jnp.bfloat16)


def copy_target(b_ref, b_s):
    b_s[0:EMB, :] = b_ref[0:EMB, :]
    b_s[PACK:DEPTH, :] = b_ref[PACK:DEPTH, :]


def score(a, b):
    return lax.dot_general(a, b, (((1,), (0,)), ((), ())), preferred_element_type=jnp.float32)


def row_sums(a_s, b_s, acc_s, tile):
    acc_s[...] = jnp.zeros_like(acc_s)

    def step(index, carry):
        cut = pl.ds(pl.multiple_of(index * tile, tile), tile)
        value = jnp.exp(score(a_s[...], b_s[:, cut]))
        part = value[:, 0:128]
        for col in range(128, tile, 128):
            part += value[:, col : col + 128]
        acc_s[...] += part
        return carry

    lax.fori_loop(0, b_s.shape[1] // tile, step, 0)


def row_tops(a_s, b_s, acc_s, tile, count):
    acc_s[...] = jnp.full(acc_s.shape, -jnp.inf, jnp.float32)

    def step(index, carry):
        cut = pl.ds(pl.multiple_of(index * tile, tile), tile)
        value = score(a_s[...], b_s[:, cut])
        part = value[:, 0:128]
        for col in range(128, tile, 128):
            part = jnp.maximum(part, value[:, col : col + 128])
        acc_s[...] = jnp.maximum(acc_s[...], part)
        return carry

    lax.fori_loop(0, count, step, 0)


def over_lanes(acc_s, out_s, join):
    for at in range(0, acc_s.shape[0], 128):
        out_s[:, at : at + 128] = join(acc_s[at : at + 128, :].T, axis=0, keepdims=True)


def in_range(total):
    return jnp.logical_and(jnp.min(total) > LOW, jnp.max(total) < HIGH)


def row_pass(a_ref, b_ref, r_ref, c, guess_ref, out_ref, a_s, b_s, acc_s, guess_s, total_s, tile):
    cols = b_ref.shape[1]
    copy_target(b_ref, b_s)
    set_target(b_ref, c, b_s)

    def about_tops(count):
        set_source(a_ref, r_ref[...], a_s)
        row_tops(a_s, b_s, acc_s, tile, count)
        over_lanes(acc_s, guess_s, jnp.max)

    def sums():
        set_source(a_ref, r_ref[...] - guess_s[...], a_s)
        row_sums(a_s, b_s, acc_s, tile)
        over_lanes(acc_s, total_s, jnp.sum)

    if guess_ref is None:
        about_tops(1)
    else:
        guess_s[...] = guess_ref[...]
    sums()

    @pl.when(jnp.logical_not(in_range(total_s[...])))
    def _():
        about_tops(cols // tile)
        sums()

    out_ref[...] = guess_s[...] + jnp.log(total_s[...])


def first_kernel(emb_ref, pos_ref, own_ref, other_ref, out_ref, a_ref, b_ref, r_ref, c_ref, w_ref, a_s, b_s, acc_s, guess_s, total_s, *, tile):
    half = own_ref.shape[1]
    r_ref[...] = source_static(emb_ref, pos_ref, a_ref)
    c_ref[:, 0:half], w_ref[:, 0:half] = target_static(own_ref, 0, b_ref)
    c_ref[:, half:], w_ref[:, half:] = target_static(other_ref, half, b_ref)
    row_pass(a_ref, b_ref, r_ref, c_ref[...] + w_ref[...], None, out_ref, a_s, b_s, acc_s, guess_s, total_s, tile)


def target_shift(c_ref, w_ref, own_ref, other_ref):
    lse = jnp.concatenate([own_ref[...], other_ref[...]], axis=1)
    return c_ref[...] + w_ref[...] - LAM * lse


def row_kernel(a_ref, b_ref, r_ref, c_ref, w_ref, own_ref, other_ref, guess_ref, out_ref, a_s, b_s, acc_s, guess_s, total_s, *, tile):
    c = target_shift(c_ref, w_ref, own_ref, other_ref)
    row_pass(a_ref, b_ref, r_ref, c, guess_ref, out_ref, a_s, b_s, acc_s, guess_s, total_s, tile)


def joined(first, second):
    top = jnp.maximum(first, second)
    return top + jnp.log(jnp.exp(first - top) + jnp.exp(second - top))


def col_kernel(a_ref, b_ref, r_ref, c_ref, logw_ref, one_ref, two_ref, *refs, tile, first):
    if first:
        own_ref, other_ref, f_ref, a_s, b_s, guess_s, total_s = refs
    else:
        last_own_ref, last_other_ref, own_ref, other_ref, f_ref, a_s, b_s, guess_s, total_s = refs
    cols = b_ref.shape[1]
    lse = joined(one_ref[...], two_ref[...])
    f_ref[...] = -LAM * EPS * lse
    set_source(a_ref, r_ref[...] + logw_ref[...] - LAM * lse, a_s)
    copy_target(b_ref, b_s)

    def over_tiles(work):
        def step(index, carry):
            cut = pl.ds(pl.multiple_of(index * tile, tile), tile)
            work(cut, score(a_s[...], b_s[:, cut]))
            return carry

        lax.fori_loop(0, cols // tile, step, 0)

    def about_tops():
        def top(cut, value):
            guess_s[:, cut] = jnp.max(value, axis=0, keepdims=True)

        set_target(b_ref, c_ref[...], b_s)
        over_tiles(top)

    def sums():
        def total(cut, value):
            total_s[:, cut] = jnp.sum(jnp.exp(value), axis=0, keepdims=True)

        set_target(b_ref, c_ref[...] - guess_s[...], b_s)
        over_tiles(total)

    if first:
        about_tops()
        sums()
    else:
        guess_s[...] = jnp.concatenate([last_own_ref[...], last_other_ref[...]], axis=1)
        sums()

        @pl.when(jnp.logical_not(in_range(total_s[...])))
        def _():
            about_tops()
            sums()

    result = guess_s[...] + jnp.log(total_s[...])
    own_ref[...] = result[:, 0 : cols // 2]
    other_ref[...] = result[:, cols // 2 :]


def plan_kernel(emb_ref, a_ref, b_ref, r_ref, c_ref, w_ref, logw_ref, f_ref, own_ref, other_ref, out_ref, a_s, b_s, mass_s, pull_s, *, tile):
    rows, cols = emb_ref.shape[1], b_ref.shape[1]
    set_source(a_ref, r_ref[...] + logw_ref[...] + f_ref[...] * (1.0 / EPS), a_s)
    copy_target(b_ref, b_s)
    set_target(b_ref, target_shift(c_ref, w_ref, own_ref, other_ref), b_s)
    mass_s[...] = jnp.zeros_like(mass_s)
    pull_s[...] = jnp.zeros_like(pull_s)

    def step(index, carry):
        cut = pl.ds(pl.multiple_of(index * tile, tile), tile)
        plan = jnp.exp(score(a_s[...], b_s[:, cut]))
        mass = plan[:, 0:128]
        for col in range(128, tile, 128):
            mass += plan[:, col : col + 128]
        mass_s[...] += mass
        pull_s[...] += lax.dot_general(
            plan.astype(jnp.bfloat16),
            b_ref[0:EMB, cut],
            (((1,), (1,)), ((), ())),
            preferred_element_type=jnp.float32,
        )
        return carry

    lax.fori_loop(0, cols // tile, step, 0)
    for at in range(0, rows, 128):
        mass = jnp.sum(mass_s[at : at + 128, :].T, axis=0, keepdims=True)
        pull = jnp.concatenate([pull_s[at : at + 128, :], jnp.zeros((128, 128 - EMB), jnp.float32)], axis=1).T
        grad = mass * emb_ref[:, at : at + 128].astype(jnp.float32) - pull[0:EMB, :]
        out_ref[:, at : at + 128] = grad.astype(out_ref.dtype)


def params(mib):
    return pltpu.CompilerParams(vmem_limit_bytes=mib * MIB)


TILE = 1024


def line(width):
    return jax.ShapeDtypeStruct((1, width), jnp.float32)


def operands(rows, cols):
    return [pltpu.VMEM((rows, DEPTH), jnp.bfloat16), pltpu.VMEM((DEPTH, cols), jnp.bfloat16)]


def row_scratch(rows, cols):
    return operands(rows, cols) + [
        pltpu.VMEM((rows, 128), jnp.float32),
        pltpu.VMEM((1, rows), jnp.float32),
        pltpu.VMEM((1, rows), jnp.float32),
    ]


def first_call(src_emb, src_pos, own, other):
    rows, cols = src_emb.shape[1], 2 * own.shape[1]
    return pl.pallas_call(
        functools.partial(first_kernel, tile=min(TILE, cols)),
        out_shape=(
            line(rows),
            jax.ShapeDtypeStruct((rows, DEPTH), jnp.bfloat16),
            jax.ShapeDtypeStruct((DEPTH, cols), jnp.bfloat16),
            line(rows),
            line(cols),
            line(cols),
        ),
        scratch_shapes=row_scratch(rows, cols),
        compiler_params=params(32),
        name="first_row_lse",
    )(src_emb, src_pos, own, other)


def row_call(a, b, r, c, w, parts, guess):
    rows, cols = a.shape[0], b.shape[1]
    return pl.pallas_call(
        functools.partial(row_kernel, tile=min(TILE, cols)),
        out_shape=line(rows),
        scratch_shapes=row_scratch(rows, cols),
        compiler_params=params(32),
        name="row_lse",
    )(a, b, r, c, w, *parts, guess)


def col_call(a, b, r, c, logw, parts, last):
    rows, cols = a.shape[0], b.shape[1]
    return pl.pallas_call(
        functools.partial(col_kernel, tile=min(TILE, cols), first=not last),
        out_shape=(line(cols // 2), line(cols // 2), line(rows)),
        scratch_shapes=operands(rows, cols) + [pltpu.VMEM((1, cols), jnp.float32), pltpu.VMEM((1, cols), jnp.float32)],
        compiler_params=params(32),
        name="col_lse",
    )(a, b, r, c, logw, *parts, *last)


def plan_call(src_emb, a, b, r, c, w, logw, f, parts):
    rows, cols = a.shape[0], b.shape[1]
    return pl.pallas_call(
        functools.partial(plan_kernel, tile=min(TILE, cols)),
        out_shape=jax.ShapeDtypeStruct((EMB, rows), jnp.bfloat16),
        scratch_shapes=operands(rows, cols) + [pltpu.VMEM((rows, 128), jnp.float32), pltpu.VMEM((rows, EMB), jnp.float32)],
        compiler_params=params(32),
        name="plan_grad",
    )(src_emb, a, b, r, c, w, logw, f, *parts)


def rounded_sum(first, second):
    total = first.astype(jnp.float32) + second.astype(jnp.float32)
    return lax.reduce_precision(total, 8, 7).astype(jnp.bfloat16)


def swapped(value, axis, mask):
    return lax.ppermute(value, axis, [(k, k ^ mask) for k in range(lax.axis_size(axis))])


def exchanged(value, join):
    value = join(value, swapped(value, "tgt", 1))
    return value, swapped(value, "tgt", 3)


def spread(block):
    size = lax.axis_size("src")
    groups = [list(range(core, size, 2)) for core in range(2)]
    block = jnp.broadcast_to(block, (size // 2,) + block.shape)
    return lax.all_to_all(block, "src", 0, 0, axis_index_groups=groups, tiled=True)


def per_device(src_emb, src_pos, src_logw, tgt_emb, tgt_pos, tgt_logw):
    piece = tgt_emb.shape[1]
    half = piece * (lax.axis_size("src") // 2)
    logw = src_logw[None, :]

    count = EMB + 4
    own = jnp.concatenate([tgt_emb, tgt_pos, tgt_logw[None, :], tgt_logw[None, :]], 0).reshape(count * piece // 128, 128)
    own = spread(own).reshape(-1, count, piece).transpose(1, 0, 2).reshape(count, half)
    lse, a, b, r, c, w = first_call(src_emb, src_pos, own, swapped(own, "src", 1))

    last = ()
    for step in range(ITERS):
        if step:
            lse = row_call(a, b, r, c, w, parts, lse)
        mine, theirs, f = col_call(a, b, r, c, logw, exchanged(lse, joined), last)
        last = (mine, theirs)
        col = spread(joined(mine, swapped(theirs, "src", 1)).reshape(half // 128, 128))
        top = jnp.max(col, axis=0)
        col = (top + jnp.log(jnp.sum(jnp.exp(col - top), axis=0))).reshape(1, half)
        parts = (col, swapped(col, "src", 1))
    begin = lax.axis_index("src") // 2 * piece
    g_own = -LAM * EPS * lax.dynamic_slice_in_dim(col[0], begin, piece, 0)
    grad = plan_call(src_emb, a, b, r, c, w, logw, f, parts)
    first, second = exchanged(grad, rounded_sum)
    return f[0], g_own, first.astype(jnp.float32) + second.astype(jnp.float32)


def solution(mesh):
    placed = (
        P(None, "src"),
        P(None, "src"),
        P("src"),
        P(None, ("src", "tgt")),
        P(None, ("src", "tgt")),
        P(("src", "tgt")),
    )
    return jax.shard_map(
        per_device,
        mesh=mesh,
        in_specs=placed,
        out_specs=(P("src"), P(("src", "tgt")), P(None, "src")),
        check_vma=False,
    )
```

```python
import functools

import jax
import jax.numpy as jnp
from jax import lax
from jax.experimental import pallas as pl
from jax.experimental.pallas import tpu as pltpu
from jax.sharding import PartitionSpec as P

ITERS = 3
EPS = 0.25
RHO = 2.0
LAM = RHO / (RHO + EPS)
EMB = 64
DEPTH = 128
PACK = 80
MIB = 1 << 20
LOW, HIGH = 1e-25, 1e30


def pieces(value):
    high = value.astype(jnp.bfloat16).astype(jnp.float32)
    rest = value - high
    mid = rest.astype(jnp.bfloat16).astype(jnp.float32)
    low = (rest - mid).astype(jnp.bfloat16).astype(jnp.float32)
    return high, mid, low


def stacked(rows, height, width):
    index = lax.broadcasted_iota(jnp.int32, (height, width), 0)
    block = jnp.zeros((height, width), jnp.float32)
    for at, row in enumerate(rows):
        if row is not None:
            block = jnp.where(index == at, row, block)
    return block


def source_static(emb_ref, pos_ref, out_ref):
    width = emb_ref.shape[1]
    pos = pos_ref[...]
    emb = emb_ref[...].astype(jnp.float32)
    sq = jnp.sum(emb * emb, axis=0, keepdims=True)
    shift = -(sq * (1.0 / EMB) + pos[0:1] * pos[0:1] + pos[1:2] * pos[1:2]) * (1.0 / EPS)
    pos = pos * (2.0 / EPS)
    zero, one = jnp.zeros((1, width), jnp.float32), jnp.ones((1, width), jnp.float32)
    rows = [*pieces(pos[0:1]), *pieces(pos[1:2]), zero, zero, zero, one, one, one]
    extra = stacked(rows, 16, width)
    emb = emb * (2.0 / (EMB * EPS))
    pad = jnp.zeros((DEPTH - PACK, 128), jnp.float32)
    for at in range(0, width, 128):
        block = jnp.concatenate([emb[:, at : at + 128], extra[:, at : at + 128], pad], axis=0)
        out_ref[at : at + 128, :] = block.T.astype(jnp.bfloat16)
    return shift


def target_static(pack_ref, at, out_ref):
    width = pack_ref.shape[1]
    pack = pack_ref[...].astype(jnp.float32)
    emb, geo = pack[0:EMB], pack[EMB : EMB + 4]
    sq = jnp.sum(emb * emb, axis=0, keepdims=True)
    x, y = geo[0:1], geo[1:2]
    shift = -(sq * (1.0 / EMB) + x * x + y * y) * (1.0 / EPS)
    one = jnp.ones((1, width), jnp.float32)
    cut = slice(at, at + width)
    out_ref[0:EMB, cut] = pack_ref[0:EMB, :]
    out_ref[EMB:PACK, cut] = stacked([x, x, x, y, y, y, one, one, one], 16, width).astype(jnp.bfloat16)
    out_ref[PACK:DEPTH, cut] = jnp.zeros((DEPTH - PACK, width), jnp.bfloat16)
    return shift, geo[2:3]


def set_source(a_ref, shift, a_s):
    block = stacked([None] * 6 + [*pieces(shift)], 16, a_ref.shape[0]).astype(jnp.bfloat16)
    above = jnp.zeros((EMB, 128), jnp.bfloat16)
    below = jnp.zeros((DEPTH - PACK, 128), jnp.bfloat16)
    for at in range(0, a_ref.shape[0], 128):
        part = jnp.concatenate([above, block[:, at : at + 128], below], axis=0).T
        a_s[at : at + 128, :] = a_ref[at : at + 128, :] + part


def set_target(b_ref, shift, b_s):
    block = stacked([None] * 9 + [*pieces(shift)], 16, b_ref.shape[1])
    b_s[EMB:PACK, :] = (b_ref[EMB:PACK, :].astype(jnp.float32) + block).astype(jnp.bfloat16)


def copy_target(b_ref, b_s):
    b_s[0:EMB, :] = b_ref[0:EMB, :]
    b_s[PACK:DEPTH, :] = b_ref[PACK:DEPTH, :]


def score(a, b):
    return lax.dot_general(a, b, (((1,), (0,)), ((), ())), preferred_element_type=jnp.float32)


def row_sums(a_s, b_s, acc_s, tile):
    acc_s[...] = jnp.zeros_like(acc_s)

    def step(index, carry):
        cut = pl.ds(pl.multiple_of(index * tile, tile), tile)
        value = jnp.exp(score(a_s[...], b_s[:, cut]))
        part = value[:, 0:128]
        for col in range(128, tile, 128):
            part += value[:, col : col + 128]
        acc_s[...] += part
        return carry

    lax.fori_loop(0, b_s.shape[1] // tile, step, 0)


def row_tops(a_s, b_s, acc_s, tile, count):
    acc_s[...] = jnp.full(acc_s.shape, -jnp.inf, jnp.float32)

    def step(index, carry):
        cut = pl.ds(pl.multiple_of(index * tile, tile), tile)
        value = score(a_s[...], b_s[:, cut])
        part = value[:, 0:128]
        for col in range(128, tile, 128):
            part = jnp.maximum(part, value[:, col : col + 128])
        acc_s[...] = jnp.maximum(acc_s[...], part)
        return carry

    lax.fori_loop(0, count, step, 0)


def over_lanes(acc_s, out_s, join):
    for at in range(0, acc_s.shape[0], 128):
        out_s[:, at : at + 128] = join(acc_s[at : at + 128, :].T, axis=0, keepdims=True)


def in_range(total):
    return jnp.logical_and(jnp.min(total) > LOW, jnp.max(total) < HIGH)


def row_pass(a_ref, b_ref, r_ref, c, ready_ref, guess_ref, out_ref, a_s, b_s, acc_s, guess_s, total_s, tile):
    cols = b_ref.shape[1]
    copy_target(b_ref, b_s)
    set_target(b_ref, c, b_s)

    def about_tops(width, count):
        set_source(a_ref, r_ref[...], a_s)
        row_tops(a_s, b_s, acc_s, width, count)
        over_lanes(acc_s, guess_s, jnp.max)
        set_source(a_ref, r_ref[...] - guess_s[...], a_s)

    def sums(left):
        row_sums(left, b_s, acc_s, tile)
        over_lanes(acc_s, total_s, jnp.sum)

    if guess_ref is None:
        about_tops(min(512, cols), 1)
        sums(a_s)
    else:
        guess_s[...] = guess_ref[...]
        sums(ready_ref)

    @pl.when(jnp.logical_not(in_range(total_s[...])))
    def _():
        about_tops(tile, cols // tile)
        sums(a_s)

    out_ref[...] = guess_s[...] + jnp.log(total_s[...])


def static_kernel(emb_ref, pos_ref, own_ref, a_ref, r_ref, b_ref, c_ref, w_ref):
    r_ref[...] = source_static(emb_ref, pos_ref, a_ref)
    c_ref[...], w_ref[...] = target_static(own_ref, 0, b_ref)


def first_kernel(a_ref, r_ref, near_b_ref, near_c_ref, near_w_ref, other_ref, out_ref, b_ref, c_ref, w_ref, a_s, b_s, acc_s, guess_s, total_s, *, tile):
    half = other_ref.shape[1]
    b_ref[:, 0:half] = near_b_ref[...]
    c_ref[:, 0:half] = near_c_ref[...]
    w_ref[:, 0:half] = near_w_ref[...]
    c_ref[:, half:], w_ref[:, half:] = target_static(other_ref, half, b_ref)
    row_pass(a_ref, b_ref, r_ref, c_ref[...] + w_ref[...], None, None, out_ref, a_s, b_s, acc_s, guess_s, total_s, tile)


def target_shift(c_ref, w_ref, own_ref, other_ref):
    lse = jnp.concatenate([own_ref[...], other_ref[...]], axis=1)
    return c_ref[...] + w_ref[...] - LAM * lse


def row_kernel(a_ref, b_ref, r_ref, c_ref, w_ref, own_ref, other_ref, ready_ref, guess_ref, out_ref, a_s, b_s, acc_s, guess_s, total_s, *, tile):
    c = target_shift(c_ref, w_ref, own_ref, other_ref)
    row_pass(a_ref, b_ref, r_ref, c, ready_ref, guess_ref, out_ref, a_s, b_s, acc_s, guess_s, total_s, tile)


def joined(first, second):
    top = jnp.maximum(first, second)
    return top + jnp.log(jnp.exp(first - top) + jnp.exp(second - top))


def row_prepare_kernel(a_ref, r_ref, guess_ref, ready_ref):
    set_source(a_ref, r_ref[...] - guess_ref[...], ready_ref)


def over_tiles(left, right, tile, work):
    def step(index, carry):
        cut = pl.ds(pl.multiple_of(index * tile, tile), tile)
        work(cut, score(left[...], right[:, cut]))
        return carry

    lax.fori_loop(0, right.shape[1] // tile, step, 0)


def col_tops(left, right, out, tile):
    def top(cut, value):
        out[:, cut] = jnp.max(value, axis=0, keepdims=True)

    over_tiles(left, right, tile, top)


def col_sums(left, right, out, tile):
    def total(cut, value):
        out[:, cut] = jnp.sum(jnp.exp(value), axis=0, keepdims=True)

    over_tiles(left, right, tile, total)


def col_prepare_kernel(b_ref, c_ref, own_ref, other_ref, ready_ref, guess_ref):
    guess_ref[...] = jnp.concatenate([own_ref[...], other_ref[...]], axis=1)
    copy_target(b_ref, ready_ref)
    set_target(b_ref, c_ref[...] - guess_ref[...], ready_ref)


def col_guess_kernel(a_ref, b_ref, r_ref, c_ref, logw_ref, lse_ref, ready_ref, guess_ref, a_s, *, tile):
    set_source(a_ref, r_ref[...] + logw_ref[...] - LAM * lse_ref[...], a_s)
    copy_target(b_ref, ready_ref)
    set_target(b_ref, c_ref[...], ready_ref)
    col_tops(a_s, ready_ref, guess_ref, tile)
    set_target(b_ref, c_ref[...] - guess_ref[...], ready_ref)


def col_kernel(a_ref, b_ref, r_ref, c_ref, logw_ref, ready_ref, guess_ref, one_ref, two_ref, own_ref, other_ref, f_ref, a_s, b_s, guess_s, total_s, *, tile):
    cols = b_ref.shape[1]
    lse = joined(one_ref[...], two_ref[...])
    f_ref[...] = -LAM * EPS * lse
    set_source(a_ref, r_ref[...] + logw_ref[...] - LAM * lse, a_s)
    guess_s[...] = guess_ref[...]
    col_sums(a_s, ready_ref, total_s, tile)

    @pl.when(jnp.logical_not(in_range(total_s[...])))
    def _():
        copy_target(b_ref, b_s)
        set_target(b_ref, c_ref[...], b_s)
        col_tops(a_s, b_s, guess_s, tile)
        set_target(b_ref, c_ref[...] - guess_s[...], b_s)
        col_sums(a_s, b_s, total_s, tile)

    result = guess_s[...] + jnp.log(total_s[...])
    own_ref[...] = result[:, 0 : cols // 2]
    other_ref[...] = result[:, cols // 2 :]


def plan_kernel(emb_ref, a_s, b_ref, c_ref, w_ref, own_ref, other_ref, out_ref, b_s, mass_s, pull_s, *, begin, tile):
    rows, cols = out_ref.shape[1], b_ref.shape[1]
    copy_target(b_ref, b_s)
    set_target(b_ref, target_shift(c_ref, w_ref, own_ref, other_ref), b_s)
    mass_s[...] = jnp.zeros_like(mass_s)
    pull_s[...] = jnp.zeros_like(pull_s)

    def step(index, carry):
        cut = pl.ds(pl.multiple_of(index * tile, tile), tile)
        plan = jnp.exp(score(a_s[begin : begin + rows, :], b_s[:, cut]))
        mass = plan[:, 0:128]
        for col in range(128, tile, 128):
            mass += plan[:, col : col + 128]
        mass_s[...] += mass
        pull_s[...] += lax.dot_general(
            plan.astype(jnp.bfloat16),
            b_ref[0:EMB, cut],
            (((1,), (1,)), ((), ())),
            preferred_element_type=jnp.float32,
        )
        return carry

    lax.fori_loop(0, cols // tile, step, 0)
    for at in range(0, rows, 128):
        mass = jnp.sum(mass_s[at : at + 128, :].T, axis=0, keepdims=True)
        pull = jnp.concatenate([pull_s[at : at + 128, :], jnp.zeros((128, 128 - EMB), jnp.float32)], axis=1).T
        grad = mass * emb_ref[:, begin + at : begin + at + 128].astype(jnp.float32) - pull[0:EMB, :]
        out_ref[:, at : at + 128] = grad.astype(out_ref.dtype)


def params(mib):
    return pltpu.CompilerParams(vmem_limit_bytes=mib * MIB)


TILE = 2048


def line(width):
    return jax.ShapeDtypeStruct((1, width), jnp.float32)


def operands(rows, cols):
    return [pltpu.VMEM((rows, DEPTH), jnp.bfloat16), pltpu.VMEM((DEPTH, cols), jnp.bfloat16)]


def row_scratch(rows, cols):
    return operands(rows, cols) + [
        pltpu.VMEM((rows, 128), jnp.float32),
        pltpu.VMEM((1, rows), jnp.float32),
        pltpu.VMEM((1, rows), jnp.float32),
    ]


def static_call(src_emb, src_pos, own):
    rows, half = src_emb.shape[1], own.shape[1]
    return pl.pallas_call(
        static_kernel,
        out_shape=(
            jax.ShapeDtypeStruct((rows, DEPTH), jnp.bfloat16),
            line(rows),
            jax.ShapeDtypeStruct((DEPTH, half), jnp.bfloat16),
            line(half),
            line(half),
        ),
        compiler_params=params(16),
        cost_estimate=pl.CostEstimate(flops=10**8, bytes_accessed=2 * 10**6, transcendentals=0),
        name="static_parts",
    )(src_emb, src_pos, own)


def first_call(a, r, near, other):
    rows, cols = a.shape[0], 2 * other.shape[1]
    return pl.pallas_call(
        functools.partial(first_kernel, tile=min(TILE, cols)),
        out_shape=(line(rows), jax.ShapeDtypeStruct((DEPTH, cols), jnp.bfloat16), line(cols), line(cols)),
        scratch_shapes=row_scratch(rows, cols),
        compiler_params=params(32),
        name="first_row_lse",
    )(a, r, *near, other)


def row_call(a, b, r, c, w, parts, ready, guess):
    rows, cols = a.shape[0], b.shape[1]
    return pl.pallas_call(
        functools.partial(row_kernel, tile=min(TILE, cols)),
        out_shape=line(rows),
        scratch_shapes=row_scratch(rows, cols),
        compiler_params=params(32),
        name="row_lse",
    )(a, b, r, c, w, *parts, ready, guess)


def row_prepare(a, r, guess):
    return pl.pallas_call(
        row_prepare_kernel,
        out_shape=jax.ShapeDtypeStruct(a.shape, a.dtype),
        compiler_params=params(16),
        cost_estimate=pl.CostEstimate(flops=10**8, bytes_accessed=10**6, transcendentals=0),
        name="row_prepare",
    )(a, r, guess)


def col_prepare(b, c, last):
    return pl.pallas_call(
        col_prepare_kernel,
        out_shape=(jax.ShapeDtypeStruct(b.shape, b.dtype), line(b.shape[1])),
        compiler_params=params(16),
        cost_estimate=pl.CostEstimate(flops=10**8, bytes_accessed=2 * 10**6, transcendentals=0),
        name="col_prepare",
    )(b, c, *last)


def col_guess(a, b, r, c, logw, lse):
    rows, cols = a.shape[0], b.shape[1]
    return pl.pallas_call(
        functools.partial(col_guess_kernel, tile=min(TILE, cols)),
        out_shape=(jax.ShapeDtypeStruct(b.shape, b.dtype), line(cols)),
        scratch_shapes=[pltpu.VMEM((rows, DEPTH), jnp.bfloat16)],
        compiler_params=params(32),
        cost_estimate=pl.CostEstimate(flops=2 * rows * cols * DEPTH, bytes_accessed=2 * 10**6, transcendentals=0),
        name="col_guess",
    )(a, b, r, c, logw, lse)


def col_call(a, b, r, c, logw, prepared, parts):
    rows, cols = a.shape[0], b.shape[1]
    return pl.pallas_call(
        functools.partial(col_kernel, tile=cols),
        out_shape=(line(cols // 2), line(cols // 2), line(rows), jax.ShapeDtypeStruct(a.shape, a.dtype)),
        scratch_shapes=operands(rows, cols)[1:] + [pltpu.VMEM((1, cols), jnp.float32), pltpu.VMEM((1, cols), jnp.float32)],
        compiler_params=params(32),
        name="col_lse",
    )(a, b, r, c, logw, *prepared, *parts)


def plan_call(src_emb, a, b, c, w, parts, begin, rows):
    cols = b.shape[1]
    return pl.pallas_call(
        functools.partial(plan_kernel, begin=begin, tile=min(TILE, cols)),
        out_shape=jax.ShapeDtypeStruct((EMB, rows), jnp.bfloat16),
        scratch_shapes=operands(rows, cols)[1:] + [pltpu.VMEM((rows, 128), jnp.float32), pltpu.VMEM((rows, EMB), jnp.float32)],
        compiler_params=params(32),
        cost_estimate=pl.CostEstimate(flops=4 * rows * cols * DEPTH, bytes_accessed=2 * 10**6, transcendentals=rows * cols),
        name="plan_grad",
    )(src_emb, a, b, c, w, *parts)


def rounded_sum(first, second):
    total = first.astype(jnp.float32) + second.astype(jnp.float32)
    return lax.reduce_precision(total, 8, 7).astype(jnp.bfloat16)


def swapped(value, axis, mask):
    return lax.ppermute(value, axis, [(k, k ^ mask) for k in range(lax.axis_size(axis))])


def exchanged(value, join):
    value = join(value, swapped(value, "tgt", 1))
    return value, swapped(value, "tgt", 3)


def spread(block):
    size = lax.axis_size("src")
    groups = [list(range(core, size, 2)) for core in range(2)]
    block = jnp.broadcast_to(block, (size // 2,) + block.shape)
    return lax.all_to_all(block, "src", 0, 0, axis_index_groups=groups, tiled=True)


def per_device(src_emb, src_pos, src_logw, tgt_emb, tgt_pos, tgt_logw):
    piece = tgt_emb.shape[1]
    half = piece * (lax.axis_size("src") // 2)
    logw = src_logw[None, :]

    count = EMB + 4
    own = jnp.concatenate([tgt_emb, tgt_pos, tgt_logw[None, :], tgt_logw[None, :]], 0).reshape(count * piece // 128, 128)
    own = spread(own).reshape(-1, count, piece).transpose(1, 0, 2).reshape(count, half)
    other = swapped(own, "src", 1)
    a, r, *near = static_call(src_emb, src_pos, own)
    lse, b, c, w = first_call(a, r, near, other)

    for step in range(ITERS):
        if step:
            lse = row_call(a, b, r, c, w, parts, ready, lse)
            prepared = col_prepare(b, c, (mine, theirs))
        else:
            prepared = col_guess(a, b, r, c, logw, lse)
        if step < ITERS - 1:
            ready = row_prepare(a, r, lse)
        mine, theirs, f, left = col_call(a, b, r, c, logw, prepared, exchanged(lse, joined))
        col = spread(joined(mine, swapped(theirs, "src", 1)).reshape(half // 128, 128))
        top = jnp.max(col, axis=0)
        col = (top + jnp.log(jnp.sum(jnp.exp(col - top), axis=0))).reshape(1, half)
        parts = (col, swapped(col, "src", 1))
    begin = lax.axis_index("src") // 2 * piece
    g_own = -LAM * EPS * lax.dynamic_slice_in_dim(col[0], begin, piece, 0)
    rows = src_emb.shape[1]
    grads = []
    for begin in range(0, rows, rows // 2):
        grads.append(exchanged(plan_call(src_emb, left, b, c, w, parts, begin, rows // 2), rounded_sum))
    first, second = (jnp.concatenate(part, axis=1).astype(jnp.float32) for part in zip(*grads))
    return f[0], g_own, first + second


def solution(mesh):
    placed = (
        P(None, "src"),
        P(None, "src"),
        P("src"),
        P(None, ("src", "tgt")),
        P(None, ("src", "tgt")),
        P(("src", "tgt")),
    )
    return jax.shard_map(
        per_device,
        mesh=mesh,
        in_specs=placed,
        out_specs=(P("src"), P(("src", "tgt")), P(None, "src")),
        check_vma=False,
    )
```

```python
import functools

import jax
import jax.numpy as jnp
from jax import lax
from jax.experimental import pallas as pl
from jax.experimental.pallas import tpu as pltpu
from jax.sharding import PartitionSpec as P

ITERS = 3
EPS = 0.25
RHO = 2.0
LAM = RHO / (RHO + EPS)
EMB = 64
DEPTH = 128
PACK = 80
MIB = 1 << 20
LOW, HIGH = 1e-25, 1e30


def pieces(value):
    high = value.astype(jnp.bfloat16).astype(jnp.float32)
    rest = value - high
    mid = rest.astype(jnp.bfloat16).astype(jnp.float32)
    low = (rest - mid).astype(jnp.bfloat16).astype(jnp.float32)
    return high, mid, low


def stacked(rows, height, width):
    index = lax.broadcasted_iota(jnp.int32, (height, width), 0)
    block = jnp.zeros((height, width), jnp.float32)
    for at, row in enumerate(rows):
        if row is not None:
            block = jnp.where(index == at, row, block)
    return block


def source_static(emb_ref, pos_ref, out_ref):
    width = emb_ref.shape[1]
    pos = pos_ref[...]
    emb = emb_ref[...].astype(jnp.float32)
    sq = jnp.sum(emb * emb, axis=0, keepdims=True)
    shift = -(sq * (1.0 / EMB) + pos[0:1] * pos[0:1] + pos[1:2] * pos[1:2]) * (1.0 / EPS)
    pos = pos * (2.0 / EPS)
    zero, one = jnp.zeros((1, width), jnp.float32), jnp.ones((1, width), jnp.float32)
    rows = [*pieces(pos[0:1]), *pieces(pos[1:2]), zero, zero, zero, one, one, one]
    extra = stacked(rows, 16, width)
    emb = emb * (2.0 / (EMB * EPS))
    pad = jnp.zeros((DEPTH - PACK, 128), jnp.float32)
    for at in range(0, width, 128):
        block = jnp.concatenate([emb[:, at : at + 128], extra[:, at : at + 128], pad], axis=0)
        out_ref[at : at + 128, :] = block.T.astype(jnp.bfloat16)
    return shift


def target_static(pack_ref, at, out_ref):
    width = pack_ref.shape[1]
    pack = pack_ref[...].astype(jnp.float32)
    emb, geo = pack[0:EMB], pack[EMB : EMB + 4]
    sq = jnp.sum(emb * emb, axis=0, keepdims=True)
    x, y = geo[0:1], geo[1:2]
    shift = -(sq * (1.0 / EMB) + x * x + y * y) * (1.0 / EPS)
    one = jnp.ones((1, width), jnp.float32)
    cut = slice(at, at + width)
    out_ref[0:EMB, cut] = pack_ref[0:EMB, :]
    out_ref[EMB:PACK, cut] = stacked([x, x, x, y, y, y, one, one, one], 16, width).astype(jnp.bfloat16)
    out_ref[PACK:DEPTH, cut] = jnp.zeros((DEPTH - PACK, width), jnp.bfloat16)
    return shift, geo[2:3]


def set_source(a_ref, shift, a_s):
    block = stacked([None] * 6 + [*pieces(shift)], 16, a_ref.shape[0]).astype(jnp.bfloat16)
    above = jnp.zeros((EMB, 128), jnp.bfloat16)
    below = jnp.zeros((DEPTH - PACK, 128), jnp.bfloat16)
    for at in range(0, a_ref.shape[0], 128):
        part = jnp.concatenate([above, block[:, at : at + 128], below], axis=0).T
        a_s[at : at + 128, :] = a_ref[at : at + 128, :] + part


def set_target(b_ref, shift, b_s):
    block = stacked([None] * 9 + [*pieces(shift)], 16, b_ref.shape[1])
    b_s[EMB:PACK, :] = (b_ref[EMB:PACK, :].astype(jnp.float32) + block).astype(jnp.bfloat16)


def copy_target(b_ref, b_s):
    b_s[0:EMB, :] = b_ref[0:EMB, :]
    b_s[PACK:DEPTH, :] = b_ref[PACK:DEPTH, :]


def score(a, b):
    return lax.dot_general(a, b, (((1,), (0,)), ((), ())), preferred_element_type=jnp.float32)


def row_sums(a_s, b_s, acc_s, tile):
    acc_s[...] = jnp.zeros_like(acc_s)

    def step(index, carry):
        cut = pl.ds(pl.multiple_of(index * tile, tile), tile)
        value = jnp.exp(score(a_s[...], b_s[:, cut]))
        part = value[:, 0:128]
        for col in range(128, tile, 128):
            part += value[:, col : col + 128]
        acc_s[...] += part
        return carry

    lax.fori_loop(0, b_s.shape[1] // tile, step, 0)


def row_tops(a_s, b_s, acc_s, tile, count):
    acc_s[...] = jnp.full(acc_s.shape, -jnp.inf, jnp.float32)

    def step(index, carry):
        cut = pl.ds(pl.multiple_of(index * tile, tile), tile)
        value = score(a_s[...], b_s[:, cut])
        part = value[:, 0:128]
        for col in range(128, tile, 128):
            part = jnp.maximum(part, value[:, col : col + 128])
        acc_s[...] = jnp.maximum(acc_s[...], part)
        return carry

    lax.fori_loop(0, count, step, 0)


def over_lanes(acc_s, out_s, join):
    for at in range(0, acc_s.shape[0], 128):
        out_s[:, at : at + 128] = join(acc_s[at : at + 128, :].T, axis=0, keepdims=True)


def in_range(total):
    return jnp.logical_and(jnp.min(total) > LOW, jnp.max(total) < HIGH)


def row_pass(a_ref, b_ref, r_ref, c, ready_ref, guess_ref, out_ref, a_s, b_s, acc_s, guess_s, total_s, tile):
    cols = b_ref.shape[1]
    copy_target(b_ref, b_s)
    set_target(b_ref, c, b_s)

    def about_tops(width, count):
        set_source(a_ref, r_ref[...], a_s)
        row_tops(a_s, b_s, acc_s, width, count)
        over_lanes(acc_s, guess_s, jnp.max)
        set_source(a_ref, r_ref[...] - guess_s[...], a_s)

    def sums(left, width):
        row_sums(left, b_s, acc_s, width)
        over_lanes(acc_s, total_s, jnp.sum)

    if guess_ref is None:
        about_tops(min(512, cols), 1)
        sums(a_s, tile)
    else:
        guess_s[...] = guess_ref[...]
        sums(ready_ref, tile)

    @pl.when(jnp.logical_not(in_range(total_s[...])))
    def _():
        about_tops(SMALL, cols // SMALL)
        sums(a_s, SMALL)

    out_ref[...] = guess_s[...] + jnp.log(total_s[...])


def static_kernel(emb_ref, pos_ref, own_ref, a_ref, r_ref, b_ref, c_ref, w_ref):
    r_ref[...] = source_static(emb_ref, pos_ref, a_ref)
    c_ref[...], w_ref[...] = target_static(own_ref, 0, b_ref)


def first_kernel(a_ref, r_ref, near_b_ref, near_c_ref, near_w_ref, other_ref, out_ref, b_ref, c_ref, w_ref, a_s, b_s, acc_s, guess_s, total_s, *, tile):
    half = other_ref.shape[1]
    b_ref[:, 0:half] = near_b_ref[...]
    c_ref[:, 0:half] = near_c_ref[...]
    w_ref[:, 0:half] = near_w_ref[...]
    c_ref[:, half:], w_ref[:, half:] = target_static(other_ref, half, b_ref)
    row_pass(a_ref, b_ref, r_ref, c_ref[...] + w_ref[...], None, None, out_ref, a_s, b_s, acc_s, guess_s, total_s, tile)


def target_shift(c_ref, w_ref, own_ref, other_ref):
    lse = jnp.concatenate([own_ref[...], other_ref[...]], axis=1)
    return c_ref[...] + w_ref[...] - LAM * lse


def row_kernel(a_ref, b_ref, r_ref, c_ref, w_ref, own_ref, other_ref, ready_ref, guess_ref, out_ref, a_s, b_s, acc_s, guess_s, total_s, *, tile):
    c = target_shift(c_ref, w_ref, own_ref, other_ref)
    row_pass(a_ref, b_ref, r_ref, c, ready_ref, guess_ref, out_ref, a_s, b_s, acc_s, guess_s, total_s, tile)


def joined(first, second):
    top = jnp.maximum(first, second)
    return top + jnp.log(jnp.exp(first - top) + jnp.exp(second - top))


def row_prepare_kernel(a_ref, r_ref, guess_ref, ready_ref):
    set_source(a_ref, r_ref[...] - guess_ref[...], ready_ref)


def over_tiles(left, right, tile, work):
    def step(index, carry):
        cut = pl.ds(pl.multiple_of(index * tile, tile), tile)
        work(cut, score(left[...], right[:, cut]))
        return carry

    lax.fori_loop(0, right.shape[1] // tile, step, 0)


def col_tops(left, right, out, tile):
    def top(cut, value):
        out[:, cut] = jnp.max(value, axis=0, keepdims=True)

    over_tiles(left, right, tile, top)


def col_sums(left, right, out, tile):
    def total(cut, value):
        out[:, cut] = jnp.sum(jnp.exp(value), axis=0, keepdims=True)

    over_tiles(left, right, tile, total)


def col_prepare_kernel(b_ref, c_ref, own_ref, other_ref, ready_ref, guess_ref):
    guess_ref[...] = jnp.concatenate([own_ref[...], other_ref[...]], axis=1)
    copy_target(b_ref, ready_ref)
    set_target(b_ref, c_ref[...] - guess_ref[...], ready_ref)


def col_guess_kernel(a_ref, b_ref, r_ref, c_ref, logw_ref, lse_ref, ready_ref, guess_ref, a_s, *, tile):
    set_source(a_ref, r_ref[...] + logw_ref[...] - LAM * lse_ref[...], a_s)
    copy_target(b_ref, ready_ref)
    set_target(b_ref, c_ref[...], ready_ref)
    col_tops(a_s, ready_ref, guess_ref, tile)
    set_target(b_ref, c_ref[...] - guess_ref[...], ready_ref)


def col_kernel(a_ref, b_ref, r_ref, c_ref, logw_ref, ready_ref, guess_ref, one_ref, two_ref, own_ref, other_ref, f_ref, a_s, b_s, guess_s, total_s, *, tile):
    cols = b_ref.shape[1]
    lse = joined(one_ref[...], two_ref[...])
    f_ref[...] = -LAM * EPS * lse
    set_source(a_ref, r_ref[...] + logw_ref[...] - LAM * lse, a_s)
    guess_s[...] = guess_ref[...]
    col_sums(a_s, ready_ref, total_s, tile)

    @pl.when(jnp.logical_not(in_range(total_s[...])))
    def _():
        copy_target(b_ref, b_s)
        set_target(b_ref, c_ref[...], b_s)
        col_tops(a_s, b_s, guess_s, SMALL)
        set_target(b_ref, c_ref[...] - guess_s[...], b_s)
        col_sums(a_s, b_s, total_s, SMALL)

    result = guess_s[...] + jnp.log(total_s[...])
    own_ref[...] = result[:, 0 : cols // 2]
    other_ref[...] = result[:, cols // 2 :]


def plan_kernel(emb_ref, a_s, b_ref, c_ref, w_ref, own_ref, other_ref, out_ref, b_s, mass_s, pull_s, *, begin, tile):
    rows, cols = out_ref.shape[1], b_ref.shape[1]
    copy_target(b_ref, b_s)
    set_target(b_ref, target_shift(c_ref, w_ref, own_ref, other_ref), b_s)
    mass_s[...] = jnp.zeros_like(mass_s)
    pull_s[...] = jnp.zeros_like(pull_s)

    def step(index, carry):
        cut = pl.ds(pl.multiple_of(index * tile, tile), tile)
        plan = jnp.exp(score(a_s[begin : begin + rows, :], b_s[:, cut]))
        mass = plan[:, 0:128]
        for col in range(128, tile, 128):
            mass += plan[:, col : col + 128]
        mass_s[...] += mass
        pull_s[...] += lax.dot_general(
            plan.astype(jnp.bfloat16),
            b_ref[0:EMB, cut],
            (((1,), (1,)), ((), ())),
            preferred_element_type=jnp.float32,
        )
        return carry

    lax.fori_loop(0, cols // tile, step, 0)
    for at in range(0, rows, 128):
        mass = jnp.sum(mass_s[at : at + 128, :].T, axis=0, keepdims=True)
        pull = jnp.concatenate([pull_s[at : at + 128, :], jnp.zeros((128, 128 - EMB), jnp.float32)], axis=1).T
        grad = mass * emb_ref[:, begin + at : begin + at + 128].astype(jnp.float32) - pull[0:EMB, :]
        out_ref[:, at : at + 128] = grad.astype(out_ref.dtype)


def params(mib):
    return pltpu.CompilerParams(vmem_limit_bytes=mib * MIB)


TILE = 2048
SMALL = 128


def line(width):
    return jax.ShapeDtypeStruct((1, width), jnp.float32)


def operands(rows, cols):
    return [pltpu.VMEM((rows, DEPTH), jnp.bfloat16), pltpu.VMEM((DEPTH, cols), jnp.bfloat16)]


def row_scratch(rows, cols):
    return operands(rows, cols) + [
        pltpu.VMEM((rows, 128), jnp.float32),
        pltpu.VMEM((1, rows), jnp.float32),
        pltpu.VMEM((1, rows), jnp.float32),
    ]


def static_call(src_emb, src_pos, own):
    rows, half = src_emb.shape[1], own.shape[1]
    return pl.pallas_call(
        static_kernel,
        out_shape=(
            jax.ShapeDtypeStruct((rows, DEPTH), jnp.bfloat16),
            line(rows),
            jax.ShapeDtypeStruct((DEPTH, half), jnp.bfloat16),
            line(half),
            line(half),
        ),
        compiler_params=params(16),
        cost_estimate=pl.CostEstimate(flops=10**8, bytes_accessed=2 * 10**6, transcendentals=0),
        name="static_parts",
    )(src_emb, src_pos, own)


def first_call(a, r, near, other):
    rows, cols = a.shape[0], 2 * other.shape[1]
    return pl.pallas_call(
        functools.partial(first_kernel, tile=min(TILE, cols)),
        out_shape=(line(rows), jax.ShapeDtypeStruct((DEPTH, cols), jnp.bfloat16), line(cols), line(cols)),
        scratch_shapes=row_scratch(rows, cols),
        compiler_params=params(32),
        name="first_row_lse",
    )(a, r, *near, other)


def row_call(a, b, r, c, w, parts, ready, guess):
    rows, cols = a.shape[0], b.shape[1]
    return pl.pallas_call(
        functools.partial(row_kernel, tile=min(TILE, cols)),
        out_shape=line(rows),
        scratch_shapes=row_scratch(rows, cols),
        compiler_params=params(32),
        name="row_lse",
    )(a, b, r, c, w, *parts, ready, guess)


def row_prepare(a, r, guess):
    return pl.pallas_call(
        row_prepare_kernel,
        out_shape=jax.ShapeDtypeStruct(a.shape, a.dtype),
        compiler_params=params(16),
        cost_estimate=pl.CostEstimate(flops=10**8, bytes_accessed=10**6, transcendentals=0),
        name="row_prepare",
    )(a, r, guess)


def col_prepare(b, c, last):
    return pl.pallas_call(
        col_prepare_kernel,
        out_shape=(jax.ShapeDtypeStruct(b.shape, b.dtype), line(b.shape[1])),
        compiler_params=params(16),
        cost_estimate=pl.CostEstimate(flops=10**8, bytes_accessed=2 * 10**6, transcendentals=0),
        name="col_prepare",
    )(b, c, *last)


def col_guess(a, b, r, c, logw, lse):
    rows, cols = a.shape[0], b.shape[1]
    return pl.pallas_call(
        functools.partial(col_guess_kernel, tile=min(TILE, cols)),
        out_shape=(jax.ShapeDtypeStruct(b.shape, b.dtype), line(cols)),
        scratch_shapes=[pltpu.VMEM((rows, DEPTH), jnp.bfloat16)],
        compiler_params=params(32),
        cost_estimate=pl.CostEstimate(flops=2 * rows * cols * DEPTH, bytes_accessed=2 * 10**6, transcendentals=0),
        name="col_guess",
    )(a, b, r, c, logw, lse)


def col_call(a, b, r, c, logw, prepared, parts):
    rows, cols = a.shape[0], b.shape[1]
    return pl.pallas_call(
        functools.partial(col_kernel, tile=min(TILE, cols)),
        out_shape=(line(cols // 2), line(cols // 2), line(rows), jax.ShapeDtypeStruct(a.shape, a.dtype)),
        scratch_shapes=operands(rows, cols)[1:] + [pltpu.VMEM((1, cols), jnp.float32), pltpu.VMEM((1, cols), jnp.float32)],
        compiler_params=params(32),
        name="col_lse",
    )(a, b, r, c, logw, *prepared, *parts)


def plan_call(src_emb, a, b, c, w, parts, begin, rows):
    cols = b.shape[1]
    return pl.pallas_call(
        functools.partial(plan_kernel, begin=begin, tile=min(TILE // 2, cols)),
        out_shape=jax.ShapeDtypeStruct((EMB, rows), jnp.bfloat16),
        scratch_shapes=operands(rows, cols)[1:] + [pltpu.VMEM((rows, 128), jnp.float32), pltpu.VMEM((rows, EMB), jnp.float32)],
        compiler_params=params(32),
        cost_estimate=pl.CostEstimate(flops=4 * rows * cols * DEPTH, bytes_accessed=2 * 10**6, transcendentals=rows * cols),
        name="plan_grad",
    )(src_emb, a, b, c, w, *parts)


def rounded_sum(first, second):
    total = first.astype(jnp.float32) + second.astype(jnp.float32)
    return lax.reduce_precision(total, 8, 7).astype(jnp.bfloat16)


def swapped(value, axis, mask):
    return lax.ppermute(value, axis, [(k, k ^ mask) for k in range(lax.axis_size(axis))])


def exchanged(value, join):
    value = join(value, swapped(value, "tgt", 1))
    return value, swapped(value, "tgt", 3)


def spread(block):
    size = lax.axis_size("src")
    groups = [list(range(core, size, 2)) for core in range(2)]
    block = jnp.broadcast_to(block, (size // 2,) + block.shape)
    return lax.all_to_all(block, "src", 0, 0, axis_index_groups=groups, tiled=True)


def per_device(src_emb, src_pos, src_logw, tgt_emb, tgt_pos, tgt_logw):
    piece = tgt_emb.shape[1]
    half = piece * (lax.axis_size("src") // 2)
    logw = src_logw[None, :]

    count = EMB + 4
    own = jnp.concatenate([tgt_emb, tgt_pos, tgt_logw[None, :], tgt_logw[None, :]], 0).reshape(count * piece // 128, 128)
    own = spread(own).reshape(-1, count, piece).transpose(1, 0, 2).reshape(count, half)
    other = swapped(own, "src", 1)
    a, r, *near = static_call(src_emb, src_pos, own)
    lse, b, c, w = first_call(a, r, near, other)

    for step in range(ITERS):
        if step:
            lse = row_call(a, b, r, c, w, parts, ready, lse)
            prepared = col_prepare(b, c, (mine, theirs))
        else:
            prepared = col_guess(a, b, r, c, logw, lse)
        if step < ITERS - 1:
            ready = row_prepare(a, r, lse)
        mine, theirs, f, left = col_call(a, b, r, c, logw, prepared, exchanged(lse, joined))
        col = spread(joined(mine, swapped(theirs, "src", 1)).reshape(half // 128, 128))
        top = jnp.max(col, axis=0)
        col = (top + jnp.log(jnp.sum(jnp.exp(col - top), axis=0))).reshape(1, half)
        parts = (col, swapped(col, "src", 1))
    begin = lax.axis_index("src") // 2 * piece
    g_own = -LAM * EPS * lax.dynamic_slice_in_dim(col[0], begin, piece, 0)
    rows = src_emb.shape[1]
    grads = []
    for begin in range(0, rows, rows // 2):
        grads.append(exchanged(plan_call(src_emb, left, b, c, w, parts, begin, rows // 2), rounded_sum))
    first, second = (jnp.concatenate(part, axis=1).astype(jnp.float32) for part in zip(*grads))
    return f[0], g_own, first + second


def solution(mesh):
    placed = (
        P(None, "src"),
        P(None, "src"),
        P("src"),
        P(None, ("src", "tgt")),
        P(None, ("src", "tgt")),
        P(("src", "tgt")),
    )
    return jax.shard_map(
        per_device,
        mesh=mesh,
        in_specs=placed,
        out_specs=(P("src"), P(("src", "tgt")), P(None, "src")),
        check_vma=False,
    )
```

```python
import functools

import jax
import jax.numpy as jnp
from jax import lax
from jax.experimental import pallas as pl
from jax.experimental.pallas import tpu as pltpu
from jax.sharding import PartitionSpec as P

ITERS = 3
EPS = 0.25
RHO = 2.0
LAM = RHO / (RHO + EPS)
EMB = 64
DEPTH = 128
PACK = 80
MIB = 1 << 20
LOW, HIGH = 1e-25, 1e30


def pieces(value):
    high = value.astype(jnp.bfloat16).astype(jnp.float32)
    rest = value - high
    mid = rest.astype(jnp.bfloat16).astype(jnp.float32)
    low = (rest - mid).astype(jnp.bfloat16).astype(jnp.float32)
    return high, mid, low


def stacked(rows, height, width):
    index = lax.broadcasted_iota(jnp.int32, (height, width), 0)
    block = jnp.zeros((height, width), jnp.float32)
    for at, row in enumerate(rows):
        if row is not None:
            block = jnp.where(index == at, row, block)
    return block


def source_static(emb_ref, pos_ref, out_ref):
    width = emb_ref.shape[1]
    pos = pos_ref[...]
    emb = emb_ref[...].astype(jnp.float32)
    sq = jnp.sum(emb * emb, axis=0, keepdims=True)
    shift = -(sq * (1.0 / EMB) + pos[0:1] * pos[0:1] + pos[1:2] * pos[1:2]) * (1.0 / EPS)
    pos = pos * (2.0 / EPS)
    zero, one = jnp.zeros((1, width), jnp.float32), jnp.ones((1, width), jnp.float32)
    rows = [*pieces(pos[0:1]), *pieces(pos[1:2]), zero, zero, zero, one, one, one]
    extra = stacked(rows, 16, width)
    emb = emb * (2.0 / (EMB * EPS))
    pad = jnp.zeros((DEPTH - PACK, 128), jnp.float32)
    for at in range(0, width, 128):
        block = jnp.concatenate([emb[:, at : at + 128], extra[:, at : at + 128], pad], axis=0)
        out_ref[at : at + 128, :] = block.T.astype(jnp.bfloat16)
    return shift


def target_static(pack_ref, at, out_ref):
    width = pack_ref.shape[1]
    pack = pack_ref[...].astype(jnp.float32)
    emb, geo = pack[0:EMB], pack[EMB : EMB + 4]
    sq = jnp.sum(emb * emb, axis=0, keepdims=True)
    x, y = geo[0:1], geo[1:2]
    shift = -(sq * (1.0 / EMB) + x * x + y * y) * (1.0 / EPS)
    one = jnp.ones((1, width), jnp.float32)
    cut = slice(at, at + width)
    out_ref[0:EMB, cut] = pack_ref[0:EMB, :]
    out_ref[EMB:PACK, cut] = stacked([x, x, x, y, y, y, one, one, one], 16, width).astype(jnp.bfloat16)
    out_ref[PACK:DEPTH, cut] = jnp.zeros((DEPTH - PACK, width), jnp.bfloat16)
    return shift, geo[2:3]


def source_parts(shift):
    block = stacked([None] * 6 + [*pieces(shift)], 16, shift.shape[1]).astype(jnp.bfloat16)
    above = jnp.zeros((EMB, 128), jnp.bfloat16)
    below = jnp.zeros((DEPTH - PACK, 128), jnp.bfloat16)
    return [
        jnp.concatenate([above, block[:, at : at + 128], below], axis=0).T
        for at in range(0, shift.shape[1], 128)
    ]


def set_source(a_ref, shift, a_s):
    for index, part in enumerate(source_parts(shift)):
        cut = slice(index * 128, index * 128 + 128)
        a_s[cut, :] = a_ref[cut, :] + part


def target_parts(rows, shift):
    block = stacked([None] * 9 + [*pieces(shift)], 16, shift.shape[1])
    return (rows.astype(jnp.float32) + block).astype(jnp.bfloat16)


def set_target(b_ref, shift, b_s):
    b_s[0:EMB, :] = b_ref[0:EMB, :]
    b_s[EMB:PACK, :] = target_parts(b_ref[EMB:PACK, :], shift)
    b_s[PACK:DEPTH, :] = b_ref[PACK:DEPTH, :]


def loop_lanes(width, work):
    def step(index, carry):
        work(pl.ds(pl.multiple_of(index * 128, 128), 128))
        return carry

    lax.fori_loop(0, width // 128, step, 0)


def loop_source(a_ref, shift_of, a_s):
    def work(cut):
        a_s[cut, :] = a_ref[cut, :] + source_parts(shift_of(cut))[0]

    loop_lanes(a_ref.shape[0], work)


def loop_target(b_ref, shift_of, b_s):
    def work(cut):
        b_s[0:EMB, cut] = b_ref[0:EMB, cut]
        b_s[EMB:PACK, cut] = target_parts(b_ref[EMB:PACK, cut], shift_of(cut))
        b_s[PACK:DEPTH, cut] = b_ref[PACK:DEPTH, cut]

    loop_lanes(b_ref.shape[1], work)


def over_lanes(acc_s, out_s, join):
    for at in range(0, acc_s.shape[0], 128):
        out_s[:, at : at + 128] = join(acc_s[at : at + 128, :].T, axis=0, keepdims=True)


def loop_over_lanes(acc_s, out_s, join):
    def work(cut):
        out_s[:, cut] = join(acc_s[cut, :].T, axis=0, keepdims=True)

    loop_lanes(acc_s.shape[0], work)


def score(a, b):
    return lax.dot_general(a, b, (((1,), (0,)), ((), ())), preferred_element_type=jnp.float32)


def over_tiles(left, right, tile, work, width=None):
    width = right.shape[1] if width is None else width
    tile = min(tile, width)

    def step(index, carry):
        cut = pl.ds(pl.multiple_of(index * tile, tile), tile)
        work(cut, score(left[...], right[:, cut]))
        return carry

    lax.fori_loop(0, width // tile, step, 0)


def folded(value, join):
    part = value[:, 0:128]
    for col in range(128, value.shape[1], 128):
        part = join(part, value[:, col : col + 128])
    return part


def row_sums(left, right, acc_s, tile):
    def work(cut, value):
        acc_s[...] += folded(jnp.exp(value), jnp.add)

    over_tiles(left, right, tile, work)


def row_tops(left, right, acc_s, tile, width=None):
    def work(cut, value):
        acc_s[...] = jnp.maximum(acc_s[...], folded(value, jnp.maximum))

    over_tiles(left, right, tile, work, width)


def col_sums(left, right, out, tile):
    def work(cut, value):
        out[:, cut] = jnp.sum(jnp.exp(value), axis=0, keepdims=True)

    over_tiles(left, right, tile, work)


def col_tops(left, right, out, tile):
    def work(cut, value):
        out[:, cut] = jnp.max(value, axis=0, keepdims=True)

    over_tiles(left, right, tile, work)


def in_range(total):
    return jnp.logical_and(jnp.min(total) > LOW, jnp.max(total) < HIGH)


def static_kernel(emb_ref, pos_ref, pack_ref, a_ref, r_ref, b_ref, c_ref, w_ref, ready_ref, guess_ref, acc_ref, b_s):
    r_ref[...] = source_static(emb_ref, pos_ref, a_ref)
    c_ref[...], w_ref[...] = target_static(pack_ref, 0, b_ref)
    set_target(b_ref, c_ref[...] + w_ref[...], b_s)
    set_source(a_ref, r_ref[...], ready_ref)
    acc_ref[...] = jnp.full(acc_ref.shape, -jnp.inf, jnp.float32)
    row_tops(ready_ref, b_s, acc_ref, 512, min(512, b_s.shape[1]))
    over_lanes(acc_ref, guess_ref, jnp.max)
    set_source(a_ref, r_ref[...] - guess_ref[...], ready_ref)
    acc_ref[...] = jnp.zeros_like(acc_ref)
    row_sums(ready_ref, b_s, acc_ref, NEAR)


def row_finish(a_ref, r_ref, near_b_ref, near_of, ready_ref, guess_ref, acc_ref, out_ref, a_s, near_s, far_s, acc_s, guess_s, total_s):
    acc_s[...] = acc_ref[...]
    row_sums(ready_ref, far_s, acc_s, FAR)
    over_lanes(acc_s, total_s, jnp.sum)
    guess_s[...] = guess_ref[...]

    @pl.when(jnp.logical_not(in_range(total_s[...])))
    def _():
        loop_target(near_b_ref, near_of, near_s)
        loop_source(a_ref, lambda cut: r_ref[:, cut], a_s)
        acc_s[...] = jnp.full(acc_s.shape, -jnp.inf, jnp.float32)
        row_tops(a_s, near_s, acc_s, SMALL)
        row_tops(a_s, far_s, acc_s, SMALL)
        loop_over_lanes(acc_s, guess_s, jnp.max)
        loop_source(a_ref, lambda cut: r_ref[:, cut] - guess_s[:, cut], a_s)
        acc_s[...] = jnp.zeros_like(acc_s)
        row_sums(a_s, near_s, acc_s, SMALL)
        row_sums(a_s, far_s, acc_s, SMALL)
        loop_over_lanes(acc_s, total_s, jnp.sum)

    out_ref[...] = guess_s[...] + jnp.log(total_s[...])


def first_kernel(a_ref, r_ref, near_b_ref, near_c_ref, near_w_ref, pack_ref, ready_ref, guess_ref, acc_ref, out_ref, b_ref, c_ref, w_ref, a_s, near_s, far_s, *rest):
    c_ref[...], w_ref[...] = target_static(pack_ref, 0, b_ref)
    set_target(b_ref, c_ref[...] + w_ref[...], far_s)
    near_of = lambda cut: near_c_ref[:, cut] + near_w_ref[:, cut]
    row_finish(a_ref, r_ref, near_b_ref, near_of, ready_ref, guess_ref, acc_ref, out_ref, a_s, near_s, far_s, *rest)


def near_kernel(b_ref, c_ref, w_ref, lse_ref, ready_ref, acc_ref, b_s):
    set_target(b_ref, c_ref[...] + w_ref[...] - LAM * lse_ref[...], b_s)
    acc_ref[...] = jnp.zeros_like(acc_ref)
    row_sums(ready_ref, b_s, acc_ref, NEAR)


def row_kernel(a_ref, r_ref, near_b_ref, near_c_ref, near_w_ref, near_lse_ref, b_ref, c_ref, w_ref, lse_ref, ready_ref, guess_ref, acc_ref, out_ref, a_s, near_s, far_s, *rest):
    set_target(b_ref, c_ref[...] + w_ref[...] - LAM * lse_ref[...], far_s)
    near_of = lambda cut: near_c_ref[:, cut] + near_w_ref[:, cut] - LAM * near_lse_ref[:, cut]
    row_finish(a_ref, r_ref, near_b_ref, near_of, ready_ref, guess_ref, acc_ref, out_ref, a_s, near_s, far_s, *rest)


def joined(first, second):
    top = jnp.maximum(first, second)
    return top + jnp.log(jnp.exp(first - top) + jnp.exp(second - top))


def prepare_kernel(a_ref, r_ref, lse_ref, near_b_ref, near_c_ref, near_guess_ref, far_b_ref, far_c_ref, far_guess_ref, *outs):
    near_ref, far_ref, *rest = outs
    set_target(far_b_ref, far_c_ref[...] - far_guess_ref[...], far_ref)
    set_target(near_b_ref, near_c_ref[...] - near_guess_ref[...], near_ref)
    for ready_ref in rest:
        set_source(a_ref, r_ref[...] - lse_ref[...], ready_ref)


def guess_kernel(a_ref, r_ref, lse_ref, near_b_ref, near_c_ref, far_b_ref, far_c_ref, logw_ref, near_ref, far_ref, ready_ref, near_guess_ref, far_guess_ref):
    set_source(a_ref, r_ref[...] + logw_ref[...] - LAM * lse_ref[...], ready_ref)
    for b_ref, c_ref, out_ref, top_ref in (
        (near_b_ref, near_c_ref, near_ref, near_guess_ref),
        (far_b_ref, far_c_ref, far_ref, far_guess_ref),
    ):
        set_target(b_ref, c_ref[...], out_ref)
        col_tops(ready_ref, out_ref, top_ref, 512)
        out_ref[EMB:PACK, :] = target_parts(b_ref[EMB:PACK, :], c_ref[...] - top_ref[...])
    set_source(a_ref, r_ref[...] - lse_ref[...], ready_ref)


def col_finish(left, b_ref, c_ref, ready_ref, guess_ref, out_ref, b_s, guess_s, total_s):
    col_sums(left, ready_ref, total_s, COLS)
    guess_s[...] = guess_ref[...]

    @pl.when(jnp.logical_not(in_range(total_s[...])))
    def _():
        loop_target(b_ref, lambda cut: c_ref[:, cut], b_s)
        col_tops(left, b_s, guess_s, SMALL)
        loop_target(b_ref, lambda cut: c_ref[:, cut] - guess_s[:, cut], b_s)
        col_sums(left, b_s, total_s, SMALL)

    out_ref[...] = guess_s[...] + jnp.log(total_s[...])


def far_col_kernel(a_ref, r_ref, logw_ref, one_ref, two_ref, b_ref, c_ref, ready_ref, guess_ref, out_ref, f_ref, left_ref, *rest):
    lse = joined(one_ref[...], two_ref[...])
    f_ref[...] = -LAM * EPS * lse
    set_source(a_ref, r_ref[...] + logw_ref[...] - LAM * lse, left_ref)
    col_finish(left_ref, b_ref, c_ref, ready_ref, guess_ref, out_ref, *rest)


def near_col_kernel(left_ref, b_ref, c_ref, ready_ref, guess_ref, out_ref, *rest):
    col_finish(left_ref, b_ref, c_ref, ready_ref, guess_ref, out_ref, *rest)


def plan_sums(left, b_s, mass_s, pull_s, tile):
    def work(cut, value):
        plan = jnp.exp(value)
        mass_s[...] += folded(plan, jnp.add)
        pull_s[...] += lax.dot_general(
            plan.astype(jnp.bfloat16),
            b_s[0:EMB, cut],
            (((1,), (1,)), ((), ())),
            preferred_element_type=jnp.float32,
        )

    over_tiles(left, b_s, tile, work)


def near_plan_kernel(left_ref, b_ref, c_ref, w_ref, lse_ref, mass_ref, pull_ref, b_s):
    set_target(b_ref, c_ref[...] + w_ref[...] - LAM * lse_ref[...], b_s)
    mass_ref[...] = jnp.zeros_like(mass_ref)
    pull_ref[...] = jnp.zeros_like(pull_ref)
    plan_sums(left_ref, b_s, mass_ref, pull_ref, PLAN)


def plan_kernel(emb_ref, left_ref, b_ref, c_ref, w_ref, lse_ref, mass_ref, pull_ref, out_ref, b_s, mass_s, pull_s, *, begin):
    rows = out_ref.shape[1]
    span = slice(begin, begin + rows)
    set_target(b_ref, c_ref[...] + w_ref[...] - LAM * lse_ref[...], b_s)
    mass_s[...] = mass_ref[span, :]
    pull_s[...] = pull_ref[span, :]
    plan_sums(left_ref.at[span, :], b_s, mass_s, pull_s, 2 * PLAN)
    for at in range(0, rows, 128):
        mass = jnp.sum(mass_s[at : at + 128, :].T, axis=0, keepdims=True)
        pull = jnp.concatenate([pull_s[at : at + 128, :], jnp.zeros((128, 128 - EMB), jnp.float32)], axis=1).T
        grad = mass * emb_ref[:, begin + at : begin + at + 128].astype(jnp.float32) - pull[0:EMB, :]
        out_ref[:, at : at + 128] = grad.astype(out_ref.dtype)


NEAR, FAR, COLS, PLAN = 1024, 2048, 1024, 512
SMALL = 128


def f32(*shape):
    return jax.ShapeDtypeStruct(shape, jnp.float32)


def bf16(*shape):
    return jax.ShapeDtypeStruct(shape, jnp.bfloat16)


def call(kernel, out_shape, scratch, name, *args, flops=10**8):
    return pl.pallas_call(
        kernel,
        out_shape=out_shape,
        scratch_shapes=[pltpu.VMEM(like.shape, like.dtype) for like in scratch],
        compiler_params=pltpu.CompilerParams(vmem_limit_bytes=32 * MIB),
        cost_estimate=pl.CostEstimate(flops=flops, bytes_accessed=2 * 10**6, transcendentals=0),
        name=name,
    )(*args)


def rounded_sum(first, second):
    total = first.astype(jnp.float32) + second.astype(jnp.float32)
    return lax.reduce_precision(total, 8, 7).astype(jnp.bfloat16)


def swapped(value, axis, mask):
    return lax.ppermute(value, axis, [(k, k ^ mask) for k in range(lax.axis_size(axis))])


def exchanged(value, join):
    value = join(value, swapped(value, "tgt", 1))
    return value, swapped(value, "tgt", 3)


def spread(block):
    size = lax.axis_size("src")
    groups = [list(range(core, size, 2)) for core in range(2)]
    block = jnp.broadcast_to(block, (size // 2,) + block.shape)
    return lax.all_to_all(block, "src", 0, 0, axis_index_groups=groups, tiled=True)


def per_device(src_emb, src_pos, src_logw, tgt_emb, tgt_pos, tgt_logw):
    piece = tgt_emb.shape[1]
    half = piece * (lax.axis_size("src") // 2)
    rows = src_emb.shape[1]
    logw = src_logw[None, :]
    pass_flops = 2 * rows * half * DEPTH
    left_like, right_like = bf16(rows, DEPTH), bf16(DEPTH, half)
    row_line, half_line, acc_like = f32(1, rows), f32(1, half), f32(rows, 128)
    row_scratch = (left_like, right_like, right_like, acc_like, row_line, row_line)
    col_scratch = (right_like, half_line, half_line)

    count = EMB + 4
    own = jnp.concatenate([tgt_emb, tgt_pos, tgt_logw[None, :], tgt_logw[None, :]], 0).reshape(count * piece // 128, 128)
    own = spread(own).reshape(-1, count, piece).transpose(1, 0, 2).reshape(count, half)
    other = swapped(own, "src", 1)
    a, r, near_b, near_c, near_w, ready, guess, acc = call(
        static_kernel,
        (left_like, row_line, right_like, half_line, half_line, left_like, row_line, acc_like),
        (right_like,),
        "static_parts",
        src_emb, src_pos, own,
        flops=pass_flops,
    )
    lse, far_b, far_c, far_w = call(
        first_kernel,
        (row_line, right_like, half_line, half_line),
        row_scratch,
        "first_row_lse",
        a, r, near_b, near_c, near_w, other, ready, guess, acc,
        flops=pass_flops,
    )
    near, far = (near_b, near_c, near_w), (far_b, far_c, far_w)

    for step in range(ITERS):
        if step:
            acc = call(near_kernel, acc_like, (right_like,), "near_row_lse", *near, col, ready, flops=pass_flops)
            lse = call(
                row_kernel, row_line, row_scratch, "row_lse",
                a, r, *near, col, *far, far_col, ready, lse, acc,
                flops=pass_flops,
            )
            more = () if step == ITERS - 1 else (left_like,)
            near_ready, far_ready, *ready = call(
                prepare_kernel, (right_like, right_like, *more), (), "prepare",
                a, r, lse, near_b, near_c, mine, far_b, far_c, theirs,
            )
            ready = ready[0] if ready else None
        else:
            near_ready, far_ready, ready, mine, theirs = call(
                guess_kernel, (right_like, right_like, left_like, half_line, half_line), (), "col_guess",
                a, r, lse, near_b, near_c, far_b, far_c, logw,
                flops=2 * pass_flops,
            )
        theirs, f, left = call(
            far_col_kernel, (half_line, row_line, left_like), col_scratch, "far_col_lse",
            a, r, logw, *exchanged(lse, joined), far_b, far_c, far_ready, theirs,
            flops=pass_flops,
        )
        moved = swapped(theirs, "src", 1)
        mine = call(
            near_col_kernel, half_line, col_scratch, "near_col_lse",
            left, near_b, near_c, near_ready, mine,
            flops=pass_flops,
        )
        col = spread(joined(mine, moved).reshape(half // 128, 128))
        top = jnp.max(col, axis=0)
        col = (top + jnp.log(jnp.sum(jnp.exp(col - top), axis=0))).reshape(1, half)
        far_col = swapped(col, "src", 1)
    begin = lax.axis_index("src") // 2 * piece
    g_own = -LAM * EPS * lax.dynamic_slice_in_dim(col[0], begin, piece, 0)
    mass, pull = call(
        near_plan_kernel, (acc_like, f32(rows, EMB)), (right_like,), "near_plan",
        left, *near, col,
        flops=2 * pass_flops,
    )
    grads = []
    for begin in range(0, rows, rows // 2):
        grad = call(
            functools.partial(plan_kernel, begin=begin),
            bf16(EMB, rows // 2),
            (right_like, f32(rows // 2, 128), f32(rows // 2, EMB)),
            "plan_grad",
            src_emb, left, *far, far_col, mass, pull,
            flops=pass_flops,
        )
        grads.append(exchanged(grad, rounded_sum))
    first, second = (jnp.concatenate(part, axis=1).astype(jnp.float32) for part in zip(*grads))
    return f[0], g_own, first + second


def solution(mesh):
    placed = (
        P(None, "src"),
        P(None, "src"),
        P("src"),
        P(None, ("src", "tgt")),
        P(None, ("src", "tgt")),
        P(("src", "tgt")),
    )
    return jax.shard_map(
        per_device,
        mesh=mesh,
        in_specs=placed,
        out_specs=(P("src"), P(("src", "tgt")), P(None, "src")),
        check_vma=False,
    )
```

```python
import functools

import jax
import jax.numpy as jnp
from jax import lax
from jax.experimental import pallas as pl
from jax.experimental.pallas import tpu as pltpu
from jax.sharding import PartitionSpec as P

ITERS = 3
EPS = 0.25
RHO = 2.0
LAM = RHO / (RHO + EPS)
EMB = 64
DEPTH = 128
PACK = 80
MIB = 1 << 20
LOW, HIGH = 1e-25, 1e30


def pieces(value):
    high = value.astype(jnp.bfloat16).astype(jnp.float32)
    rest = value - high
    mid = rest.astype(jnp.bfloat16).astype(jnp.float32)
    low = (rest - mid).astype(jnp.bfloat16).astype(jnp.float32)
    return high, mid, low


def stacked(rows, height, width):
    index = lax.broadcasted_iota(jnp.int32, (height, width), 0)
    block = jnp.zeros((height, width), jnp.float32)
    for at, row in enumerate(rows):
        if row is not None:
            block = jnp.where(index == at, row, block)
    return block


def source_static(emb_ref, pos_ref, out_ref, shift_ref):
    width = emb_ref.shape[1]
    pos = pos_ref[...]
    emb = emb_ref[...].astype(jnp.float32)
    sq = jnp.sum(emb * emb, axis=0, keepdims=True)
    shift = -(sq * (1.0 / EMB) + pos[0:1] * pos[0:1] + pos[1:2] * pos[1:2]) * (1.0 / EPS)
    pos = pos * (2.0 / EPS)
    one = jnp.ones((1, width), jnp.float32)
    extra = stacked([*pieces(pos[0:1]), *pieces(pos[1:2]), one, one, one], 16, width)
    emb = emb * (2.0 / (EMB * EPS))
    pad = jnp.zeros((DEPTH - PACK, 128), jnp.float32)
    for at in range(0, width, 128):
        block = jnp.concatenate([emb[:, at : at + 128], extra[:, at : at + 128], pad], axis=0)
        out_ref[at : at + 128, :] = block.T.astype(jnp.bfloat16)
        shift_ref[at // 128 : at // 128 + 1, :] = shift[:, at : at + 128]


def target_static(pack_ref, at, out_ref):
    width = pack_ref.shape[1]
    pack = pack_ref[...].astype(jnp.float32)
    emb, geo = pack[0:EMB], pack[EMB : EMB + 4]
    sq = jnp.sum(emb * emb, axis=0, keepdims=True)
    x, y = geo[0:1], geo[1:2]
    shift = -(sq * (1.0 / EMB) + x * x + y * y) * (1.0 / EPS)
    cut = slice(at, at + width)
    out_ref[0:EMB, cut] = pack_ref[0:EMB, :]
    out_ref[EMB:PACK, cut] = stacked([x, x, x, y, y, y], 16, width).astype(jnp.bfloat16)
    depth = lax.broadcasted_iota(jnp.int32, (DEPTH - PACK, width), 0)
    out_ref[PACK:DEPTH, cut] = jnp.where(depth < 24, 1.0, 0.0).astype(jnp.bfloat16)
    return shift, geo[2:3]


def set_source(a_ref, shift, a_s):
    above = jnp.zeros((PACK, 128), jnp.float32)
    below = jnp.zeros((DEPTH - PACK - 24, 128), jnp.float32)
    turned = jnp.concatenate([above, *pieces(shift), below], axis=0).T
    own = lax.rem(lax.broadcasted_iota(jnp.int32, (128, DEPTH), 1), 8)
    for index in range(8):
        cut = slice(index * 128, index * 128 + 128)
        a_s[cut, :] = a_ref[cut, :] + jnp.where(own == index, turned, 0.0).astype(jnp.bfloat16)


def target_parts(rows, shift):
    block = stacked([None] * 6 + [*pieces(shift)], 16, shift.shape[1])
    return (rows.astype(jnp.float32) + block).astype(jnp.bfloat16)


def set_target(b_ref, shift, b_s):
    b_s[0:EMB, :] = b_ref[0:EMB, :]
    b_s[EMB:PACK, :] = target_parts(b_ref[EMB:PACK, :], shift)
    b_s[PACK:DEPTH, :] = b_ref[PACK:DEPTH, :]


def loop_lanes(width, work):
    def step(index, carry):
        work(pl.ds(pl.multiple_of(index * 128, 128), 128))
        return carry

    lax.fori_loop(0, width // 128, step, 0)


def loop_target(b_ref, shift_of, b_s):
    def work(cut):
        b_s[0:EMB, cut] = b_ref[0:EMB, cut]
        b_s[EMB:PACK, cut] = target_parts(b_ref[EMB:PACK, cut], shift_of(cut))
        b_s[PACK:DEPTH, cut] = b_ref[PACK:DEPTH, cut]

    loop_lanes(b_ref.shape[1], work)


def over_lanes(acc_s, out_s, join):
    for index in range(8):
        out_s[index : index + 1, :] = join(acc_s[index * 128 : index * 128 + 128, :].T, axis=0, keepdims=True)


def loop_over_lanes(acc_s, out_s, join):
    def step(index, carry):
        cut = pl.ds(pl.multiple_of(index * 128, 128), 128)
        out_s[pl.ds(index, 1), :] = join(acc_s[cut, :].T, axis=0, keepdims=True)
        return carry

    lax.fori_loop(0, 8, step, 0)


def score(a, b):
    return lax.dot_general(a, b, (((1,), (0,)), ((), ())), preferred_element_type=jnp.float32)


def over_tiles(left, right, tile, work, width=None):
    width = right.shape[1] if width is None else width
    tile = min(tile, width)

    def step(index, carry):
        cut = pl.ds(pl.multiple_of(index * tile, tile), tile)
        work(cut, score(left[...], right[:, cut]))
        return carry

    lax.fori_loop(0, width // tile, step, 0)


def folded(value, join):
    part = value[:, 0:128]
    for col in range(128, value.shape[1], 128):
        part = join(part, value[:, col : col + 128])
    return part


def row_sums(left, right, acc_s, tile):
    def work(cut, value):
        acc_s[...] += folded(jnp.exp(value), jnp.add)

    over_tiles(left, right, tile, work)


def row_tops(left, right, acc_s, tile, width=None):
    def work(cut, value):
        acc_s[...] = jnp.maximum(acc_s[...], folded(value, jnp.maximum))

    over_tiles(left, right, tile, work, width)


def col_sums(left, right, out, tile):
    def work(cut, value):
        part = jnp.sum(jnp.exp(value).reshape(-1, 16, value.shape[1]), axis=0)
        out[:, cut] = jnp.sum(part, axis=0, keepdims=True)

    over_tiles(left, right, tile, work)


def col_tops(left, right, out, tile):
    def work(cut, value):
        out[:, cut] = jnp.max(value, axis=0, keepdims=True)

    over_tiles(left, right, tile, work)


def in_range(total):
    return jnp.logical_and(jnp.min(total) > LOW, jnp.max(total) < HIGH)


def static_kernel(emb_ref, pos_ref, pack_ref, a_ref, r_ref, b_ref, c_ref, w_ref, ready_ref, guess_ref, acc_ref, b_s):
    source_static(emb_ref, pos_ref, a_ref, r_ref)
    c_ref[...], w_ref[...] = target_static(pack_ref, 0, b_ref)
    set_target(b_ref, c_ref[...] + w_ref[...], b_s)
    set_source(a_ref, r_ref[...], ready_ref)
    acc_ref[...] = jnp.full(acc_ref.shape, -jnp.inf, jnp.float32)
    row_tops(ready_ref, b_s, acc_ref, 512, min(512, b_s.shape[1]))
    over_lanes(acc_ref, guess_ref, jnp.max)
    set_source(a_ref, r_ref[...] - guess_ref[...], ready_ref)
    acc_ref[...] = jnp.zeros_like(acc_ref)
    row_sums(ready_ref, b_s, acc_ref, NEAR)


def row_finish(a_ref, r_ref, near_b_ref, near_of, ready_ref, guess_ref, acc_ref, out_ref, a_s, near_s, far_s, acc_s, guess_s, total_s):
    acc_s[...] = acc_ref[...]
    row_sums(ready_ref, far_s, acc_s, FAR)
    over_lanes(acc_s, total_s, jnp.sum)
    guess_s[...] = guess_ref[...]

    @pl.when(jnp.logical_not(in_range(total_s[...])))
    def _():
        loop_target(near_b_ref, near_of, near_s)
        set_source(a_ref, r_ref[...], a_s)
        acc_s[...] = jnp.full(acc_s.shape, -jnp.inf, jnp.float32)
        row_tops(a_s, near_s, acc_s, SMALL)
        row_tops(a_s, far_s, acc_s, SMALL)
        loop_over_lanes(acc_s, guess_s, jnp.max)
        set_source(a_ref, r_ref[...] - guess_s[...], a_s)
        acc_s[...] = jnp.zeros_like(acc_s)
        row_sums(a_s, near_s, acc_s, SMALL)
        row_sums(a_s, far_s, acc_s, SMALL)
        loop_over_lanes(acc_s, total_s, jnp.sum)

    out_ref[...] = guess_s[...] + jnp.log(total_s[...])


def first_kernel(a_ref, r_ref, near_b_ref, near_c_ref, near_w_ref, pack_ref, ready_ref, guess_ref, acc_ref, out_ref, b_ref, c_ref, w_ref, a_s, near_s, far_s, *rest):
    c_ref[...], w_ref[...] = target_static(pack_ref, 0, b_ref)
    set_target(b_ref, c_ref[...] + w_ref[...], far_s)
    near_of = lambda cut: near_c_ref[:, cut] + near_w_ref[:, cut]
    row_finish(a_ref, r_ref, near_b_ref, near_of, ready_ref, guess_ref, acc_ref, out_ref, a_s, near_s, far_s, *rest)


def near_kernel(b_ref, c_ref, w_ref, lse_ref, ready_ref, acc_ref, b_s):
    set_target(b_ref, c_ref[...] + w_ref[...] - LAM * lse_ref[...], b_s)
    acc_ref[...] = jnp.zeros_like(acc_ref)
    row_sums(ready_ref, b_s, acc_ref, NEAR)


def row_kernel(a_ref, r_ref, near_b_ref, near_c_ref, near_w_ref, near_lse_ref, b_ref, c_ref, w_ref, lse_ref, ready_ref, guess_ref, acc_ref, out_ref, a_s, near_s, far_s, *rest):
    set_target(b_ref, c_ref[...] + w_ref[...] - LAM * lse_ref[...], far_s)
    near_of = lambda cut: near_c_ref[:, cut] + near_w_ref[:, cut] - LAM * near_lse_ref[:, cut]
    row_finish(a_ref, r_ref, near_b_ref, near_of, ready_ref, guess_ref, acc_ref, out_ref, a_s, near_s, far_s, *rest)


def joined(first, second):
    top = jnp.maximum(first, second)
    return top + jnp.log(jnp.exp(first - top) + jnp.exp(second - top))


def prepare_kernel(a_ref, r_ref, lse_ref, near_b_ref, near_c_ref, near_guess_ref, far_b_ref, far_c_ref, far_guess_ref, *outs):
    near_ref, far_ref, *rest = outs
    set_target(far_b_ref, far_c_ref[...] - far_guess_ref[...], far_ref)
    set_target(near_b_ref, near_c_ref[...] - near_guess_ref[...], near_ref)
    for ready_ref in rest:
        set_source(a_ref, r_ref[...] - lse_ref[...], ready_ref)


def guess_kernel(a_ref, r_ref, lse_ref, near_b_ref, near_c_ref, far_b_ref, far_c_ref, logw_ref, near_ref, far_ref, ready_ref, near_guess_ref, far_guess_ref):
    set_source(a_ref, r_ref[...] + logw_ref[...] - LAM * lse_ref[...], ready_ref)
    for b_ref, c_ref, out_ref, top_ref in (
        (near_b_ref, near_c_ref, near_ref, near_guess_ref),
        (far_b_ref, far_c_ref, far_ref, far_guess_ref),
    ):
        set_target(b_ref, c_ref[...], out_ref)
        col_tops(ready_ref, out_ref, top_ref, 512)
        out_ref[EMB:PACK, :] = target_parts(b_ref[EMB:PACK, :], c_ref[...] - top_ref[...])
    set_source(a_ref, r_ref[...] - lse_ref[...], ready_ref)


def col_finish(left, b_ref, c_ref, ready_ref, guess_ref, out_ref, b_s, guess_s, total_s):
    col_sums(left, ready_ref, total_s, COLS)
    guess_s[...] = guess_ref[...]

    @pl.when(jnp.logical_not(in_range(total_s[...])))
    def _():
        loop_target(b_ref, lambda cut: c_ref[:, cut], b_s)
        col_tops(left, b_s, guess_s, SMALL)
        loop_target(b_ref, lambda cut: c_ref[:, cut] - guess_s[:, cut], b_s)
        col_sums(left, b_s, total_s, SMALL)

    out_ref[...] = guess_s[...] + jnp.log(total_s[...])


def far_col_kernel(a_ref, r_ref, logw_ref, one_ref, two_ref, b_ref, c_ref, ready_ref, guess_ref, out_ref, f_ref, left_ref, *rest):
    lse = joined(one_ref[...], two_ref[...])
    f_ref[...] = -LAM * EPS * lse
    set_source(a_ref, r_ref[...] + logw_ref[...] - LAM * lse, left_ref)
    col_finish(left_ref, b_ref, c_ref, ready_ref, guess_ref, out_ref, *rest)


def near_col_kernel(left_ref, b_ref, c_ref, ready_ref, guess_ref, out_ref, *rest):
    col_finish(left_ref, b_ref, c_ref, ready_ref, guess_ref, out_ref, *rest)


def plan_sums(left, b_s, mass_s, pull_s, tile):
    def work(cut, value):
        plan = jnp.exp(value)
        mass_s[...] += folded(plan, jnp.add)
        pull_s[...] += lax.dot_general(
            plan.astype(jnp.bfloat16),
            b_s[0:EMB, cut],
            (((1,), (1,)), ((), ())),
            preferred_element_type=jnp.float32,
        )

    over_tiles(left, b_s, tile, work)


def plan_pass(left_ref, b_ref, c_ref, w_ref, lse_ref, b_s, mass_s, pull_s, tile):
    set_target(b_ref, c_ref[...] + w_ref[...] - LAM * lse_ref[...], b_s)
    plan_sums(left_ref, b_s, mass_s, pull_s, tile)


def near_plan_kernel(left_ref, b_ref, c_ref, w_ref, lse_ref, mass_ref, pull_ref, b_s):
    mass_ref[...] = jnp.zeros_like(mass_ref)
    pull_ref[...] = jnp.zeros_like(pull_ref)
    plan_pass(left_ref.at[0 : mass_ref.shape[0], :], b_ref, c_ref, w_ref, lse_ref, b_s, mass_ref, pull_ref, PLAN)


def plan_finish(emb_ref, begin, mass_s, pull_s, out_ref):
    for at in range(0, out_ref.shape[1], 128):
        mass = jnp.sum(mass_s[at : at + 128, :].T, axis=0, keepdims=True)
        pull = jnp.concatenate([pull_s[at : at + 128, :], jnp.zeros((128, 128 - EMB), jnp.float32)], axis=1).T
        grad = mass * emb_ref[:, begin + at : begin + at + 128].astype(jnp.float32) - pull[0:EMB, :]
        out_ref[:, at : at + 128] = grad.astype(out_ref.dtype)


def first_plan_kernel(emb_ref, left_ref, b_ref, c_ref, w_ref, lse_ref, mass_ref, pull_ref, out_ref, b_s, mass_s, pull_s):
    mass_s[...] = mass_ref[...]
    pull_s[...] = pull_ref[...]
    plan_pass(left_ref.at[0 : out_ref.shape[1], :], b_ref, c_ref, w_ref, lse_ref, b_s, mass_s, pull_s, 2 * PLAN)
    plan_finish(emb_ref, 0, mass_s, pull_s, out_ref)


def last_plan_kernel(emb_ref, left_ref, near_b_ref, near_c_ref, near_w_ref, near_lse_ref, b_ref, c_ref, w_ref, lse_ref, out_ref, b_s, mass_s, pull_s):
    mass_s[...] = jnp.zeros_like(mass_s)
    pull_s[...] = jnp.zeros_like(pull_s)
    begin = emb_ref.shape[1] - out_ref.shape[1]
    left = left_ref.at[begin : emb_ref.shape[1], :]
    plan_pass(left, near_b_ref, near_c_ref, near_w_ref, near_lse_ref, b_s, mass_s, pull_s, PLAN)
    plan_pass(left, b_ref, c_ref, w_ref, lse_ref, b_s, mass_s, pull_s, PLAN)
    plan_finish(emb_ref, begin, mass_s, pull_s, out_ref)


NEAR, FAR, COLS, PLAN = 1024, 2048, 1024, 512
SMALL = 128


def f32(*shape):
    return jax.ShapeDtypeStruct(shape, jnp.float32)


def bf16(*shape):
    return jax.ShapeDtypeStruct(shape, jnp.bfloat16)


def call(kernel, out_shape, scratch, name, *args, flops=10**8):
    return pl.pallas_call(
        kernel,
        out_shape=out_shape,
        scratch_shapes=[pltpu.VMEM(like.shape, like.dtype) for like in scratch],
        compiler_params=pltpu.CompilerParams(vmem_limit_bytes=32 * MIB),
        cost_estimate=pl.CostEstimate(flops=flops, bytes_accessed=2 * 10**6, transcendentals=0),
        name=name,
    )(*args)


def rounded_sum(first, second):
    total = first.astype(jnp.float32) + second.astype(jnp.float32)
    return lax.reduce_precision(total, 8, 7).astype(jnp.bfloat16)


def swapped(value, axis, mask):
    return lax.ppermute(value, axis, [(k, k ^ mask) for k in range(lax.axis_size(axis))])


def exchanged(value, join):
    value = join(value, swapped(value, "tgt", 1))
    return value, swapped(value, "tgt", 3)


def spread(block):
    size = lax.axis_size("src")
    groups = [list(range(core, size, 2)) for core in range(2)]
    block = jnp.broadcast_to(block, (size // 2,) + block.shape)
    return lax.all_to_all(block, "src", 0, 0, axis_index_groups=groups, tiled=True)


def per_device(src_emb, src_pos, src_logw, tgt_emb, tgt_pos, tgt_logw):
    piece = tgt_emb.shape[1]
    half = piece * (lax.axis_size("src") // 2)
    rows = src_emb.shape[1]
    logw = src_logw.reshape(8, rows // 8)
    pass_flops = 2 * rows * half * DEPTH
    left_like, right_like = bf16(rows, DEPTH), bf16(DEPTH, half)
    row_line, half_line, acc_like = f32(8, rows // 8), f32(1, half), f32(rows, 128)
    row_scratch = (left_like, right_like, right_like, acc_like, row_line, row_line)
    col_scratch = (right_like, half_line, half_line)

    count = EMB + 4
    own = jnp.concatenate([tgt_emb, tgt_pos, tgt_logw[None, :], tgt_logw[None, :]], 0).reshape(count * piece // 128, 128)
    own = spread(own).reshape(-1, count, piece).transpose(1, 0, 2).reshape(count, half)
    other = swapped(own, "src", 1)
    a, r, near_b, near_c, near_w, ready, guess, acc = call(
        static_kernel,
        (left_like, row_line, right_like, half_line, half_line, left_like, row_line, acc_like),
        (right_like,),
        "static_parts",
        src_emb, src_pos, own,
        flops=pass_flops,
    )
    lse, far_b, far_c, far_w = call(
        first_kernel,
        (row_line, right_like, half_line, half_line),
        row_scratch,
        "first_row_lse",
        a, r, near_b, near_c, near_w, other, ready, guess, acc,
        flops=pass_flops,
    )
    near, far = (near_b, near_c, near_w), (far_b, far_c, far_w)

    for step in range(ITERS):
        if step:
            acc = call(near_kernel, acc_like, (right_like,), "near_row_lse", *near, col, ready, flops=pass_flops)
            lse = call(
                row_kernel, row_line, row_scratch, "row_lse",
                a, r, *near, col, *far, far_col, ready, lse, acc,
                flops=pass_flops,
            )
            more = () if step == ITERS - 1 else (left_like,)
            near_ready, far_ready, *ready = call(
                prepare_kernel, (right_like, right_like, *more), (), "prepare",
                a, r, lse, near_b, near_c, mine, far_b, far_c, theirs,
            )
            ready = ready[0] if ready else None
        else:
            near_ready, far_ready, ready, mine, theirs = call(
                guess_kernel, (right_like, right_like, left_like, half_line, half_line), (), "col_guess",
                a, r, lse, near_b, near_c, far_b, far_c, logw,
                flops=2 * pass_flops,
            )
        theirs, f, left = call(
            far_col_kernel, (half_line, row_line, left_like), col_scratch, "far_col_lse",
            a, r, logw, *exchanged(lse, joined), far_b, far_c, far_ready, theirs,
            flops=pass_flops,
        )
        moved = swapped(theirs, "src", 1)
        mine = call(
            near_col_kernel, half_line, col_scratch, "near_col_lse",
            left, near_b, near_c, near_ready, mine,
            flops=pass_flops,
        )
        col = spread(joined(mine, moved).reshape(half // 128, 128))
        top = jnp.max(col, axis=0)
        col = (top + jnp.log(jnp.sum(jnp.exp(col - top), axis=0))).reshape(1, half)
        far_col = swapped(col, "src", 1)
    begin = lax.axis_index("src") // 2 * piece
    g_own = -LAM * EPS * lax.dynamic_slice_in_dim(col[0], begin, piece, 0)
    part = rows // 2
    sums_like = (f32(part, 128), f32(part, EMB))
    sums = call(
        near_plan_kernel, sums_like, (right_like,), "near_plan",
        left, *near, col,
        flops=pass_flops,
    )
    grad = call(
        first_plan_kernel, bf16(EMB, part), (right_like, *sums_like), "first_plan",
        src_emb, left, *far, far_col, *sums,
        flops=pass_flops,
    )
    grads = [exchanged(grad, rounded_sum)]
    grad = call(
        last_plan_kernel, bf16(EMB, part), (right_like, *sums_like), "last_plan",
        src_emb, left, *near, col, *far, far_col,
        flops=2 * pass_flops,
    )
    grads.append(exchanged(grad, rounded_sum))
    first, second = (jnp.concatenate(part, axis=1).astype(jnp.float32) for part in zip(*grads))
    return f.reshape(rows), g_own, first + second


def solution(mesh):
    placed = (
        P(None, "src"),
        P(None, "src"),
        P("src"),
        P(None, ("src", "tgt")),
        P(None, ("src", "tgt")),
        P(("src", "tgt")),
    )
    return jax.shard_map(
        per_device,
        mesh=mesh,
        in_specs=placed,
        out_specs=(P("src"), P(("src", "tgt")), P(None, "src")),
        check_vma=False,
    )
```

```python
import functools

import jax
import jax.numpy as jnp
from jax import lax
from jax.experimental import pallas as pl
from jax.experimental.pallas import tpu as pltpu
from jax.sharding import PartitionSpec as P

ITERS = 3
EPS = 0.25
RHO = 2.0
LAM = RHO / (RHO + EPS)
EMB = 64
DEPTH = 128
PACK = 80
MIB = 1 << 20
LOW, HIGH = 1e-25, 1e30


def pieces(value):
    high = value.astype(jnp.bfloat16).astype(jnp.float32)
    rest = value - high
    mid = rest.astype(jnp.bfloat16).astype(jnp.float32)
    low = (rest - mid).astype(jnp.bfloat16).astype(jnp.float32)
    return high, mid, low


def stacked(rows, height, width):
    index = lax.broadcasted_iota(jnp.int32, (height, width), 0)
    block = jnp.zeros((height, width), jnp.float32)
    for at, row in enumerate(rows):
        if row is not None:
            block = jnp.where(index == at, row, block)
    return block


def source_static(emb_ref, pos_ref, out_ref, shift_ref):
    width = emb_ref.shape[1]
    pos = pos_ref[...]
    emb = emb_ref[...].astype(jnp.float32)
    sq = jnp.sum(emb * emb, axis=0, keepdims=True)
    shift = -(sq * (1.0 / EMB) + pos[0:1] * pos[0:1] + pos[1:2] * pos[1:2]) * (1.0 / EPS)
    pos = pos * (2.0 / EPS)
    one = jnp.ones((1, width), jnp.float32)
    extra = stacked([*pieces(pos[0:1]), *pieces(pos[1:2]), one, one, one], 16, width)
    emb = emb * (2.0 / (EMB * EPS))
    pad = jnp.zeros((DEPTH - PACK, 128), jnp.float32)
    for at in range(0, width, 128):
        block = jnp.concatenate([emb[:, at : at + 128], extra[:, at : at + 128], pad], axis=0)
        out_ref[at : at + 128, :] = block.T.astype(jnp.bfloat16)
        shift_ref[at // 128 : at // 128 + 1, :] = shift[:, at : at + 128]


def target_static(pack_ref, at, out_ref):
    width = pack_ref.shape[1]
    pack = pack_ref[...].astype(jnp.float32)
    emb, geo = pack[0:EMB], pack[EMB : EMB + 4]
    sq = jnp.sum(emb * emb, axis=0, keepdims=True)
    x, y = geo[0:1], geo[1:2]
    shift = -(sq * (1.0 / EMB) + x * x + y * y) * (1.0 / EPS)
    cut = slice(at, at + width)
    out_ref[0:EMB, cut] = pack_ref[0:EMB, :]
    out_ref[EMB:PACK, cut] = stacked([x, x, x, y, y, y], 16, width).astype(jnp.bfloat16)
    depth = lax.broadcasted_iota(jnp.int32, (DEPTH - PACK, width), 0)
    out_ref[PACK:DEPTH, cut] = jnp.where(depth < 24, 1.0, 0.0).astype(jnp.bfloat16)
    return shift, geo[2:3]


def set_source(a_ref, shift, a_s):
    above = jnp.zeros((PACK, 128), jnp.float32)
    below = jnp.zeros((DEPTH - PACK - 24, 128), jnp.float32)
    turned = jnp.concatenate([above, *pieces(shift), below], axis=0).T
    own = lax.rem(lax.broadcasted_iota(jnp.int32, (128, DEPTH), 1), 8)
    for index in range(8):
        cut = slice(index * 128, index * 128 + 128)
        a_s[cut, :] = a_ref[cut, :] + jnp.where(own == index, turned, 0.0).astype(jnp.bfloat16)


def target_parts(rows, shift):
    block = stacked([None] * 6 + [*pieces(shift)], 16, shift.shape[1])
    return (rows.astype(jnp.float32) + block).astype(jnp.bfloat16)


def set_target(b_ref, shift, b_s):
    b_s[0:EMB, :] = b_ref[0:EMB, :]
    b_s[EMB:PACK, :] = target_parts(b_ref[EMB:PACK, :], shift)
    b_s[PACK:DEPTH, :] = b_ref[PACK:DEPTH, :]


def loop_lanes(width, work):
    def step(index, carry):
        work(pl.ds(pl.multiple_of(index * 128, 128), 128))
        return carry

    lax.fori_loop(0, width // 128, step, 0)


def loop_target(b_ref, shift_of, b_s):
    def work(cut):
        b_s[0:EMB, cut] = b_ref[0:EMB, cut]
        b_s[EMB:PACK, cut] = target_parts(b_ref[EMB:PACK, cut], shift_of(cut))
        b_s[PACK:DEPTH, cut] = b_ref[PACK:DEPTH, cut]

    loop_lanes(b_ref.shape[1], work)


def over_lanes(acc_s, out_s, join):
    for index in range(8):
        out_s[index : index + 1, :] = join(acc_s[index * 128 : index * 128 + 128, :].T, axis=0, keepdims=True)


def loop_over_lanes(acc_s, out_s, join):
    def step(index, carry):
        cut = pl.ds(pl.multiple_of(index * 128, 128), 128)
        out_s[pl.ds(index, 1), :] = join(acc_s[cut, :].T, axis=0, keepdims=True)
        return carry

    lax.fori_loop(0, 8, step, 0)


def score(a, b):
    return lax.dot_general(a, b, (((1,), (0,)), ((), ())), preferred_element_type=jnp.float32)


def over_tiles(left, right, tile, work, width=None):
    width = right.shape[1] if width is None else width
    tile = min(tile, width)

    def step(index, carry):
        cut = pl.ds(pl.multiple_of(index * tile, tile), tile)
        work(cut, score(left[...], right[:, cut]))
        return carry

    lax.fori_loop(0, width // tile, step, 0)


def folded(value, join):
    part = value[:, 0:128]
    for col in range(128, value.shape[1], 128):
        part = join(part, value[:, col : col + 128])
    return part


def row_sums(left, right, acc_s, tile):
    def work(cut, value):
        acc_s[...] += folded(jnp.exp(value), jnp.add)

    over_tiles(left, right, tile, work)


def row_tops(left, right, acc_s, tile, width=None):
    def work(cut, value):
        acc_s[...] = jnp.maximum(acc_s[...], folded(value, jnp.maximum))

    over_tiles(left, right, tile, work, width)


def col_sums(left, right, out, tile):
    def work(cut, value):
        part = jnp.sum(jnp.exp(value).reshape(-1, 16, value.shape[1]), axis=0)
        out[:, cut] = jnp.sum(part, axis=0, keepdims=True)

    over_tiles(left, right, tile, work)


def col_tops(left, right, out, tile):
    def work(cut, value):
        out[:, cut] = jnp.max(value, axis=0, keepdims=True)

    over_tiles(left, right, tile, work)


def in_range(total):
    return jnp.logical_and(jnp.min(total) > LOW, jnp.max(total) < HIGH)


def static_kernel(emb_ref, pos_ref, pack_ref, a_ref, r_ref, b_ref, c_ref, w_ref, ready_ref, guess_ref, acc_ref, b_s):
    source_static(emb_ref, pos_ref, a_ref, r_ref)
    c_ref[...], w_ref[...] = target_static(pack_ref, 0, b_ref)
    set_target(b_ref, c_ref[...] + w_ref[...], b_s)
    set_source(a_ref, r_ref[...], ready_ref)
    acc_ref[...] = jnp.full(acc_ref.shape, -jnp.inf, jnp.float32)
    row_tops(ready_ref, b_s, acc_ref, 512, min(512, b_s.shape[1]))
    over_lanes(acc_ref, guess_ref, jnp.max)
    set_source(a_ref, r_ref[...] - guess_ref[...], ready_ref)
    acc_ref[...] = jnp.zeros_like(acc_ref)
    row_sums(ready_ref, b_s, acc_ref, NEAR)


def row_finish(a_ref, r_ref, near_b_ref, near_of, ready_ref, guess_ref, acc_ref, out_ref, a_s, near_s, far_s, acc_s, guess_s, total_s):
    acc_s[...] = acc_ref[...]
    row_sums(ready_ref, far_s, acc_s, FAR)
    over_lanes(acc_s, total_s, jnp.sum)
    guess_s[...] = guess_ref[...]

    @pl.when(jnp.logical_not(in_range(total_s[...])))
    def _():
        loop_target(near_b_ref, near_of, near_s)
        set_source(a_ref, r_ref[...], a_s)
        acc_s[...] = jnp.full(acc_s.shape, -jnp.inf, jnp.float32)
        row_tops(a_s, near_s, acc_s, SMALL)
        row_tops(a_s, far_s, acc_s, SMALL)
        loop_over_lanes(acc_s, guess_s, jnp.max)
        set_source(a_ref, r_ref[...] - guess_s[...], a_s)
        acc_s[...] = jnp.zeros_like(acc_s)
        row_sums(a_s, near_s, acc_s, SMALL)
        row_sums(a_s, far_s, acc_s, SMALL)
        loop_over_lanes(acc_s, total_s, jnp.sum)

    out_ref[...] = guess_s[...] + jnp.log(total_s[...])


def first_kernel(a_ref, r_ref, near_b_ref, near_c_ref, near_w_ref, pack_ref, ready_ref, guess_ref, acc_ref, out_ref, b_ref, c_ref, w_ref, a_s, near_s, far_s, *rest):
    c_ref[...], w_ref[...] = target_static(pack_ref, 0, b_ref)
    set_target(b_ref, c_ref[...] + w_ref[...], far_s)
    near_of = lambda cut: near_c_ref[:, cut] + near_w_ref[:, cut]
    row_finish(a_ref, r_ref, near_b_ref, near_of, ready_ref, guess_ref, acc_ref, out_ref, a_s, near_s, far_s, *rest)


def near_kernel(b_ref, c_ref, w_ref, lse_ref, ready_ref, acc_ref, b_s):
    set_target(b_ref, c_ref[...] + w_ref[...] - LAM * lse_ref[...], b_s)
    acc_ref[...] = jnp.zeros_like(acc_ref)
    row_sums(ready_ref, b_s, acc_ref, NEAR)


def row_kernel(a_ref, r_ref, near_b_ref, near_c_ref, near_w_ref, near_lse_ref, b_ref, c_ref, w_ref, lse_ref, ready_ref, guess_ref, acc_ref, out_ref, a_s, near_s, far_s, *rest):
    set_target(b_ref, c_ref[...] + w_ref[...] - LAM * lse_ref[...], far_s)
    near_of = lambda cut: near_c_ref[:, cut] + near_w_ref[:, cut] - LAM * near_lse_ref[:, cut]
    row_finish(a_ref, r_ref, near_b_ref, near_of, ready_ref, guess_ref, acc_ref, out_ref, a_s, near_s, far_s, *rest)


def joined(first, second):
    top = jnp.maximum(first, second)
    return top + jnp.log(jnp.exp(first - top) + jnp.exp(second - top))


def prepare_kernel(a_ref, r_ref, lse_ref, near_b_ref, near_c_ref, near_guess_ref, far_b_ref, far_c_ref, far_guess_ref, *outs):
    near_ref, far_ref, *rest = outs
    set_target(far_b_ref, far_c_ref[...] - far_guess_ref[...], far_ref)
    set_target(near_b_ref, near_c_ref[...] - near_guess_ref[...], near_ref)
    for ready_ref in rest:
        set_source(a_ref, r_ref[...] - lse_ref[...], ready_ref)


def guess_kernel(a_ref, r_ref, lse_ref, near_b_ref, near_c_ref, far_b_ref, far_c_ref, logw_ref, near_ref, far_ref, ready_ref, near_guess_ref, far_guess_ref):
    set_source(a_ref, r_ref[...] + logw_ref[...] - LAM * lse_ref[...], ready_ref)
    for b_ref, c_ref, out_ref, top_ref in (
        (near_b_ref, near_c_ref, near_ref, near_guess_ref),
        (far_b_ref, far_c_ref, far_ref, far_guess_ref),
    ):
        set_target(b_ref, c_ref[...], out_ref)
        col_tops(ready_ref, out_ref, top_ref, 512)
        out_ref[EMB:PACK, :] = target_parts(b_ref[EMB:PACK, :], c_ref[...] - top_ref[...])
    set_source(a_ref, r_ref[...] - lse_ref[...], ready_ref)


def col_finish(left, b_ref, c_ref, ready_ref, guess_ref, out_ref, b_s, guess_s, total_s):
    col_sums(left, ready_ref, total_s, COLS)
    guess_s[...] = guess_ref[...]

    @pl.when(jnp.logical_not(in_range(total_s[...])))
    def _():
        loop_target(b_ref, lambda cut: c_ref[:, cut], b_s)
        col_tops(left, b_s, guess_s, SMALL)
        loop_target(b_ref, lambda cut: c_ref[:, cut] - guess_s[:, cut], b_s)
        col_sums(left, b_s, total_s, SMALL)

    out_ref[...] = guess_s[...] + jnp.log(total_s[...])


def far_col_kernel(a_ref, r_ref, logw_ref, one_ref, two_ref, b_ref, c_ref, ready_ref, guess_ref, out_ref, f_ref, left_ref, *rest):
    lse = joined(one_ref[...], two_ref[...])
    f_ref[...] = -LAM * EPS * lse
    set_source(a_ref, r_ref[...] + logw_ref[...] - LAM * lse, left_ref)
    col_finish(left_ref, b_ref, c_ref, ready_ref, guess_ref, out_ref, *rest)


def near_col_kernel(left_ref, b_ref, c_ref, ready_ref, guess_ref, out_ref, *rest):
    col_finish(left_ref, b_ref, c_ref, ready_ref, guess_ref, out_ref, *rest)


def plan_sums(left, b_s, mass_s, pull_s, tile):
    def work(cut, value):
        plan = jnp.exp(value)
        mass_s[...] += folded(plan, jnp.add)
        pull_s[...] += lax.dot_general(
            plan.astype(jnp.bfloat16),
            b_s[0:EMB, cut],
            (((1,), (1,)), ((), ())),
            preferred_element_type=jnp.float32,
        )

    over_tiles(left, b_s, tile, work)


def plan_pass(left_ref, b_ref, c_ref, w_ref, lse_ref, b_s, mass_s, pull_s, tile):
    set_target(b_ref, c_ref[...] + w_ref[...] - LAM * lse_ref[...], b_s)
    plan_sums(left_ref, b_s, mass_s, pull_s, tile)


def near_plan_kernel(left_ref, b_ref, c_ref, w_ref, lse_ref, mass_ref, pull_ref, b_s):
    mass_ref[...] = jnp.zeros_like(mass_ref)
    pull_ref[...] = jnp.zeros_like(pull_ref)
    plan_pass(left_ref.at[0 : mass_ref.shape[0], :], b_ref, c_ref, w_ref, lse_ref, b_s, mass_ref, pull_ref, PLAN)


def plan_finish(emb_ref, begin, mass_s, pull_s, out_ref):
    for at in range(0, out_ref.shape[1], 128):
        mass = jnp.sum(mass_s[at : at + 128, :].T, axis=0, keepdims=True)
        pull = jnp.concatenate([pull_s[at : at + 128, :], jnp.zeros((128, 128 - EMB), jnp.float32)], axis=1).T
        grad = mass * emb_ref[:, begin + at : begin + at + 128].astype(jnp.float32) - pull[0:EMB, :]
        out_ref[:, at : at + 128] = grad.astype(out_ref.dtype)


def first_plan_kernel(emb_ref, left_ref, b_ref, c_ref, w_ref, lse_ref, mass_ref, pull_ref, out_ref, b_s, mass_s, pull_s):
    mass_s[...] = mass_ref[...]
    pull_s[...] = pull_ref[...]
    plan_pass(left_ref.at[0 : out_ref.shape[1], :], b_ref, c_ref, w_ref, lse_ref, b_s, mass_s, pull_s, 2 * PLAN)
    plan_finish(emb_ref, 0, mass_s, pull_s, out_ref)


def own_piece(lse_ref, g_ref):
    piece = g_ref.shape[1]
    own = lax.shift_right_logical(lax.axis_index("src"), 1) * piece
    lane = lax.broadcasted_iota(jnp.int32, lse_ref.shape, 1) - own
    kept = jnp.where(jnp.logical_and(lane >= 0, lane < piece), lse_ref[...], 0.0)
    kept = folded(kept, jnp.add)
    total = kept[:, 0:piece]
    for at in range(piece, 128, piece):
        total += kept[:, at : at + piece]
    g_ref[...] = -LAM * EPS * total


def last_plan_kernel(emb_ref, left_ref, near_b_ref, near_c_ref, near_w_ref, near_lse_ref, b_ref, c_ref, w_ref, lse_ref, out_ref, g_ref, b_s, mass_s, pull_s):
    own_piece(near_lse_ref, g_ref)
    mass_s[...] = jnp.zeros_like(mass_s)
    pull_s[...] = jnp.zeros_like(pull_s)
    begin = emb_ref.shape[1] - out_ref.shape[1]
    left = left_ref.at[begin : emb_ref.shape[1], :]
    plan_pass(left, near_b_ref, near_c_ref, near_w_ref, near_lse_ref, b_s, mass_s, pull_s, 2 * PLAN)
    plan_pass(left, b_ref, c_ref, w_ref, lse_ref, b_s, mass_s, pull_s, 2 * PLAN)
    plan_finish(emb_ref, begin, mass_s, pull_s, out_ref)


NEAR, FAR, COLS, PLAN = 1024, 2048, 1024, 512
SMALL = 128


def f32(*shape):
    return jax.ShapeDtypeStruct(shape, jnp.float32)


def bf16(*shape):
    return jax.ShapeDtypeStruct(shape, jnp.bfloat16)


def call(kernel, out_shape, scratch, name, *args, flops=10**8):
    return pl.pallas_call(
        kernel,
        out_shape=out_shape,
        scratch_shapes=[pltpu.VMEM(like.shape, like.dtype) for like in scratch],
        compiler_params=pltpu.CompilerParams(vmem_limit_bytes=32 * MIB),
        cost_estimate=pl.CostEstimate(flops=flops, bytes_accessed=2 * 10**6, transcendentals=0),
        name=name,
    )(*args)


def rounded_sum(first, second):
    total = first.astype(jnp.float32) + second.astype(jnp.float32)
    return lax.reduce_precision(total, 8, 7).astype(jnp.bfloat16)


def swapped(value, axis, mask):
    return lax.ppermute(value, axis, [(k, k ^ mask) for k in range(lax.axis_size(axis))])


def exchanged(value, join):
    value = join(value, swapped(value, "tgt", 1))
    return value, swapped(value, "tgt", 3)


def spread(block):
    size = lax.axis_size("src")
    groups = [list(range(core, size, 2)) for core in range(2)]
    block = jnp.broadcast_to(block, (size // 2,) + block.shape)
    return lax.all_to_all(block, "src", 0, 0, axis_index_groups=groups, tiled=True)


def per_device(src_emb, src_pos, src_logw, tgt_emb, tgt_pos, tgt_logw):
    piece = tgt_emb.shape[1]
    half = piece * (lax.axis_size("src") // 2)
    rows = src_emb.shape[1]
    logw = src_logw.reshape(8, rows // 8)
    pass_flops = 2 * rows * half * DEPTH
    left_like, right_like = bf16(rows, DEPTH), bf16(DEPTH, half)
    row_line, half_line, acc_like = f32(8, rows // 8), f32(1, half), f32(rows, 128)
    row_scratch = (left_like, right_like, right_like, acc_like, row_line, row_line)
    col_scratch = (right_like, half_line, half_line)

    count = EMB + 4
    own = jnp.concatenate([tgt_emb, tgt_pos, tgt_logw[None, :], tgt_logw[None, :]], 0).reshape(count * piece // 128, 128)
    own = spread(own).reshape(-1, count, piece).transpose(1, 0, 2).reshape(count, half)
    other = swapped(own, "src", 1)
    a, r, near_b, near_c, near_w, ready, guess, acc = call(
        static_kernel,
        (left_like, row_line, right_like, half_line, half_line, left_like, row_line, acc_like),
        (right_like,),
        "static_parts",
        src_emb, src_pos, own,
        flops=pass_flops,
    )
    lse, far_b, far_c, far_w = call(
        first_kernel,
        (row_line, right_like, half_line, half_line),
        row_scratch,
        "first_row_lse",
        a, r, near_b, near_c, near_w, other, ready, guess, acc,
        flops=pass_flops,
    )
    near, far = (near_b, near_c, near_w), (far_b, far_c, far_w)

    for step in range(ITERS):
        if step:
            acc = call(near_kernel, acc_like, (right_like,), "near_row_lse", *near, col, ready, flops=pass_flops)
            lse = call(
                row_kernel, row_line, row_scratch, "row_lse",
                a, r, *near, col, *far, far_col, ready, lse, acc,
                flops=pass_flops,
            )
            more = () if step == ITERS - 1 else (left_like,)
            near_ready, far_ready, *ready = call(
                prepare_kernel, (right_like, right_like, *more), (), "prepare",
                a, r, lse, near_b, near_c, mine, far_b, far_c, theirs,
            )
            ready = ready[0] if ready else None
        else:
            near_ready, far_ready, ready, mine, theirs = call(
                guess_kernel, (right_like, right_like, left_like, half_line, half_line), (), "col_guess",
                a, r, lse, near_b, near_c, far_b, far_c, logw,
                flops=2 * pass_flops,
            )
        theirs, f, left = call(
            far_col_kernel, (half_line, row_line, left_like), col_scratch, "far_col_lse",
            a, r, logw, *exchanged(lse, joined), far_b, far_c, far_ready, theirs,
            flops=pass_flops,
        )
        moved = swapped(theirs, "src", 1)
        mine = call(
            near_col_kernel, half_line, col_scratch, "near_col_lse",
            left, near_b, near_c, near_ready, mine,
            flops=pass_flops,
        )
        col = spread(joined(mine, moved).reshape(half // 128, 128))
        top = jnp.max(col, axis=0)
        col = (top + jnp.log(jnp.sum(jnp.exp(col - top), axis=0))).reshape(1, half)
        far_col = swapped(col, "src", 1)
    part = rows // 2
    sums_like = (f32(part, 128), f32(part, EMB))
    sums = call(
        near_plan_kernel, sums_like, (right_like,), "near_plan",
        left, *near, col,
        flops=pass_flops,
    )
    grad = call(
        first_plan_kernel, bf16(EMB, part), (right_like, *sums_like), "first_plan",
        src_emb, left, *far, far_col, *sums,
        flops=pass_flops,
    )
    grads = [exchanged(grad, rounded_sum)]
    grad, g_own = call(
        last_plan_kernel, (bf16(EMB, part), f32(1, piece)), (right_like, *sums_like), "last_plan",
        src_emb, left, *near, col, *far, far_col,
        flops=2 * pass_flops,
    )
    grads.append(exchanged(grad, rounded_sum))
    first, second = (jnp.concatenate(part, axis=1).astype(jnp.float32) for part in zip(*grads))
    return f.reshape(rows), g_own[0], first + second


def solution(mesh):
    placed = (
        P(None, "src"),
        P(None, "src"),
        P("src"),
        P(None, ("src", "tgt")),
        P(None, ("src", "tgt")),
        P(("src", "tgt")),
    )
    return jax.shard_map(
        per_device,
        mesh=mesh,
        in_specs=placed,
        out_specs=(P("src"), P(("src", "tgt")), P(None, "src")),
        check_vma=False,
    )
```

```python
import functools

import jax
import jax.numpy as jnp
from jax import lax
from jax.experimental import pallas as pl
from jax.experimental.pallas import tpu as pltpu
from jax.sharding import PartitionSpec as P

ITERS = 3
EPS = 0.25
RHO = 2.0
LAM = RHO / (RHO + EPS)
EMB = 64
DEPTH = 128
PACK = 80
MIB = 1 << 20
LOW, HIGH = 1e-25, 1e30


def pieces(value):
    high = value.astype(jnp.bfloat16).astype(jnp.float32)
    rest = value - high
    mid = rest.astype(jnp.bfloat16).astype(jnp.float32)
    low = (rest - mid).astype(jnp.bfloat16).astype(jnp.float32)
    return high, mid, low


def stacked(rows, height, width):
    index = lax.broadcasted_iota(jnp.int32, (height, width), 0)
    block = jnp.zeros((height, width), jnp.float32)
    for at, row in enumerate(rows):
        if row is not None:
            block = jnp.where(index == at, row, block)
    return block


def source_static(emb_ref, pos_ref, out_ref, shift_ref):
    width = emb_ref.shape[1]
    pos = pos_ref[...]
    emb = emb_ref[...].astype(jnp.float32)
    sq = jnp.sum(emb * emb, axis=0, keepdims=True)
    shift = -(sq * (1.0 / EMB) + pos[0:1] * pos[0:1] + pos[1:2] * pos[1:2]) * (1.0 / EPS)
    pos = pos * (2.0 / EPS)
    one = jnp.ones((1, width), jnp.float32)
    extra = stacked([*pieces(pos[0:1]), *pieces(pos[1:2]), one, one, one], 16, width)
    emb = emb * (2.0 / (EMB * EPS))
    pad = jnp.zeros((DEPTH - PACK, 128), jnp.float32)
    for at in range(0, width, 128):
        block = jnp.concatenate([emb[:, at : at + 128], extra[:, at : at + 128], pad], axis=0)
        out_ref[at : at + 128, :] = block.T.astype(jnp.bfloat16)
        shift_ref[at // 128 : at // 128 + 1, :] = shift[:, at : at + 128]


def target_static(pack_ref, b_ref, c_ref, w_ref):
    count, _, width = pack_ref.shape
    piece = width // 2
    for index in range(0, count, 2):
        blocks = [pack_ref[index + k].astype(jnp.float32) for k in range(2)]
        low, high = (
            jnp.concatenate([block[:, at : at + piece] for block in blocks], axis=1) for at in (0, piece)
        )
        cut = slice(index * piece, index * piece + width)
        upper, lower = low[0 : EMB // 2], high[0 : EMB // 2]
        x, y, w = low[EMB // 2 : EMB // 2 + 1], low[EMB // 2 + 1 : EMB // 2 + 2], high[EMB // 2 : EMB // 2 + 1]
        sq = jnp.sum(upper * upper + lower * lower, axis=0, keepdims=True)
        c_ref[:, cut] = -(sq * (1.0 / EMB) + x * x + y * y) * (1.0 / EPS)
        w_ref[:, cut] = w
        b_ref[0 : EMB // 2, cut] = upper.astype(jnp.bfloat16)
        b_ref[EMB // 2 : EMB, cut] = lower.astype(jnp.bfloat16)
        b_ref[EMB:PACK, cut] = stacked([x, x, x, y, y, y], PACK - EMB, width).astype(jnp.bfloat16)
    depth = lax.broadcasted_iota(jnp.int32, (DEPTH - PACK, b_ref.shape[1]), 0)
    b_ref[PACK:DEPTH, :] = jnp.where(depth < 24, 1.0, 0.0).astype(jnp.bfloat16)


def set_source(a_ref, shift, a_s):
    above = jnp.zeros((PACK, 128), jnp.float32)
    below = jnp.zeros((DEPTH - PACK - 24, 128), jnp.float32)
    turned = jnp.concatenate([above, *pieces(shift), below], axis=0).T
    own = lax.rem(lax.broadcasted_iota(jnp.int32, (128, DEPTH), 1), 8)
    for index in range(8):
        cut = slice(index * 128, index * 128 + 128)
        a_s[cut, :] = a_ref[cut, :] + jnp.where(own == index, turned, 0.0).astype(jnp.bfloat16)


def target_parts(rows, shift):
    block = stacked([None] * 6 + [*pieces(shift)], 16, shift.shape[1])
    return (rows.astype(jnp.float32) + block).astype(jnp.bfloat16)


def set_target(b_ref, shift, b_s):
    b_s[0:EMB, :] = b_ref[0:EMB, :]
    b_s[EMB:PACK, :] = target_parts(b_ref[EMB:PACK, :], shift)
    b_s[PACK:DEPTH, :] = b_ref[PACK:DEPTH, :]


def loop_lanes(width, work):
    def step(index, carry):
        work(pl.ds(pl.multiple_of(index * 128, 128), 128))
        return carry

    lax.fori_loop(0, width // 128, step, 0)


def loop_target(b_ref, shift_of, b_s):
    def work(cut):
        b_s[0:EMB, cut] = b_ref[0:EMB, cut]
        b_s[EMB:PACK, cut] = target_parts(b_ref[EMB:PACK, cut], shift_of(cut))
        b_s[PACK:DEPTH, cut] = b_ref[PACK:DEPTH, cut]

    loop_lanes(b_ref.shape[1], work)


def over_lanes(acc_s, out_s, join):
    for index in range(8):
        out_s[index : index + 1, :] = join(acc_s[index * 128 : index * 128 + 128, :].T, axis=0, keepdims=True)


def loop_over_lanes(acc_s, out_s, join):
    def step(index, carry):
        cut = pl.ds(pl.multiple_of(index * 128, 128), 128)
        out_s[pl.ds(index, 1), :] = join(acc_s[cut, :].T, axis=0, keepdims=True)
        return carry

    lax.fori_loop(0, 8, step, 0)


def score(a, b):
    return lax.dot_general(a, b, (((1,), (0,)), ((), ())), preferred_element_type=jnp.float32)


def over_tiles(left, right, tile, work, width=None):
    width = right.shape[1] if width is None else width
    tile = min(tile, width)

    def step(index, carry):
        cut = pl.ds(pl.multiple_of(index * tile, tile), tile)
        work(cut, score(left[...], right[:, cut]))
        return carry

    lax.fori_loop(0, width // tile, step, 0)


def folded(value, join):
    part = value[:, 0:128]
    for col in range(128, value.shape[1], 128):
        part = join(part, value[:, col : col + 128])
    return part


def row_sums(left, right, acc_s, tile):
    def work(cut, value):
        acc_s[...] += folded(jnp.exp(value), jnp.add)

    over_tiles(left, right, tile, work)


def row_tops(left, right, acc_s, tile, width=None):
    def work(cut, value):
        acc_s[...] = jnp.maximum(acc_s[...], folded(value, jnp.maximum))

    over_tiles(left, right, tile, work, width)


def col_sums(left, right, out, tile):
    def work(cut, value):
        part = jnp.sum(jnp.exp(value).reshape(-1, 16, value.shape[1]), axis=0)
        out[:, cut] = jnp.sum(part, axis=0, keepdims=True)

    over_tiles(left, right, tile, work)


def col_tops(left, right, out, tile):
    def work(cut, value):
        out[:, cut] = jnp.max(value, axis=0, keepdims=True)

    over_tiles(left, right, tile, work)


def in_range(total):
    return jnp.logical_and(jnp.min(total) > LOW, jnp.max(total) < HIGH)


def static_kernel(emb_ref, pos_ref, pack_ref, a_ref, r_ref, b_ref, c_ref, w_ref, ready_ref, guess_ref, acc_ref, b_s):
    source_static(emb_ref, pos_ref, a_ref, r_ref)
    target_static(pack_ref, b_ref, c_ref, w_ref)
    set_target(b_ref, c_ref[...] + w_ref[...], b_s)
    set_source(a_ref, r_ref[...], ready_ref)
    acc_ref[...] = jnp.full(acc_ref.shape, -jnp.inf, jnp.float32)
    row_tops(ready_ref, b_s, acc_ref, 512, min(512, b_s.shape[1]))
    over_lanes(acc_ref, guess_ref, jnp.max)
    set_source(a_ref, r_ref[...] - guess_ref[...], ready_ref)
    acc_ref[...] = jnp.zeros_like(acc_ref)
    row_sums(ready_ref, b_s, acc_ref, NEAR)


def row_finish(a_ref, r_ref, near_b_ref, near_of, ready_ref, guess_ref, acc_ref, out_ref, a_s, near_s, far_s, acc_s, guess_s, total_s):
    acc_s[...] = acc_ref[...]
    row_sums(ready_ref, far_s, acc_s, FAR)
    over_lanes(acc_s, total_s, jnp.sum)
    guess_s[...] = guess_ref[...]

    @pl.when(jnp.logical_not(in_range(total_s[...])))
    def _():
        loop_target(near_b_ref, near_of, near_s)
        set_source(a_ref, r_ref[...], a_s)
        acc_s[...] = jnp.full(acc_s.shape, -jnp.inf, jnp.float32)
        row_tops(a_s, near_s, acc_s, SMALL)
        row_tops(a_s, far_s, acc_s, SMALL)
        loop_over_lanes(acc_s, guess_s, jnp.max)
        set_source(a_ref, r_ref[...] - guess_s[...], a_s)
        acc_s[...] = jnp.zeros_like(acc_s)
        row_sums(a_s, near_s, acc_s, SMALL)
        row_sums(a_s, far_s, acc_s, SMALL)
        loop_over_lanes(acc_s, total_s, jnp.sum)

    out_ref[...] = guess_s[...] + jnp.log(total_s[...])


def first_kernel(a_ref, r_ref, near_b_ref, near_c_ref, near_w_ref, pack_ref, ready_ref, guess_ref, acc_ref, out_ref, b_ref, c_ref, w_ref, a_s, near_s, far_s, *rest):
    target_static(pack_ref, b_ref, c_ref, w_ref)
    set_target(b_ref, c_ref[...] + w_ref[...], far_s)
    near_of = lambda cut: near_c_ref[:, cut] + near_w_ref[:, cut]
    row_finish(a_ref, r_ref, near_b_ref, near_of, ready_ref, guess_ref, acc_ref, out_ref, a_s, near_s, far_s, *rest)


def near_kernel(b_ref, c_ref, w_ref, lse_ref, ready_ref, acc_ref, b_s):
    set_target(b_ref, c_ref[...] + w_ref[...] - LAM * lse_ref[...], b_s)
    acc_ref[...] = jnp.zeros_like(acc_ref)
    row_sums(ready_ref, b_s, acc_ref, NEAR)


def row_kernel(a_ref, r_ref, near_b_ref, near_c_ref, near_w_ref, near_lse_ref, b_ref, c_ref, w_ref, lse_ref, ready_ref, guess_ref, acc_ref, out_ref, a_s, near_s, far_s, *rest):
    set_target(b_ref, c_ref[...] + w_ref[...] - LAM * lse_ref[...], far_s)
    near_of = lambda cut: near_c_ref[:, cut] + near_w_ref[:, cut] - LAM * near_lse_ref[:, cut]
    row_finish(a_ref, r_ref, near_b_ref, near_of, ready_ref, guess_ref, acc_ref, out_ref, a_s, near_s, far_s, *rest)


def joined(first, second):
    top = jnp.maximum(first, second)
    return top + jnp.log(jnp.exp(first - top) + jnp.exp(second - top))


def prepare_kernel(a_ref, r_ref, lse_ref, near_b_ref, near_c_ref, near_guess_ref, far_b_ref, far_c_ref, far_guess_ref, *outs):
    near_ref, far_ref, *rest = outs
    set_target(far_b_ref, far_c_ref[...] - far_guess_ref[...], far_ref)
    set_target(near_b_ref, near_c_ref[...] - near_guess_ref[...], near_ref)
    for ready_ref in rest:
        set_source(a_ref, r_ref[...] - lse_ref[...], ready_ref)


def guess_kernel(a_ref, r_ref, lse_ref, near_b_ref, near_c_ref, far_b_ref, far_c_ref, logw_ref, near_ref, far_ref, ready_ref, near_guess_ref, far_guess_ref):
    set_source(a_ref, r_ref[...] + logw_ref[...] - LAM * lse_ref[...], ready_ref)
    for b_ref, c_ref, out_ref, top_ref in (
        (near_b_ref, near_c_ref, near_ref, near_guess_ref),
        (far_b_ref, far_c_ref, far_ref, far_guess_ref),
    ):
        set_target(b_ref, c_ref[...], out_ref)
        col_tops(ready_ref, out_ref, top_ref, 512)
        out_ref[EMB:PACK, :] = target_parts(b_ref[EMB:PACK, :], c_ref[...] - top_ref[...])
    set_source(a_ref, r_ref[...] - lse_ref[...], ready_ref)


def col_finish(tile, left, b_ref, c_ref, ready_ref, guess_ref, out_ref, b_s, guess_s, total_s):
    col_sums(left, ready_ref, total_s, tile)
    guess_s[...] = guess_ref[...]

    @pl.when(jnp.logical_not(in_range(total_s[...])))
    def _():
        loop_target(b_ref, lambda cut: c_ref[:, cut], b_s)
        col_tops(left, b_s, guess_s, SMALL)
        loop_target(b_ref, lambda cut: c_ref[:, cut] - guess_s[:, cut], b_s)
        col_sums(left, b_s, total_s, SMALL)

    out_ref[...] = guess_s[...] + jnp.log(total_s[...])


def far_col_kernel(a_ref, r_ref, logw_ref, one_ref, two_ref, b_ref, c_ref, ready_ref, guess_ref, out_ref, f_ref, left_ref, *rest):
    lse = joined(one_ref[...], two_ref[...])
    f_ref[...] = -LAM * EPS * lse
    set_source(a_ref, r_ref[...] + logw_ref[...] - LAM * lse, left_ref)
    col_finish(NEAR, left_ref, b_ref, c_ref, ready_ref, guess_ref, out_ref, *rest)


def near_col_kernel(left_ref, b_ref, c_ref, ready_ref, guess_ref, out_ref, *rest):
    col_finish(NEAR, left_ref, b_ref, c_ref, ready_ref, guess_ref, out_ref, *rest)


def plan_sums(left, b_s, mass_s, pull_s, tile):
    def work(cut, value):
        plan = jnp.exp(value)
        mass_s[...] += folded(plan, jnp.add)
        pull_s[...] += lax.dot_general(
            plan.astype(jnp.bfloat16),
            b_s[0:EMB, cut],
            (((1,), (1,)), ((), ())),
            preferred_element_type=jnp.float32,
        )

    over_tiles(left, b_s, tile, work)


def plan_pass(left_ref, b_ref, c_ref, w_ref, lse_ref, b_s, mass_s, pull_s, tile):
    set_target(b_ref, c_ref[...] + w_ref[...] - LAM * lse_ref[...], b_s)
    plan_sums(left_ref, b_s, mass_s, pull_s, tile)


def near_plan_kernel(left_ref, b_ref, c_ref, w_ref, lse_ref, mass_ref, pull_ref, b_s):
    mass_ref[...] = jnp.zeros_like(mass_ref)
    pull_ref[...] = jnp.zeros_like(pull_ref)
    plan_pass(left_ref.at[0 : mass_ref.shape[0], :], b_ref, c_ref, w_ref, lse_ref, b_s, mass_ref, pull_ref, PLAN)


def plan_finish(emb_ref, begin, mass_s, pull_s, out_ref):
    for at in range(0, out_ref.shape[1], 128):
        mass = jnp.sum(mass_s[at : at + 128, :].T, axis=0, keepdims=True)
        pull = jnp.concatenate([pull_s[at : at + 128, :], jnp.zeros((128, 128 - EMB), jnp.float32)], axis=1).T
        grad = mass * emb_ref[:, begin + at : begin + at + 128].astype(jnp.float32) - pull[0:EMB, :]
        out_ref[:, at : at + 128] = grad.astype(out_ref.dtype)


def first_plan_kernel(emb_ref, left_ref, b_ref, c_ref, w_ref, lse_ref, mass_ref, pull_ref, out_ref, b_s, mass_s, pull_s):
    mass_s[...] = mass_ref[...]
    pull_s[...] = pull_ref[...]
    plan_pass(left_ref.at[0 : out_ref.shape[1], :], b_ref, c_ref, w_ref, lse_ref, b_s, mass_s, pull_s, 2 * PLAN)
    plan_finish(emb_ref, 0, mass_s, pull_s, out_ref)


def own_piece(lse_ref, g_ref):
    piece = g_ref.shape[1]
    own = lax.shift_right_logical(lax.axis_index("src"), 1) * piece
    lane = lax.broadcasted_iota(jnp.int32, lse_ref.shape, 1) - own
    kept = jnp.where(jnp.logical_and(lane >= 0, lane < piece), lse_ref[...], 0.0)
    kept = folded(kept, jnp.add)
    total = kept[:, 0:piece]
    for at in range(piece, 128, piece):
        total += kept[:, at : at + piece]
    g_ref[...] = -LAM * EPS * total


def last_plan_kernel(emb_ref, left_ref, near_b_ref, near_c_ref, near_w_ref, near_lse_ref, b_ref, c_ref, w_ref, lse_ref, out_ref, g_ref, b_s, mass_s, pull_s):
    own_piece(near_lse_ref, g_ref)
    mass_s[...] = jnp.zeros_like(mass_s)
    pull_s[...] = jnp.zeros_like(pull_s)
    begin = emb_ref.shape[1] - out_ref.shape[1]
    left = left_ref.at[begin : emb_ref.shape[1], :]
    plan_pass(left, near_b_ref, near_c_ref, near_w_ref, near_lse_ref, b_s, mass_s, pull_s, 2 * PLAN)
    plan_pass(left, b_ref, c_ref, w_ref, lse_ref, b_s, mass_s, pull_s, 2 * PLAN)
    plan_finish(emb_ref, begin, mass_s, pull_s, out_ref)


NEAR, FAR, PLAN = 1024, 2048, 512
SMALL = 128


def f32(*shape):
    return jax.ShapeDtypeStruct(shape, jnp.float32)


def bf16(*shape):
    return jax.ShapeDtypeStruct(shape, jnp.bfloat16)


def call(kernel, out_shape, scratch, name, *args, flops=10**8):
    return pl.pallas_call(
        kernel,
        out_shape=out_shape,
        scratch_shapes=[pltpu.VMEM(like.shape, like.dtype) for like in scratch],
        compiler_params=pltpu.CompilerParams(vmem_limit_bytes=32 * MIB),
        cost_estimate=pl.CostEstimate(flops=flops, bytes_accessed=2 * 10**6, transcendentals=0),
        name=name,
    )(*args)


def rounded_sum(first, second):
    total = first.astype(jnp.float32) + second.astype(jnp.float32)
    return lax.reduce_precision(total, 8, 7).astype(jnp.bfloat16)


def swapped(value, axis, mask):
    return lax.ppermute(value, axis, [(k, k ^ mask) for k in range(lax.axis_size(axis))])


def exchanged(value, join):
    value = join(value, swapped(value, "tgt", 1))
    return value, swapped(value, "tgt", 3)


def spread(block):
    size = lax.axis_size("src")
    groups = [list(range(core, size, 2)) for core in range(2)]
    block = jnp.broadcast_to(block, (size // 2,) + block.shape)
    return lax.all_to_all(block, "src", 0, 0, axis_index_groups=groups, tiled=True)


def per_device(src_emb, src_pos, src_logw, tgt_emb, tgt_pos, tgt_logw):
    piece = tgt_emb.shape[1]
    half = piece * (lax.axis_size("src") // 2)
    rows = src_emb.shape[1]
    logw = src_logw.reshape(8, rows // 8)
    pass_flops = 2 * rows * half * DEPTH
    left_like, right_like = bf16(rows, DEPTH), bf16(DEPTH, half)
    row_line, half_line, acc_like = f32(8, rows // 8), f32(1, half), f32(rows, 128)
    row_scratch = (left_like, right_like, right_like, acc_like, row_line, row_line)
    col_scratch = (right_like, half_line, half_line)

    line = tgt_logw[None, :]
    own = jnp.concatenate(
        [
            jnp.concatenate([tgt_emb[0 : EMB // 2], tgt_pos], 0),
            jnp.concatenate([tgt_emb[EMB // 2 :], line, line], 0),
        ],
        1,
    )
    own = spread(own)
    other = swapped(own, "src", 1)
    a, r, near_b, near_c, near_w, ready, guess, acc = call(
        static_kernel,
        (left_like, row_line, right_like, half_line, half_line, left_like, row_line, acc_like),
        (right_like,),
        "static_parts",
        src_emb, src_pos, own,
        flops=pass_flops,
    )
    lse, far_b, far_c, far_w = call(
        first_kernel,
        (row_line, right_like, half_line, half_line),
        row_scratch,
        "first_row_lse",
        a, r, near_b, near_c, near_w, other, ready, guess, acc,
        flops=pass_flops,
    )
    near, far = (near_b, near_c, near_w), (far_b, far_c, far_w)

    for step in range(ITERS):
        if step:
            acc = call(near_kernel, acc_like, (right_like,), "near_row_lse", *near, col, ready, flops=pass_flops)
            lse = call(
                row_kernel, row_line, row_scratch, "row_lse",
                a, r, *near, col, *far, far_col, ready, lse, acc,
                flops=pass_flops,
            )
            more = () if step == ITERS - 1 else (left_like,)
            near_ready, far_ready, *ready = call(
                prepare_kernel, (right_like, right_like, *more), (), "prepare",
                a, r, lse, near_b, near_c, mine, far_b, far_c, theirs,
            )
            ready = ready[0] if ready else None
        else:
            near_ready, far_ready, ready, mine, theirs = call(
                guess_kernel, (right_like, right_like, left_like, half_line, half_line), (), "col_guess",
                a, r, lse, near_b, near_c, far_b, far_c, logw,
                flops=2 * pass_flops,
            )
        theirs, f, left = call(
            far_col_kernel, (half_line, row_line, left_like), col_scratch, "far_col_lse",
            a, r, logw, *exchanged(lse, joined), far_b, far_c, far_ready, theirs,
            flops=pass_flops,
        )
        moved = swapped(theirs, "src", 1)
        mine = call(
            near_col_kernel, half_line, col_scratch, "near_col_lse",
            left, near_b, near_c, near_ready, mine,
            flops=pass_flops,
        )
        col = spread(joined(mine, moved).reshape(half // 128, 128))
        top = jnp.max(col, axis=0)
        col = (top + jnp.log(jnp.sum(jnp.exp(col - top), axis=0))).reshape(1, half)
        far_col = swapped(col, "src", 1)
    part = rows // 2
    sums_like = (f32(part, 128), f32(part, EMB))
    sums = call(
        near_plan_kernel, sums_like, (right_like,), "near_plan",
        left, *near, col,
        flops=pass_flops,
    )
    grad = call(
        first_plan_kernel, bf16(EMB, part), (right_like, *sums_like), "first_plan",
        src_emb, left, *far, far_col, *sums,
        flops=pass_flops,
    )
    grads = [exchanged(grad, rounded_sum)]
    grad, g_own = call(
        last_plan_kernel, (bf16(EMB, part), f32(1, piece)), (right_like, *sums_like), "last_plan",
        src_emb, left, *near, col, *far, far_col,
        flops=2 * pass_flops,
    )
    grads.append(exchanged(grad, rounded_sum))
    first, second = (jnp.concatenate(part, axis=1).astype(jnp.float32) for part in zip(*grads))
    return f.reshape(rows), g_own[0], first + second


def solution(mesh):
    placed = (
        P(None, "src"),
        P(None, "src"),
        P("src"),
        P(None, ("src", "tgt")),
        P(None, ("src", "tgt")),
        P(("src", "tgt")),
    )
    return jax.shard_map(
        per_device,
        mesh=mesh,
        in_specs=placed,
        out_specs=(P("src"), P(("src", "tgt")), P(None, "src")),
        check_vma=False,
    )
```

```python
import functools

import jax
import jax.numpy as jnp
from jax import lax
from jax.experimental import pallas as pl
from jax.experimental.pallas import tpu as pltpu
from jax.sharding import PartitionSpec as P

ITERS = 3
EPS = 0.25
RHO = 2.0
LAM = RHO / (RHO + EPS)
EMB = 64
DEPTH = 128
PACK = 80
MIB = 1 << 20
LOW, HIGH = 1e-25, 1e30


def pieces(value):
    high = value.astype(jnp.bfloat16).astype(jnp.float32)
    rest = value - high
    mid = rest.astype(jnp.bfloat16).astype(jnp.float32)
    low = (rest - mid).astype(jnp.bfloat16).astype(jnp.float32)
    return high, mid, low


def stacked(rows, height, width):
    index = lax.broadcasted_iota(jnp.int32, (height, width), 0)
    block = jnp.zeros((height, width), jnp.float32)
    for at, row in enumerate(rows):
        if row is not None:
            block = jnp.where(index == at, row, block)
    return block


def source_static(emb_ref, pos_ref, out_ref, shift_ref):
    width = emb_ref.shape[1]
    pos = pos_ref[...]
    emb = emb_ref[...].astype(jnp.float32)
    sq = jnp.sum(emb * emb, axis=0, keepdims=True)
    shift = -(sq * (1.0 / EMB) + pos[0:1] * pos[0:1] + pos[1:2] * pos[1:2]) * (1.0 / EPS)
    pos = pos * (2.0 / EPS)
    one = jnp.ones((1, width), jnp.float32)
    extra = stacked([*pieces(pos[0:1]), *pieces(pos[1:2]), one, one, one], 16, width)
    emb = emb * (2.0 / (EMB * EPS))
    pad = jnp.zeros((DEPTH - PACK, 128), jnp.float32)
    for at in range(0, width, 128):
        block = jnp.concatenate([emb[:, at : at + 128], extra[:, at : at + 128], pad], axis=0)
        out_ref[at : at + 128, :] = block.T.astype(jnp.bfloat16)
        shift_ref[at // 128 : at // 128 + 1, :] = shift[:, at : at + 128]


def target_static(pack_ref, b_ref, c_ref, w_ref):
    count, _, width = pack_ref.shape
    piece = width // 2
    for index in range(0, count, 2):
        blocks = [pack_ref[index + k].astype(jnp.float32) for k in range(2)]
        low, high = (
            jnp.concatenate([block[:, at : at + piece] for block in blocks], axis=1) for at in (0, piece)
        )
        cut = slice(index * piece, index * piece + width)
        upper, lower = low[0 : EMB // 2], high[0 : EMB // 2]
        x, y, w = low[EMB // 2 : EMB // 2 + 1], low[EMB // 2 + 1 : EMB // 2 + 2], high[EMB // 2 : EMB // 2 + 1]
        sq = jnp.sum(upper * upper + lower * lower, axis=0, keepdims=True)
        c_ref[:, cut] = -(sq * (1.0 / EMB) + x * x + y * y) * (1.0 / EPS)
        w_ref[:, cut] = w
        b_ref[0 : EMB // 2, cut] = upper.astype(jnp.bfloat16)
        b_ref[EMB // 2 : EMB, cut] = lower.astype(jnp.bfloat16)
        b_ref[EMB:PACK, cut] = stacked([x, x, x, y, y, y], PACK - EMB, width).astype(jnp.bfloat16)
    depth = lax.broadcasted_iota(jnp.int32, (DEPTH - PACK, b_ref.shape[1]), 0)
    b_ref[PACK:DEPTH, :] = jnp.where(depth < 24, 1.0, 0.0).astype(jnp.bfloat16)


def set_source(a_ref, shift, a_s):
    above = jnp.zeros((PACK, 128), jnp.float32)
    below = jnp.zeros((DEPTH - PACK - 24, 128), jnp.float32)
    turned = jnp.concatenate([above, *pieces(shift), below], axis=0).T
    own = lax.rem(lax.broadcasted_iota(jnp.int32, (128, DEPTH), 1), 8)
    for index in range(8):
        cut = slice(index * 128, index * 128 + 128)
        a_s[cut, :] = a_ref[cut, :] + jnp.where(own == index, turned, 0.0).astype(jnp.bfloat16)


def target_parts(rows, shift):
    block = stacked([None] * 6 + [*pieces(shift)], 16, shift.shape[1])
    return (rows.astype(jnp.float32) + block).astype(jnp.bfloat16)


def set_target(b_ref, shift, b_s):
    b_s[0:EMB, :] = b_ref[0:EMB, :]
    b_s[EMB:PACK, :] = target_parts(b_ref[EMB:PACK, :], shift)
    b_s[PACK:DEPTH, :] = b_ref[PACK:DEPTH, :]


def loop_lanes(width, work):
    def step(index, carry):
        work(pl.ds(pl.multiple_of(index * 128, 128), 128))
        return carry

    lax.fori_loop(0, width // 128, step, 0)


def loop_target(b_ref, shift_of, b_s):
    def work(cut):
        b_s[0:EMB, cut] = b_ref[0:EMB, cut]
        b_s[EMB:PACK, cut] = target_parts(b_ref[EMB:PACK, cut], shift_of(cut))
        b_s[PACK:DEPTH, cut] = b_ref[PACK:DEPTH, cut]

    loop_lanes(b_ref.shape[1], work)


def over_lanes(acc_s, out_s, join):
    for index in range(8):
        out_s[index : index + 1, :] = join(acc_s[index * 128 : index * 128 + 128, :].T, axis=0, keepdims=True)


def loop_over_lanes(acc_s, out_s, join):
    def step(index, carry):
        cut = pl.ds(pl.multiple_of(index * 128, 128), 128)
        out_s[pl.ds(index, 1), :] = join(acc_s[cut, :].T, axis=0, keepdims=True)
        return carry

    lax.fori_loop(0, 8, step, 0)


def score(a, b):
    return lax.dot_general(a, b, (((1,), (0,)), ((), ())), preferred_element_type=jnp.float32)


def over_tiles(left, right, tile, work, width=None):
    width = right.shape[1] if width is None else width
    tile = min(tile, width)

    def step(index, carry):
        cut = pl.ds(pl.multiple_of(index * tile, tile), tile)
        work(cut, score(left[...], right[:, cut]))
        return carry

    lax.fori_loop(0, width // tile, step, 0)


def folded(value, join):
    part = value[:, 0:128]
    for col in range(128, value.shape[1], 128):
        part = join(part, value[:, col : col + 128])
    return part


def row_sums(left, right, acc_s, tile):
    def work(cut, value):
        acc_s[...] += folded(jnp.exp(value), jnp.add)

    over_tiles(left, right, tile, work)


def row_tops(left, right, acc_s, tile, width=None):
    def work(cut, value):
        acc_s[...] = jnp.maximum(acc_s[...], folded(value, jnp.maximum))

    over_tiles(left, right, tile, work, width)


def col_sums(left, right, out, tile):
    def work(cut, value):
        part = jnp.sum(jnp.exp(value).reshape(-1, 16, value.shape[1]), axis=0)
        out[:, cut] = jnp.sum(part, axis=0, keepdims=True)

    over_tiles(left, right, tile, work)


def col_tops(left, right, out, tile):
    def work(cut, value):
        out[:, cut] = jnp.max(value, axis=0, keepdims=True)

    over_tiles(left, right, tile, work)


def in_range(total):
    return jnp.logical_and(jnp.min(total) > LOW, jnp.max(total) < HIGH)


def static_kernel(emb_ref, pos_ref, pack_ref, a_ref, r_ref, b_ref, c_ref, w_ref, ready_ref, guess_ref, acc_ref, b_s):
    source_static(emb_ref, pos_ref, a_ref, r_ref)
    target_static(pack_ref, b_ref, c_ref, w_ref)
    set_target(b_ref, c_ref[...] + w_ref[...], b_s)
    set_source(a_ref, r_ref[...], ready_ref)
    acc_ref[...] = jnp.full(acc_ref.shape, -jnp.inf, jnp.float32)
    row_tops(ready_ref, b_s, acc_ref, 256, min(256, b_s.shape[1]))
    over_lanes(acc_ref, guess_ref, jnp.max)
    set_source(a_ref, r_ref[...] - guess_ref[...], ready_ref)
    acc_ref[...] = jnp.zeros_like(acc_ref)
    row_sums(ready_ref, b_s, acc_ref, NEAR)


def row_finish(a_ref, r_ref, near_b_ref, near_of, ready_ref, guess_ref, acc_ref, out_ref, a_s, near_s, far_s, acc_s, guess_s, total_s):
    acc_s[...] = acc_ref[...]
    row_sums(ready_ref, far_s, acc_s, FAR)
    over_lanes(acc_s, total_s, jnp.sum)
    guess_s[...] = guess_ref[...]

    @pl.when(jnp.logical_not(in_range(total_s[...])))
    def _():
        loop_target(near_b_ref, near_of, near_s)
        set_source(a_ref, r_ref[...], a_s)
        acc_s[...] = jnp.full(acc_s.shape, -jnp.inf, jnp.float32)
        row_tops(a_s, near_s, acc_s, SMALL)
        row_tops(a_s, far_s, acc_s, SMALL)
        loop_over_lanes(acc_s, guess_s, jnp.max)
        set_source(a_ref, r_ref[...] - guess_s[...], a_s)
        acc_s[...] = jnp.zeros_like(acc_s)
        row_sums(a_s, near_s, acc_s, SMALL)
        row_sums(a_s, far_s, acc_s, SMALL)
        loop_over_lanes(acc_s, total_s, jnp.sum)

    out_ref[...] = guess_s[...] + jnp.log(total_s[...])


def first_kernel(a_ref, r_ref, near_b_ref, near_c_ref, near_w_ref, pack_ref, ready_ref, guess_ref, acc_ref, out_ref, b_ref, c_ref, w_ref, a_s, near_s, far_s, *rest):
    target_static(pack_ref, b_ref, c_ref, w_ref)
    set_target(b_ref, c_ref[...] + w_ref[...], far_s)
    near_of = lambda cut: near_c_ref[:, cut] + near_w_ref[:, cut]
    row_finish(a_ref, r_ref, near_b_ref, near_of, ready_ref, guess_ref, acc_ref, out_ref, a_s, near_s, far_s, *rest)


def near_kernel(b_ref, c_ref, w_ref, lse_ref, ready_ref, acc_ref, b_s):
    set_target(b_ref, c_ref[...] + w_ref[...] - LAM * lse_ref[...], b_s)
    acc_ref[...] = jnp.zeros_like(acc_ref)
    row_sums(ready_ref, b_s, acc_ref, NEAR)


def row_kernel(a_ref, r_ref, near_b_ref, near_c_ref, near_w_ref, near_lse_ref, b_ref, c_ref, w_ref, lse_ref, ready_ref, guess_ref, acc_ref, out_ref, a_s, near_s, far_s, *rest):
    set_target(b_ref, c_ref[...] + w_ref[...] - LAM * lse_ref[...], far_s)
    near_of = lambda cut: near_c_ref[:, cut] + near_w_ref[:, cut] - LAM * near_lse_ref[:, cut]
    row_finish(a_ref, r_ref, near_b_ref, near_of, ready_ref, guess_ref, acc_ref, out_ref, a_s, near_s, far_s, *rest)


def joined(first, second):
    top = jnp.maximum(first, second)
    return top + jnp.log(jnp.exp(first - top) + jnp.exp(second - top))


def prepare_kernel(a_ref, r_ref, lse_ref, near_b_ref, near_c_ref, near_guess_ref, far_b_ref, far_c_ref, far_guess_ref, *outs):
    near_ref, far_ref, *rest = outs
    set_target(far_b_ref, far_c_ref[...] - far_guess_ref[...], far_ref)
    set_target(near_b_ref, near_c_ref[...] - near_guess_ref[...], near_ref)
    for ready_ref in rest:
        set_source(a_ref, r_ref[...] - lse_ref[...], ready_ref)


def guess_kernel(a_ref, r_ref, lse_ref, near_b_ref, near_c_ref, far_b_ref, far_c_ref, logw_ref, near_ref, far_ref, ready_ref, near_guess_ref, far_guess_ref):
    set_source(a_ref, r_ref[...] + logw_ref[...] - LAM * lse_ref[...], ready_ref)
    for b_ref, c_ref, out_ref, top_ref in (
        (near_b_ref, near_c_ref, near_ref, near_guess_ref),
        (far_b_ref, far_c_ref, far_ref, far_guess_ref),
    ):
        set_target(b_ref, c_ref[...], out_ref)
        col_tops(ready_ref.at[0 : ready_ref.shape[0] // 2, :], out_ref, top_ref, 1024)
        out_ref[EMB:PACK, :] = target_parts(b_ref[EMB:PACK, :], c_ref[...] - top_ref[...])
    set_source(a_ref, r_ref[...] - lse_ref[...], ready_ref)


def col_finish(tile, left, b_ref, c_ref, ready_ref, guess_ref, out_ref, b_s, guess_s, total_s):
    col_sums(left, ready_ref, total_s, tile)
    guess_s[...] = guess_ref[...]

    @pl.when(jnp.logical_not(in_range(total_s[...])))
    def _():
        loop_target(b_ref, lambda cut: c_ref[:, cut], b_s)
        col_tops(left, b_s, guess_s, SMALL)
        loop_target(b_ref, lambda cut: c_ref[:, cut] - guess_s[:, cut], b_s)
        col_sums(left, b_s, total_s, SMALL)

    out_ref[...] = guess_s[...] + jnp.log(total_s[...])


def far_col_kernel(a_ref, r_ref, logw_ref, one_ref, two_ref, b_ref, c_ref, ready_ref, guess_ref, out_ref, f_ref, left_ref, *rest):
    lse = joined(one_ref[...], two_ref[...])
    f_ref[...] = -LAM * EPS * lse
    set_source(a_ref, r_ref[...] + logw_ref[...] - LAM * lse, left_ref)
    col_finish(NEAR, left_ref, b_ref, c_ref, ready_ref, guess_ref, out_ref, *rest)


def near_col_kernel(left_ref, b_ref, c_ref, ready_ref, guess_ref, out_ref, *rest):
    col_finish(NEAR, left_ref, b_ref, c_ref, ready_ref, guess_ref, out_ref, *rest)


def plan_sums(left, b_s, mass_s, pull_s, tile):
    def work(cut, value):
        plan = jnp.exp(value)
        mass_s[...] += folded(plan, jnp.add)
        pull_s[...] += lax.dot_general(
            plan.astype(jnp.bfloat16),
            b_s[0:EMB, cut],
            (((1,), (1,)), ((), ())),
            preferred_element_type=jnp.float32,
        )

    over_tiles(left, b_s, tile, work)


def plan_pass(left_ref, b_ref, c_ref, w_ref, lse_ref, b_s, mass_s, pull_s, tile):
    set_target(b_ref, c_ref[...] + w_ref[...] - LAM * lse_ref[...], b_s)
    plan_sums(left_ref, b_s, mass_s, pull_s, tile)


def near_plan_kernel(left_ref, b_ref, c_ref, w_ref, lse_ref, mass_ref, pull_ref, b_s):
    mass_ref[...] = jnp.zeros_like(mass_ref)
    pull_ref[...] = jnp.zeros_like(pull_ref)
    plan_pass(left_ref.at[0 : mass_ref.shape[0], :], b_ref, c_ref, w_ref, lse_ref, b_s, mass_ref, pull_ref, PLAN)


def plan_finish(emb_ref, begin, mass_s, pull_s, out_ref):
    for at in range(0, out_ref.shape[1], 128):
        mass = jnp.sum(mass_s[at : at + 128, :].T, axis=0, keepdims=True)
        pull = jnp.concatenate([pull_s[at : at + 128, :], jnp.zeros((128, 128 - EMB), jnp.float32)], axis=1).T
        grad = mass * emb_ref[:, begin + at : begin + at + 128].astype(jnp.float32) - pull[0:EMB, :]
        out_ref[:, at : at + 128] = grad.astype(out_ref.dtype)


def first_plan_kernel(emb_ref, left_ref, b_ref, c_ref, w_ref, lse_ref, mass_ref, pull_ref, out_ref, b_s, mass_s, pull_s):
    mass_s[...] = mass_ref[...]
    pull_s[...] = pull_ref[...]
    plan_pass(left_ref.at[0 : out_ref.shape[1], :], b_ref, c_ref, w_ref, lse_ref, b_s, mass_s, pull_s, 2 * PLAN)
    plan_finish(emb_ref, 0, mass_s, pull_s, out_ref)


def own_piece(lse_ref, g_ref):
    piece = g_ref.shape[1]
    own = lax.shift_right_logical(lax.axis_index("src"), 1) * piece
    lane = lax.broadcasted_iota(jnp.int32, lse_ref.shape, 1) - own
    kept = jnp.where(jnp.logical_and(lane >= 0, lane < piece), lse_ref[...], 0.0)
    kept = folded(kept, jnp.add)
    total = kept[:, 0:piece]
    for at in range(piece, 128, piece):
        total += kept[:, at : at + piece]
    g_ref[...] = -LAM * EPS * total


def last_plan_kernel(emb_ref, left_ref, near_b_ref, near_c_ref, near_w_ref, near_lse_ref, b_ref, c_ref, w_ref, lse_ref, out_ref, g_ref, b_s, mass_s, pull_s):
    own_piece(near_lse_ref, g_ref)
    mass_s[...] = jnp.zeros_like(mass_s)
    pull_s[...] = jnp.zeros_like(pull_s)
    begin = emb_ref.shape[1] - out_ref.shape[1]
    left = left_ref.at[begin : emb_ref.shape[1], :]
    plan_pass(left, near_b_ref, near_c_ref, near_w_ref, near_lse_ref, b_s, mass_s, pull_s, 2 * PLAN)
    plan_pass(left, b_ref, c_ref, w_ref, lse_ref, b_s, mass_s, pull_s, 2 * PLAN)
    plan_finish(emb_ref, begin, mass_s, pull_s, out_ref)


NEAR, FAR, PLAN = 1024, 2048, 512
SMALL = 128


def f32(*shape):
    return jax.ShapeDtypeStruct(shape, jnp.float32)


def bf16(*shape):
    return jax.ShapeDtypeStruct(shape, jnp.bfloat16)


def call(kernel, out_shape, scratch, name, *args, flops=10**8):
    return pl.pallas_call(
        kernel,
        out_shape=out_shape,
        scratch_shapes=[pltpu.VMEM(like.shape, like.dtype) for like in scratch],
        compiler_params=pltpu.CompilerParams(vmem_limit_bytes=32 * MIB),
        cost_estimate=pl.CostEstimate(flops=flops, bytes_accessed=2 * 10**6, transcendentals=0),
        name=name,
    )(*args)


def rounded_sum(first, second):
    total = first.astype(jnp.float32) + second.astype(jnp.float32)
    return lax.reduce_precision(total, 8, 7).astype(jnp.bfloat16)


def swapped(value, axis, mask):
    return lax.ppermute(value, axis, [(k, k ^ mask) for k in range(lax.axis_size(axis))])


def exchanged(value, join):
    value = join(value, swapped(value, "tgt", 1))
    return value, swapped(value, "tgt", 3)


def spread(block):
    size = lax.axis_size("src")
    groups = [list(range(core, size, 2)) for core in range(2)]
    block = jnp.broadcast_to(block, (size // 2,) + block.shape)
    return lax.all_to_all(block, "src", 0, 0, axis_index_groups=groups, tiled=True)


def per_device(src_emb, src_pos, src_logw, tgt_emb, tgt_pos, tgt_logw):
    piece = tgt_emb.shape[1]
    half = piece * (lax.axis_size("src") // 2)
    rows = src_emb.shape[1]
    logw = src_logw.reshape(8, rows // 8)
    pass_flops = 2 * rows * half * DEPTH
    left_like, right_like = bf16(rows, DEPTH), bf16(DEPTH, half)
    row_line, half_line, acc_like = f32(8, rows // 8), f32(1, half), f32(rows, 128)
    row_scratch = (left_like, right_like, right_like, acc_like, row_line, row_line)
    col_scratch = (right_like, half_line, half_line)

    line = tgt_logw[None, :]
    own = jnp.concatenate(
        [
            jnp.concatenate([tgt_emb[0 : EMB // 2], tgt_pos], 0),
            jnp.concatenate([tgt_emb[EMB // 2 :], line, line], 0),
        ],
        1,
    )
    own = spread(own)
    other = swapped(own, "src", 1)
    a, r, near_b, near_c, near_w, ready, guess, acc = call(
        static_kernel,
        (left_like, row_line, right_like, half_line, half_line, left_like, row_line, acc_like),
        (right_like,),
        "static_parts",
        src_emb, src_pos, own,
        flops=pass_flops,
    )
    lse, far_b, far_c, far_w = call(
        first_kernel,
        (row_line, right_like, half_line, half_line),
        row_scratch,
        "first_row_lse",
        a, r, near_b, near_c, near_w, other, ready, guess, acc,
        flops=pass_flops,
    )
    near, far = (near_b, near_c, near_w), (far_b, far_c, far_w)

    for step in range(ITERS):
        if step:
            acc = call(near_kernel, acc_like, (right_like,), "near_row_lse", *near, col, ready, flops=pass_flops)
            lse = call(
                row_kernel, row_line, row_scratch, "row_lse",
                a, r, *near, col, *far, far_col, ready, lse, acc,
                flops=pass_flops,
            )
            more = () if step == ITERS - 1 else (left_like,)
            near_ready, far_ready, *ready = call(
                prepare_kernel, (right_like, right_like, *more), (), "prepare",
                a, r, lse, near_b, near_c, mine, far_b, far_c, theirs,
            )
            ready = ready[0] if ready else None
        else:
            near_ready, far_ready, ready, mine, theirs = call(
                guess_kernel, (right_like, right_like, left_like, half_line, half_line), (), "col_guess",
                a, r, lse, near_b, near_c, far_b, far_c, logw,
                flops=2 * pass_flops,
            )
        theirs, f, left = call(
            far_col_kernel, (half_line, row_line, left_like), col_scratch, "far_col_lse",
            a, r, logw, *exchanged(lse, joined), far_b, far_c, far_ready, theirs,
            flops=pass_flops,
        )
        moved = swapped(theirs, "src", 1)
        mine = call(
            near_col_kernel, half_line, col_scratch, "near_col_lse",
            left, near_b, near_c, near_ready, mine,
            flops=pass_flops,
        )
        col = spread(joined(mine, moved).reshape(half // 128, 128))
        top = jnp.max(col, axis=0)
        col = (top + jnp.log(jnp.sum(jnp.exp(col - top), axis=0))).reshape(1, half)
        far_col = swapped(col, "src", 1)
    part = rows // 2
    sums_like = (f32(part, 128), f32(part, EMB))
    sums = call(
        near_plan_kernel, sums_like, (right_like,), "near_plan",
        left, *near, col,
        flops=pass_flops,
    )
    grad = call(
        first_plan_kernel, bf16(EMB, part), (right_like, *sums_like), "first_plan",
        src_emb, left, *far, far_col, *sums,
        flops=pass_flops,
    )
    grads = [exchanged(grad, rounded_sum)]
    grad, g_own = call(
        last_plan_kernel, (bf16(EMB, part), f32(1, piece)), (right_like, *sums_like), "last_plan",
        src_emb, left, *near, col, *far, far_col,
        flops=2 * pass_flops,
    )
    grads.append(exchanged(grad, rounded_sum))
    first, second = (jnp.concatenate(part, axis=1).astype(jnp.float32) for part in zip(*grads))
    return f.reshape(rows), g_own[0], first + second


def solution(mesh):
    placed = (
        P(None, "src"),
        P(None, "src"),
        P("src"),
        P(None, ("src", "tgt")),
        P(None, ("src", "tgt")),
        P(("src", "tgt")),
    )
    return jax.shard_map(
        per_device,
        mesh=mesh,
        in_specs=placed,
        out_specs=(P("src"), P(("src", "tgt")), P(None, "src")),
        check_vma=False,
    )
```

```python
import functools

import jax
import jax.numpy as jnp
from jax import lax
from jax.experimental import pallas as pl
from jax.experimental.pallas import tpu as pltpu
from jax.sharding import PartitionSpec as P

ITERS = 3
EPS = 0.25
RHO = 2.0
LAM = RHO / (RHO + EPS)
EMB = 64
DEPTH = 128
PACK = 80
MIB = 1 << 20
LOW, HIGH = 1e-25, 1e30


def pieces(value):
    high = value.astype(jnp.bfloat16).astype(jnp.float32)
    rest = value - high
    mid = rest.astype(jnp.bfloat16).astype(jnp.float32)
    low = (rest - mid).astype(jnp.bfloat16).astype(jnp.float32)
    return high, mid, low


def stacked(rows, height, width):
    index = lax.broadcasted_iota(jnp.int32, (height, width), 0)
    block = jnp.zeros((height, width), jnp.float32)
    for at, row in enumerate(rows):
        if row is not None:
            block = jnp.where(index == at, row, block)
    return block


def source_static(emb_ref, pos_ref, out_ref, shift_ref):
    width = emb_ref.shape[1]
    pos = pos_ref[...]
    emb = emb_ref[...].astype(jnp.float32)
    sq = jnp.sum(emb * emb, axis=0, keepdims=True)
    shift = -(sq * (1.0 / EMB) + pos[0:1] * pos[0:1] + pos[1:2] * pos[1:2]) * (1.0 / EPS)
    pos = pos * (2.0 / EPS)
    one = jnp.ones((1, width), jnp.float32)
    extra = stacked([*pieces(pos[0:1]), *pieces(pos[1:2]), one, one, one], 16, width)
    emb = emb * (2.0 / (EMB * EPS))
    pad = jnp.zeros((DEPTH - PACK, 128), jnp.float32)
    for at in range(0, width, 128):
        block = jnp.concatenate([emb[:, at : at + 128], extra[:, at : at + 128], pad], axis=0)
        out_ref[at : at + 128, :] = block.T.astype(jnp.bfloat16)
        shift_ref[at // 128 : at // 128 + 1, :] = shift[:, at : at + 128]


def target_static(pack_ref, b_ref, c_ref, w_ref):
    count, _, width = pack_ref.shape
    piece = width // 2
    for index in range(0, count, 2):
        blocks = [pack_ref[index + k].astype(jnp.float32) for k in range(2)]
        low, high = (
            jnp.concatenate([block[:, at : at + piece] for block in blocks], axis=1) for at in (0, piece)
        )
        cut = slice(index * piece, index * piece + width)
        upper, lower = low[0 : EMB // 2], high[0 : EMB // 2]
        x, y, w = low[EMB // 2 : EMB // 2 + 1], low[EMB // 2 + 1 : EMB // 2 + 2], high[EMB // 2 : EMB // 2 + 1]
        sq = jnp.sum(upper * upper + lower * lower, axis=0, keepdims=True)
        c_ref[:, cut] = -(sq * (1.0 / EMB) + x * x + y * y) * (1.0 / EPS)
        w_ref[:, cut] = w
        b_ref[0 : EMB // 2, cut] = upper.astype(jnp.bfloat16)
        b_ref[EMB // 2 : EMB, cut] = lower.astype(jnp.bfloat16)
        b_ref[EMB:PACK, cut] = stacked([x, x, x, y, y, y], PACK - EMB, width).astype(jnp.bfloat16)
    depth = lax.broadcasted_iota(jnp.int32, (DEPTH - PACK, b_ref.shape[1]), 0)
    b_ref[PACK:DEPTH, :] = jnp.where(depth < 24, 1.0, 0.0).astype(jnp.bfloat16)


def set_source(a_ref, shift, a_s):
    above = jnp.zeros((PACK, 128), jnp.float32)
    below = jnp.zeros((DEPTH - PACK - 24, 128), jnp.float32)
    turned = jnp.concatenate([above, *pieces(shift), below], axis=0).T
    own = lax.rem(lax.broadcasted_iota(jnp.int32, (128, DEPTH), 1), 8)
    for index in range(8):
        cut = slice(index * 128, index * 128 + 128)
        a_s[cut, :] = a_ref[cut, :] + jnp.where(own == index, turned, 0.0).astype(jnp.bfloat16)


def target_parts(rows, shift):
    block = stacked([None] * 6 + [*pieces(shift)], 16, shift.shape[1])
    return (rows.astype(jnp.float32) + block).astype(jnp.bfloat16)


def set_target(b_ref, shift, b_s):
    b_s[0:EMB, :] = b_ref[0:EMB, :]
    b_s[EMB:PACK, :] = target_parts(b_ref[EMB:PACK, :], shift)
    b_s[PACK:DEPTH, :] = b_ref[PACK:DEPTH, :]


def loop_lanes(width, work):
    def step(index, carry):
        work(pl.ds(pl.multiple_of(index * 128, 128), 128))
        return carry

    lax.fori_loop(0, width // 128, step, 0)


def loop_target(b_ref, shift_of, b_s):
    def work(cut):
        b_s[0:EMB, cut] = b_ref[0:EMB, cut]
        b_s[EMB:PACK, cut] = target_parts(b_ref[EMB:PACK, cut], shift_of(cut))
        b_s[PACK:DEPTH, cut] = b_ref[PACK:DEPTH, cut]

    loop_lanes(b_ref.shape[1], work)


def over_lanes(acc_s, out_s, join):
    for index in range(8):
        out_s[index : index + 1, :] = join(acc_s[index * 128 : index * 128 + 128, :].T, axis=0, keepdims=True)


def loop_over_lanes(acc_s, out_s, join):
    def step(index, carry):
        cut = pl.ds(pl.multiple_of(index * 128, 128), 128)
        out_s[pl.ds(index, 1), :] = join(acc_s[cut, :].T, axis=0, keepdims=True)
        return carry

    lax.fori_loop(0, 8, step, 0)


def score(a, b):
    return lax.dot_general(a, b, (((1,), (0,)), ((), ())), preferred_element_type=jnp.float32)


def over_tiles(left, right, tile, work, width=None):
    width = right.shape[1] if width is None else width
    tile = min(tile, width)

    def step(index, carry):
        cut = pl.ds(pl.multiple_of(index * tile, tile), tile)
        work(cut, score(left[...], right[:, cut]))
        return carry

    lax.fori_loop(0, width // tile, step, 0)


def folded(value, join):
    part = value[:, 0:128]
    for col in range(128, value.shape[1], 128):
        part = join(part, value[:, col : col + 128])
    return part


def row_sums(left, right, acc_s, tile):
    def work(cut, value):
        acc_s[...] += folded(jnp.exp(value), jnp.add)

    over_tiles(left, right, tile, work)


def row_tops(left, right, acc_s, tile, width=None):
    def work(cut, value):
        acc_s[...] = jnp.maximum(acc_s[...], folded(value, jnp.maximum))

    over_tiles(left, right, tile, work, width)


def col_sums(left, right, out, tile):
    def work(cut, value):
        part = jnp.sum(jnp.exp(value).reshape(-1, 16, value.shape[1]), axis=0)
        out[:, cut] = jnp.sum(part, axis=0, keepdims=True)

    over_tiles(left, right, tile, work)


def col_tops(left, right, out, tile):
    def work(cut, value):
        out[:, cut] = jnp.max(value, axis=0, keepdims=True)

    over_tiles(left, right, tile, work)


def in_range(total):
    return jnp.logical_and(jnp.min(total) > LOW, jnp.max(total) < HIGH)


def static_kernel(emb_ref, pos_ref, pack_ref, a_ref, r_ref, b_ref, c_ref, w_ref, ready_ref, guess_ref, acc_ref, b_s):
    source_static(emb_ref, pos_ref, a_ref, r_ref)
    target_static(pack_ref, b_ref, c_ref, w_ref)
    set_target(b_ref, c_ref[...] + w_ref[...], b_s)
    set_source(a_ref, r_ref[...], ready_ref)
    acc_ref[...] = jnp.full(acc_ref.shape, -jnp.inf, jnp.float32)
    row_tops(ready_ref, b_s, acc_ref, 256, min(256, b_s.shape[1]))
    over_lanes(acc_ref, guess_ref, jnp.max)
    set_source(a_ref, r_ref[...] - guess_ref[...], ready_ref)
    acc_ref[...] = jnp.zeros_like(acc_ref)
    row_sums(ready_ref, b_s, acc_ref, NEAR)


def row_finish(a_ref, r_ref, near_b_ref, near_of, ready_ref, guess_ref, acc_ref, out_ref, a_s, near_s, far_s, acc_s, guess_s, total_s):
    acc_s[...] = acc_ref[...]
    row_sums(ready_ref, far_s, acc_s, FAR)
    over_lanes(acc_s, total_s, jnp.sum)
    guess_s[...] = guess_ref[...]

    @pl.when(jnp.logical_not(in_range(total_s[...])))
    def _():
        loop_target(near_b_ref, near_of, near_s)
        set_source(a_ref, r_ref[...], a_s)
        acc_s[...] = jnp.full(acc_s.shape, -jnp.inf, jnp.float32)
        row_tops(a_s, near_s, acc_s, SMALL)
        row_tops(a_s, far_s, acc_s, SMALL)
        loop_over_lanes(acc_s, guess_s, jnp.max)
        set_source(a_ref, r_ref[...] - guess_s[...], a_s)
        acc_s[...] = jnp.zeros_like(acc_s)
        row_sums(a_s, near_s, acc_s, SMALL)
        row_sums(a_s, far_s, acc_s, SMALL)
        loop_over_lanes(acc_s, total_s, jnp.sum)

    out_ref[...] = guess_s[...] + jnp.log(total_s[...])


def first_kernel(a_ref, r_ref, near_b_ref, near_c_ref, near_w_ref, pack_ref, ready_ref, guess_ref, acc_ref, out_ref, b_ref, c_ref, w_ref, a_s, near_s, far_s, *rest):
    target_static(pack_ref, b_ref, c_ref, w_ref)
    set_target(b_ref, c_ref[...] + w_ref[...], far_s)
    near_of = lambda cut: near_c_ref[:, cut] + near_w_ref[:, cut]
    row_finish(a_ref, r_ref, near_b_ref, near_of, ready_ref, guess_ref, acc_ref, out_ref, a_s, near_s, far_s, *rest)


def near_kernel(b_ref, c_ref, w_ref, lse_ref, ready_ref, acc_ref, b_s):
    set_target(b_ref, c_ref[...] + w_ref[...] - LAM * lse_ref[...], b_s)
    acc_ref[...] = jnp.zeros_like(acc_ref)
    row_sums(ready_ref, b_s, acc_ref, NEAR)


def row_kernel(a_ref, r_ref, near_b_ref, near_c_ref, near_w_ref, near_lse_ref, b_ref, c_ref, w_ref, lse_ref, ready_ref, guess_ref, acc_ref, out_ref, a_s, near_s, far_s, *rest):
    set_target(b_ref, c_ref[...] + w_ref[...] - LAM * lse_ref[...], far_s)
    near_of = lambda cut: near_c_ref[:, cut] + near_w_ref[:, cut] - LAM * near_lse_ref[:, cut]
    row_finish(a_ref, r_ref, near_b_ref, near_of, ready_ref, guess_ref, acc_ref, out_ref, a_s, near_s, far_s, *rest)


def joined(first, second):
    top = jnp.maximum(first, second)
    return top + jnp.log(jnp.exp(first - top) + jnp.exp(second - top))


def prepare_kernel(a_ref, r_ref, lse_ref, near_b_ref, near_c_ref, near_guess_ref, far_b_ref, far_c_ref, far_guess_ref, *outs):
    near_ref, far_ref, *rest = outs
    set_target(far_b_ref, far_c_ref[...] - far_guess_ref[...], far_ref)
    set_target(near_b_ref, near_c_ref[...] - near_guess_ref[...], near_ref)
    for ready_ref in rest:
        set_source(a_ref, r_ref[...] - lse_ref[...], ready_ref)


def guess_kernel(a_ref, r_ref, lse_ref, near_b_ref, near_c_ref, far_b_ref, far_c_ref, logw_ref, near_ref, far_ref, ready_ref, near_guess_ref, far_guess_ref):
    set_source(a_ref, r_ref[...] + logw_ref[...] - LAM * lse_ref[...], ready_ref)
    for b_ref, c_ref, out_ref, top_ref in (
        (near_b_ref, near_c_ref, near_ref, near_guess_ref),
        (far_b_ref, far_c_ref, far_ref, far_guess_ref),
    ):
        set_target(b_ref, c_ref[...], out_ref)
        col_tops(ready_ref.at[0 : ready_ref.shape[0] // 2, :], out_ref, top_ref, 1024)
        out_ref[EMB:PACK, :] = target_parts(b_ref[EMB:PACK, :], c_ref[...] - top_ref[...])
    set_source(a_ref, r_ref[...] - lse_ref[...], ready_ref)


def col_finish(tile, left, b_ref, c_ref, ready_ref, guess_ref, out_ref, b_s, guess_s, total_s):
    col_sums(left, ready_ref, total_s, tile)
    guess_s[...] = guess_ref[...]

    @pl.when(jnp.logical_not(in_range(total_s[...])))
    def _():
        loop_target(b_ref, lambda cut: c_ref[:, cut], b_s)
        col_tops(left, b_s, guess_s, SMALL)
        loop_target(b_ref, lambda cut: c_ref[:, cut] - guess_s[:, cut], b_s)
        col_sums(left, b_s, total_s, SMALL)

    out_ref[...] = guess_s[...] + jnp.log(total_s[...])


def far_col_kernel(a_ref, r_ref, logw_ref, one_ref, two_ref, b_ref, c_ref, ready_ref, guess_ref, out_ref, f_ref, left_ref, *rest):
    lse = joined(one_ref[...], two_ref[...])
    f_ref[...] = -LAM * EPS * lse
    set_source(a_ref, r_ref[...] + logw_ref[...] - LAM * lse, left_ref)
    col_finish(FAR, left_ref, b_ref, c_ref, ready_ref, guess_ref, out_ref, *rest)


def near_col_kernel(left_ref, b_ref, c_ref, ready_ref, guess_ref, out_ref, *rest):
    col_finish(NEAR, left_ref, b_ref, c_ref, ready_ref, guess_ref, out_ref, *rest)


def plan_sums(left, b_s, mass_s, pull_s, tile):
    def work(cut, value):
        plan = jnp.exp(value)
        mass_s[...] += folded(plan, jnp.add)
        pull_s[...] += lax.dot_general(
            plan.astype(jnp.bfloat16),
            b_s[0:EMB, cut],
            (((1,), (1,)), ((), ())),
            preferred_element_type=jnp.float32,
        )

    over_tiles(left, b_s, tile, work)


def plan_pass(left_ref, b_ref, c_ref, w_ref, lse_ref, b_s, mass_s, pull_s, tile):
    set_target(b_ref, c_ref[...] + w_ref[...] - LAM * lse_ref[...], b_s)
    plan_sums(left_ref, b_s, mass_s, pull_s, tile)


def near_plan_kernel(left_ref, b_ref, c_ref, w_ref, lse_ref, mass_ref, pull_ref, b_s):
    mass_ref[...] = jnp.zeros_like(mass_ref)
    pull_ref[...] = jnp.zeros_like(pull_ref)
    plan_pass(left_ref.at[0 : mass_ref.shape[0], :], b_ref, c_ref, w_ref, lse_ref, b_s, mass_ref, pull_ref, 2 * PLAN)


def plan_finish(emb_ref, begin, mass_s, pull_s, out_ref):
    for at in range(0, out_ref.shape[1], 128):
        mass = jnp.sum(mass_s[at : at + 128, :].T, axis=0, keepdims=True)
        pull = jnp.concatenate([pull_s[at : at + 128, :], jnp.zeros((128, 128 - EMB), jnp.float32)], axis=1).T
        grad = mass * emb_ref[:, begin + at : begin + at + 128].astype(jnp.float32) - pull[0:EMB, :]
        out_ref[:, at : at + 128] = grad.astype(out_ref.dtype)


def first_plan_kernel(emb_ref, left_ref, b_ref, c_ref, w_ref, lse_ref, mass_ref, pull_ref, out_ref, b_s, mass_s, pull_s):
    mass_s[...] = mass_ref[...]
    pull_s[...] = pull_ref[...]
    plan_pass(left_ref.at[0 : out_ref.shape[1], :], b_ref, c_ref, w_ref, lse_ref, b_s, mass_s, pull_s, 2 * PLAN)
    plan_finish(emb_ref, 0, mass_s, pull_s, out_ref)


def own_piece(lse_ref, g_ref):
    piece = g_ref.shape[1]
    own = lax.shift_right_logical(lax.axis_index("src"), 1) * piece
    lane = lax.broadcasted_iota(jnp.int32, lse_ref.shape, 1) - own
    kept = jnp.where(jnp.logical_and(lane >= 0, lane < piece), lse_ref[...], 0.0)
    kept = folded(kept, jnp.add)
    total = kept[:, 0:piece]
    for at in range(piece, 128, piece):
        total += kept[:, at : at + piece]
    g_ref[...] = -LAM * EPS * total


def last_plan_kernel(emb_ref, left_ref, near_b_ref, near_c_ref, near_w_ref, near_lse_ref, b_ref, c_ref, w_ref, lse_ref, out_ref, g_ref, b_s, mass_s, pull_s):
    own_piece(near_lse_ref, g_ref)
    mass_s[...] = jnp.zeros_like(mass_s)
    pull_s[...] = jnp.zeros_like(pull_s)
    begin = emb_ref.shape[1] - out_ref.shape[1]
    left = left_ref.at[begin : emb_ref.shape[1], :]
    plan_pass(left, near_b_ref, near_c_ref, near_w_ref, near_lse_ref, b_s, mass_s, pull_s, 2 * PLAN)
    plan_pass(left, b_ref, c_ref, w_ref, lse_ref, b_s, mass_s, pull_s, 2 * PLAN)
    plan_finish(emb_ref, begin, mass_s, pull_s, out_ref)


NEAR, FAR, PLAN = 1024, 2048, 512
SMALL = 128


def f32(*shape):
    return jax.ShapeDtypeStruct(shape, jnp.float32)


def bf16(*shape):
    return jax.ShapeDtypeStruct(shape, jnp.bfloat16)


def call(kernel, out_shape, scratch, name, *args, flops=10**8):
    return pl.pallas_call(
        kernel,
        out_shape=out_shape,
        scratch_shapes=[pltpu.VMEM(like.shape, like.dtype) for like in scratch],
        compiler_params=pltpu.CompilerParams(vmem_limit_bytes=32 * MIB),
        cost_estimate=pl.CostEstimate(flops=flops, bytes_accessed=2 * 10**6, transcendentals=0),
        name=name,
    )(*args)


def rounded_sum(first, second):
    total = first.astype(jnp.float32) + second.astype(jnp.float32)
    return lax.reduce_precision(total, 8, 7).astype(jnp.bfloat16)


def swapped(value, axis, mask):
    return lax.ppermute(value, axis, [(k, k ^ mask) for k in range(lax.axis_size(axis))])


def exchanged(value, join):
    value = join(value, swapped(value, "tgt", 1))
    return value, swapped(value, "tgt", 3)


def spread(block):
    size = lax.axis_size("src")
    groups = [list(range(core, size, 2)) for core in range(2)]
    block = jnp.broadcast_to(block, (size // 2,) + block.shape)
    return lax.all_to_all(block, "src", 0, 0, axis_index_groups=groups, tiled=True)


def per_device(src_emb, src_pos, src_logw, tgt_emb, tgt_pos, tgt_logw):
    piece = tgt_emb.shape[1]
    half = piece * (lax.axis_size("src") // 2)
    rows = src_emb.shape[1]
    logw = src_logw.reshape(8, rows // 8)
    pass_flops = 2 * rows * half * DEPTH
    left_like, right_like = bf16(rows, DEPTH), bf16(DEPTH, half)
    row_line, half_line, acc_like = f32(8, rows // 8), f32(1, half), f32(rows, 128)
    row_scratch = (left_like, right_like, right_like, acc_like, row_line, row_line)
    col_scratch = (right_like, half_line, half_line)

    line = tgt_logw[None, :]
    own = jnp.concatenate(
        [
            jnp.concatenate([tgt_emb[0 : EMB // 2], tgt_pos], 0),
            jnp.concatenate([tgt_emb[EMB // 2 :], line, line], 0),
        ],
        1,
    )
    own = spread(own)
    other = swapped(own, "src", 1)
    a, r, near_b, near_c, near_w, ready, guess, acc = call(
        static_kernel,
        (left_like, row_line, right_like, half_line, half_line, left_like, row_line, acc_like),
        (right_like,),
        "static_parts",
        src_emb, src_pos, own,
        flops=pass_flops,
    )
    lse, far_b, far_c, far_w = call(
        first_kernel,
        (row_line, right_like, half_line, half_line),
        row_scratch,
        "first_row_lse",
        a, r, near_b, near_c, near_w, other, ready, guess, acc,
        flops=pass_flops,
    )
    near, far = (near_b, near_c, near_w), (far_b, far_c, far_w)

    for step in range(ITERS):
        if step:
            acc = call(near_kernel, acc_like, (right_like,), "near_row_lse", *near, col, ready, flops=pass_flops)
            lse = call(
                row_kernel, row_line, row_scratch, "row_lse",
                a, r, *near, col, *far, far_col, ready, lse, acc,
                flops=pass_flops,
            )
            more = () if step == ITERS - 1 else (left_like,)
            near_ready, far_ready, *ready = call(
                prepare_kernel, (right_like, right_like, *more), (), "prepare",
                a, r, lse, near_b, near_c, mine, far_b, far_c, theirs,
            )
            ready = ready[0] if ready else None
        else:
            near_ready, far_ready, ready, mine, theirs = call(
                guess_kernel, (right_like, right_like, left_like, half_line, half_line), (), "col_guess",
                a, r, lse, near_b, near_c, far_b, far_c, logw,
                flops=2 * pass_flops,
            )
        theirs, f, left = call(
            far_col_kernel, (half_line, row_line, left_like), col_scratch, "far_col_lse",
            a, r, logw, *exchanged(lse, joined), far_b, far_c, far_ready, theirs,
            flops=pass_flops,
        )
        moved = swapped(theirs, "src", 1)
        mine = call(
            near_col_kernel, half_line, col_scratch, "near_col_lse",
            left, near_b, near_c, near_ready, mine,
            flops=pass_flops,
        )
        col = spread(joined(mine, moved).reshape(half // 128, 128))
        top = jnp.max(col, axis=0)
        col = (top + jnp.log(jnp.sum(jnp.exp(col - top), axis=0))).reshape(1, half)
        far_col = swapped(col, "src", 1)
    part = rows // 2
    sums_like = (f32(part, 128), f32(part, EMB))
    sums = call(
        near_plan_kernel, sums_like, (right_like,), "near_plan",
        left, *near, col,
        flops=pass_flops,
    )
    grad = call(
        first_plan_kernel, bf16(EMB, part), (right_like, *sums_like), "first_plan",
        src_emb, left, *far, far_col, *sums,
        flops=pass_flops,
    )
    grads = [exchanged(grad, rounded_sum)]
    grad, g_own = call(
        last_plan_kernel, (bf16(EMB, part), f32(1, piece)), (right_like, *sums_like), "last_plan",
        src_emb, left, *near, col, *far, far_col,
        flops=2 * pass_flops,
    )
    grads.append(exchanged(grad, rounded_sum))
    first, second = (jnp.concatenate(part, axis=1).astype(jnp.float32) for part in zip(*grads))
    return f.reshape(rows), g_own[0], first + second


def solution(mesh):
    placed = (
        P(None, "src"),
        P(None, "src"),
        P("src"),
        P(None, ("src", "tgt")),
        P(None, ("src", "tgt")),
        P(("src", "tgt")),
    )
    return jax.shard_map(
        per_device,
        mesh=mesh,
        in_specs=placed,
        out_specs=(P("src"), P(("src", "tgt")), P(None, "src")),
        check_vma=False,
    )
```

```python
import functools

import jax
import jax.numpy as jnp
from jax import lax
from jax.experimental import pallas as pl
from jax.experimental.pallas import tpu as pltpu
from jax.sharding import PartitionSpec as P

ITERS = 3
EPS = 0.25
RHO = 2.0
LAM = RHO / (RHO + EPS)
EMB = 64
DEPTH = 128
PACK = 80
MIB = 1 << 20
LOW, HIGH = 1e-25, 1e30


def pieces(value):
    high = value.astype(jnp.bfloat16).astype(jnp.float32)
    rest = value - high
    mid = rest.astype(jnp.bfloat16).astype(jnp.float32)
    low = (rest - mid).astype(jnp.bfloat16).astype(jnp.float32)
    return high, mid, low


def stacked(rows, height, width):
    index = lax.broadcasted_iota(jnp.int32, (height, width), 0)
    block = jnp.zeros((height, width), jnp.float32)
    for at, row in enumerate(rows):
        if row is not None:
            block = jnp.where(index == at, row, block)
    return block


def source_static(emb_ref, pos_ref, out_ref, shift_ref):
    width = emb_ref.shape[1]
    pos = pos_ref[...]
    emb = emb_ref[...].astype(jnp.float32)
    sq = jnp.sum(emb * emb, axis=0, keepdims=True)
    shift = -(sq * (1.0 / EMB) + pos[0:1] * pos[0:1] + pos[1:2] * pos[1:2]) * (1.0 / EPS)
    pos = pos * (2.0 / EPS)
    one = jnp.ones((1, width), jnp.float32)
    extra = stacked([*pieces(pos[0:1]), *pieces(pos[1:2]), one, one, one], 16, width)
    emb = emb * (2.0 / (EMB * EPS))
    pad = jnp.zeros((DEPTH - PACK, 128), jnp.float32)
    for at in range(0, width, 128):
        block = jnp.concatenate([emb[:, at : at + 128], extra[:, at : at + 128], pad], axis=0)
        out_ref[at : at + 128, :] = block.T.astype(jnp.bfloat16)
        shift_ref[at // 128 : at // 128 + 1, :] = shift[:, at : at + 128]


def target_static(pack_ref, b_ref, c_ref, w_ref):
    count, _, width = pack_ref.shape
    piece = width // 2
    for index in range(0, count, 2):
        blocks = [pack_ref[index + k].astype(jnp.float32) for k in range(2)]
        low, high = (
            jnp.concatenate([block[:, at : at + piece] for block in blocks], axis=1) for at in (0, piece)
        )
        cut = slice(index * piece, index * piece + width)
        upper, lower = low[0 : EMB // 2], high[0 : EMB // 2]
        x, y, w = low[EMB // 2 : EMB // 2 + 1], low[EMB // 2 + 1 : EMB // 2 + 2], high[EMB // 2 : EMB // 2 + 1]
        sq = jnp.sum(upper * upper + lower * lower, axis=0, keepdims=True)
        c_ref[:, cut] = -(sq * (1.0 / EMB) + x * x + y * y) * (1.0 / EPS)
        w_ref[:, cut] = w
        b_ref[0 : EMB // 2, cut] = upper.astype(jnp.bfloat16)
        b_ref[EMB // 2 : EMB, cut] = lower.astype(jnp.bfloat16)
        b_ref[EMB:PACK, cut] = stacked([x, x, x, y, y, y], PACK - EMB, width).astype(jnp.bfloat16)
    depth = lax.broadcasted_iota(jnp.int32, (DEPTH - PACK, b_ref.shape[1]), 0)
    b_ref[PACK:DEPTH, :] = jnp.where(depth < 24, 1.0, 0.0).astype(jnp.bfloat16)


def set_source(a_ref, shift, a_s):
    above = jnp.zeros((PACK, 128), jnp.float32)
    below = jnp.zeros((DEPTH - PACK - 24, 128), jnp.float32)
    turned = jnp.concatenate([above, *pieces(shift), below], axis=0).T
    own = lax.rem(lax.broadcasted_iota(jnp.int32, (128, DEPTH), 1), 8)
    for index in range(8):
        cut = slice(index * 128, index * 128 + 128)
        a_s[cut, :] = a_ref[cut, :] + jnp.where(own == index, turned, 0.0).astype(jnp.bfloat16)


def target_parts(rows, shift):
    block = stacked([None] * 6 + [*pieces(shift)], 16, shift.shape[1])
    return (rows.astype(jnp.float32) + block).astype(jnp.bfloat16)


def set_target(b_ref, shift, b_s):
    b_s[0:EMB, :] = b_ref[0:EMB, :]
    b_s[EMB:PACK, :] = target_parts(b_ref[EMB:PACK, :], shift)
    b_s[PACK:DEPTH, :] = b_ref[PACK:DEPTH, :]


def loop_lanes(width, work):
    def step(index, carry):
        work(pl.ds(pl.multiple_of(index * 128, 128), 128))
        return carry

    lax.fori_loop(0, width // 128, step, 0)


def loop_target(b_ref, shift_of, b_s):
    def work(cut):
        b_s[0:EMB, cut] = b_ref[0:EMB, cut]
        b_s[EMB:PACK, cut] = target_parts(b_ref[EMB:PACK, cut], shift_of(cut))
        b_s[PACK:DEPTH, cut] = b_ref[PACK:DEPTH, cut]

    loop_lanes(b_ref.shape[1], work)


def over_lanes(acc_s, out_s, join):
    for index in range(8):
        out_s[index : index + 1, :] = join(acc_s[index * 128 : index * 128 + 128, :].T, axis=0, keepdims=True)


def loop_over_lanes(acc_s, out_s, join):
    def step(index, carry):
        cut = pl.ds(pl.multiple_of(index * 128, 128), 128)
        out_s[pl.ds(index, 1), :] = join(acc_s[cut, :].T, axis=0, keepdims=True)
        return carry

    lax.fori_loop(0, 8, step, 0)


def score(a, b):
    return lax.dot_general(a, b, (((1,), (0,)), ((), ())), preferred_element_type=jnp.float32)


def over_tiles(left, right, tile, work, width=None):
    width = right.shape[1] if width is None else width
    tile = min(tile, width)

    def step(index, carry):
        cut = pl.ds(pl.multiple_of(index * tile, tile), tile)
        work(cut, score(left[...], right[:, cut]))
        return carry

    lax.fori_loop(0, width // tile, step, 0)


def folded(value, join):
    part = value[:, 0:128]
    for col in range(128, value.shape[1], 128):
        part = join(part, value[:, col : col + 128])
    return part


def row_sums(left, right, acc_s, tile):
    def work(cut, value):
        acc_s[...] += folded(jnp.exp(value), jnp.add)

    over_tiles(left, right, tile, work)


def row_tops(left, right, acc_s, tile, width=None):
    def work(cut, value):
        acc_s[...] = jnp.maximum(acc_s[...], folded(value, jnp.maximum))

    over_tiles(left, right, tile, work, width)


def col_sums(left, right, out, tile):
    def work(cut, value):
        part = jnp.sum(jnp.exp(value).reshape(-1, 16, value.shape[1]), axis=0)
        out[:, cut] = jnp.sum(part, axis=0, keepdims=True)

    over_tiles(left, right, tile, work)


def col_tops(left, right, out, tile):
    def work(cut, value):
        out[:, cut] = jnp.max(value, axis=0, keepdims=True)

    over_tiles(left, right, tile, work)


def in_range(total):
    return jnp.logical_and(jnp.min(total) > LOW, jnp.max(total) < HIGH)


def static_kernel(emb_ref, pos_ref, pack_ref, a_ref, r_ref, b_ref, c_ref, w_ref, ready_ref, guess_ref, acc_ref, b_s):
    source_static(emb_ref, pos_ref, a_ref, r_ref)
    target_static(pack_ref, b_ref, c_ref, w_ref)
    set_target(b_ref, c_ref[...] + w_ref[...], b_s)
    set_source(a_ref, r_ref[...], ready_ref)
    acc_ref[...] = jnp.full(acc_ref.shape, -jnp.inf, jnp.float32)
    row_tops(ready_ref, b_s, acc_ref, 256, min(256, b_s.shape[1]))
    over_lanes(acc_ref, guess_ref, jnp.max)
    set_source(a_ref, r_ref[...] - guess_ref[...], ready_ref)
    acc_ref[...] = jnp.zeros_like(acc_ref)
    row_sums(ready_ref, b_s, acc_ref, NEAR)


def row_finish(a_ref, r_ref, near_b_ref, near_of, ready_ref, guess_ref, acc_ref, out_ref, a_s, near_s, far_s, acc_s, guess_s, total_s):
    acc_s[...] = acc_ref[...]
    row_sums(ready_ref, far_s, acc_s, FAR)
    over_lanes(acc_s, total_s, jnp.sum)
    guess_s[...] = guess_ref[...]

    @pl.when(jnp.logical_not(in_range(total_s[...])))
    def _():
        loop_target(near_b_ref, near_of, near_s)
        set_source(a_ref, r_ref[...], a_s)
        acc_s[...] = jnp.full(acc_s.shape, -jnp.inf, jnp.float32)
        row_tops(a_s, near_s, acc_s, SMALL)
        row_tops(a_s, far_s, acc_s, SMALL)
        loop_over_lanes(acc_s, guess_s, jnp.max)
        set_source(a_ref, r_ref[...] - guess_s[...], a_s)
        acc_s[...] = jnp.zeros_like(acc_s)
        row_sums(a_s, near_s, acc_s, SMALL)
        row_sums(a_s, far_s, acc_s, SMALL)
        loop_over_lanes(acc_s, total_s, jnp.sum)

    out_ref[...] = guess_s[...] + jnp.log(total_s[...])


def first_kernel(a_ref, r_ref, near_b_ref, near_c_ref, near_w_ref, pack_ref, ready_ref, guess_ref, acc_ref, out_ref, b_ref, c_ref, w_ref, a_s, near_s, far_s, *rest):
    target_static(pack_ref, b_ref, c_ref, w_ref)
    set_target(b_ref, c_ref[...] + w_ref[...], far_s)
    near_of = lambda cut: near_c_ref[:, cut] + near_w_ref[:, cut]
    row_finish(a_ref, r_ref, near_b_ref, near_of, ready_ref, guess_ref, acc_ref, out_ref, a_s, near_s, far_s, *rest)


def near_kernel(b_ref, c_ref, w_ref, lse_ref, ready_ref, acc_ref, b_s):
    set_target(b_ref, c_ref[...] + w_ref[...] - LAM * lse_ref[...], b_s)
    acc_ref[...] = jnp.zeros_like(acc_ref)
    row_sums(ready_ref, b_s, acc_ref, NEAR)


def row_kernel(a_ref, r_ref, near_b_ref, near_c_ref, near_w_ref, near_lse_ref, b_ref, c_ref, w_ref, lse_ref, ready_ref, guess_ref, acc_ref, out_ref, a_s, near_s, far_s, *rest):
    set_target(b_ref, c_ref[...] + w_ref[...] - LAM * lse_ref[...], far_s)
    near_of = lambda cut: near_c_ref[:, cut] + near_w_ref[:, cut] - LAM * near_lse_ref[:, cut]
    row_finish(a_ref, r_ref, near_b_ref, near_of, ready_ref, guess_ref, acc_ref, out_ref, a_s, near_s, far_s, *rest)


def joined(first, second):
    top = jnp.maximum(first, second)
    return top + jnp.log(jnp.exp(first - top) + jnp.exp(second - top))


def prepare_kernel(a_ref, r_ref, lse_ref, near_b_ref, near_c_ref, near_guess_ref, far_b_ref, far_c_ref, far_guess_ref, *outs):
    near_ref, far_ref, *rest = outs
    set_target(far_b_ref, far_c_ref[...] - far_guess_ref[...], far_ref)
    set_target(near_b_ref, near_c_ref[...] - near_guess_ref[...], near_ref)
    for ready_ref in rest:
        set_source(a_ref, r_ref[...] - lse_ref[...], ready_ref)


def guess_kernel(a_ref, r_ref, lse_ref, near_b_ref, near_c_ref, far_b_ref, far_c_ref, logw_ref, near_ref, far_ref, ready_ref, near_guess_ref, far_guess_ref):
    set_source(a_ref, r_ref[...] + logw_ref[...] - LAM * lse_ref[...], ready_ref)
    for b_ref, c_ref, out_ref, top_ref in (
        (near_b_ref, near_c_ref, near_ref, near_guess_ref),
        (far_b_ref, far_c_ref, far_ref, far_guess_ref),
    ):
        set_target(b_ref, c_ref[...], out_ref)
        col_tops(ready_ref.at[0 : ready_ref.shape[0] // 2, :], out_ref, top_ref, 1024)
        out_ref[EMB:PACK, :] = target_parts(b_ref[EMB:PACK, :], c_ref[...] - top_ref[...])
    set_source(a_ref, r_ref[...] - lse_ref[...], ready_ref)


def col_finish(tile, left, b_ref, c_ref, ready_ref, guess_ref, out_ref, b_s, guess_s, total_s):
    col_sums(left, ready_ref, total_s, tile)
    guess_s[...] = guess_ref[...]

    @pl.when(jnp.logical_not(in_range(total_s[...])))
    def _():
        loop_target(b_ref, lambda cut: c_ref[:, cut], b_s)
        col_tops(left, b_s, guess_s, SMALL)
        loop_target(b_ref, lambda cut: c_ref[:, cut] - guess_s[:, cut], b_s)
        col_sums(left, b_s, total_s, SMALL)

    out_ref[...] = guess_s[...] + jnp.log(total_s[...])


def far_col_kernel(a_ref, r_ref, logw_ref, one_ref, two_ref, b_ref, c_ref, ready_ref, guess_ref, out_ref, f_ref, left_ref, *rest):
    lse = joined(one_ref[...], two_ref[...])
    f_ref[...] = -LAM * EPS * lse
    set_source(a_ref, r_ref[...] + logw_ref[...] - LAM * lse, left_ref)
    col_finish(FAR, left_ref, b_ref, c_ref, ready_ref, guess_ref, out_ref, *rest)


def near_col_kernel(left_ref, b_ref, c_ref, ready_ref, guess_ref, out_ref, *rest):
    col_finish(NEAR, left_ref, b_ref, c_ref, ready_ref, guess_ref, out_ref, *rest)


def plan_sums(left, b_s, mass_s, pull_s, tile):
    def work(cut, value):
        plan = jnp.exp(value)
        mass_s[...] += folded(plan, jnp.add)
        pull_s[...] += lax.dot_general(
            plan.astype(jnp.bfloat16),
            b_s[0:EMB, cut],
            (((1,), (1,)), ((), ())),
            preferred_element_type=jnp.float32,
        )

    over_tiles(left, b_s, tile, work)


def plan_pass(left_ref, b_ref, c_ref, w_ref, lse_ref, b_s, mass_s, pull_s, tile):
    set_target(b_ref, c_ref[...] + w_ref[...] - LAM * lse_ref[...], b_s)
    plan_sums(left_ref, b_s, mass_s, pull_s, tile)


def near_plan_kernel(left_ref, b_ref, c_ref, w_ref, lse_ref, mass_ref, pull_ref, b_s):
    mass_ref[...] = jnp.zeros_like(mass_ref)
    pull_ref[...] = jnp.zeros_like(pull_ref)
    plan_pass(left_ref.at[0 : mass_ref.shape[0], :], b_ref, c_ref, w_ref, lse_ref, b_s, mass_ref, pull_ref, 2 * PLAN)


def plan_finish(emb_ref, begin, mass_s, pull_s, out_ref):
    for at in range(0, out_ref.shape[1], 128):
        mass = jnp.sum(mass_s[at : at + 128, :].T, axis=0, keepdims=True)
        pull = jnp.concatenate([pull_s[at : at + 128, :], jnp.zeros((128, 128 - EMB), jnp.float32)], axis=1).T
        grad = mass * emb_ref[:, begin + at : begin + at + 128].astype(jnp.float32) - pull[0:EMB, :]
        out_ref[:, at : at + 128] = grad.astype(out_ref.dtype)


def first_plan_kernel(emb_ref, left_ref, b_ref, c_ref, w_ref, lse_ref, mass_ref, pull_ref, out_ref, b_s, mass_s, pull_s):
    mass_s[...] = mass_ref[...]
    pull_s[...] = pull_ref[...]
    plan_pass(left_ref.at[0 : out_ref.shape[1], :], b_ref, c_ref, w_ref, lse_ref, b_s, mass_s, pull_s, 4 * PLAN)
    plan_finish(emb_ref, 0, mass_s, pull_s, out_ref)


def own_piece(lse_ref, g_ref):
    piece = g_ref.shape[1]
    own = lax.shift_right_logical(lax.axis_index("src"), 1) * piece
    lane = lax.broadcasted_iota(jnp.int32, lse_ref.shape, 1) - own
    kept = jnp.where(jnp.logical_and(lane >= 0, lane < piece), lse_ref[...], 0.0)
    kept = folded(kept, jnp.add)
    total = kept[:, 0:piece]
    for at in range(piece, 128, piece):
        total += kept[:, at : at + piece]
    g_ref[...] = -LAM * EPS * total


def last_plan_kernel(emb_ref, left_ref, near_b_ref, near_c_ref, near_w_ref, near_lse_ref, b_ref, c_ref, w_ref, lse_ref, out_ref, g_ref, b_s, mass_s, pull_s):
    own_piece(near_lse_ref, g_ref)
    mass_s[...] = jnp.zeros_like(mass_s)
    pull_s[...] = jnp.zeros_like(pull_s)
    begin = emb_ref.shape[1] - out_ref.shape[1]
    left = left_ref.at[begin : emb_ref.shape[1], :]
    plan_pass(left, near_b_ref, near_c_ref, near_w_ref, near_lse_ref, b_s, mass_s, pull_s, 2 * PLAN)
    plan_pass(left, b_ref, c_ref, w_ref, lse_ref, b_s, mass_s, pull_s, 2 * PLAN)
    plan_finish(emb_ref, begin, mass_s, pull_s, out_ref)


NEAR, FAR, PLAN = 1024, 2048, 512
SMALL = 128


def f32(*shape):
    return jax.ShapeDtypeStruct(shape, jnp.float32)


def bf16(*shape):
    return jax.ShapeDtypeStruct(shape, jnp.bfloat16)


def call(kernel, out_shape, scratch, name, *args, flops=10**8):
    return pl.pallas_call(
        kernel,
        out_shape=out_shape,
        scratch_shapes=[pltpu.VMEM(like.shape, like.dtype) for like in scratch],
        compiler_params=pltpu.CompilerParams(vmem_limit_bytes=32 * MIB),
        cost_estimate=pl.CostEstimate(flops=flops, bytes_accessed=2 * 10**6, transcendentals=0),
        name=name,
    )(*args)


def rounded_sum(first, second):
    total = first.astype(jnp.float32) + second.astype(jnp.float32)
    return lax.reduce_precision(total, 8, 7).astype(jnp.bfloat16)


def swapped(value, axis, mask):
    return lax.ppermute(value, axis, [(k, k ^ mask) for k in range(lax.axis_size(axis))])


def exchanged(value, join):
    value = join(value, swapped(value, "tgt", 1))
    return value, swapped(value, "tgt", 3)


def spread(block):
    size = lax.axis_size("src")
    groups = [list(range(core, size, 2)) for core in range(2)]
    block = jnp.broadcast_to(block, (size // 2,) + block.shape)
    return lax.all_to_all(block, "src", 0, 0, axis_index_groups=groups, tiled=True)


def per_device(src_emb, src_pos, src_logw, tgt_emb, tgt_pos, tgt_logw):
    piece = tgt_emb.shape[1]
    half = piece * (lax.axis_size("src") // 2)
    rows = src_emb.shape[1]
    logw = src_logw.reshape(8, rows // 8)
    pass_flops = 2 * rows * half * DEPTH
    left_like, right_like = bf16(rows, DEPTH), bf16(DEPTH, half)
    row_line, half_line, acc_like = f32(8, rows // 8), f32(1, half), f32(rows, 128)
    row_scratch = (left_like, right_like, right_like, acc_like, row_line, row_line)
    col_scratch = (right_like, half_line, half_line)

    line = tgt_logw[None, :]
    own = jnp.concatenate(
        [
            jnp.concatenate([tgt_emb[0 : EMB // 2], tgt_pos], 0),
            jnp.concatenate([tgt_emb[EMB // 2 :], line, line], 0),
        ],
        1,
    )
    own = spread(own)
    other = swapped(own, "src", 1)
    a, r, near_b, near_c, near_w, ready, guess, acc = call(
        static_kernel,
        (left_like, row_line, right_like, half_line, half_line, left_like, row_line, acc_like),
        (right_like,),
        "static_parts",
        src_emb, src_pos, own,
        flops=pass_flops,
    )
    lse, far_b, far_c, far_w = call(
        first_kernel,
        (row_line, right_like, half_line, half_line),
        row_scratch,
        "first_row_lse",
        a, r, near_b, near_c, near_w, other, ready, guess, acc,
        flops=pass_flops,
    )
    near, far = (near_b, near_c, near_w), (far_b, far_c, far_w)

    for step in range(ITERS):
        if step:
            acc = call(near_kernel, acc_like, (right_like,), "near_row_lse", *near, col, ready, flops=pass_flops)
            lse = call(
                row_kernel, row_line, row_scratch, "row_lse",
                a, r, *near, col, *far, far_col, ready, lse, acc,
                flops=pass_flops,
            )
            more = () if step == ITERS - 1 else (left_like,)
            near_ready, far_ready, *ready = call(
                prepare_kernel, (right_like, right_like, *more), (), "prepare",
                a, r, lse, near_b, near_c, mine, far_b, far_c, theirs,
            )
            ready = ready[0] if ready else None
        else:
            near_ready, far_ready, ready, mine, theirs = call(
                guess_kernel, (right_like, right_like, left_like, half_line, half_line), (), "col_guess",
                a, r, lse, near_b, near_c, far_b, far_c, logw,
                flops=2 * pass_flops,
            )
        theirs, f, left = call(
            far_col_kernel, (half_line, row_line, left_like), col_scratch, "far_col_lse",
            a, r, logw, *exchanged(lse, joined), far_b, far_c, far_ready, theirs,
            flops=pass_flops,
        )
        moved = swapped(theirs, "src", 1)
        mine = call(
            near_col_kernel, half_line, col_scratch, "near_col_lse",
            left, near_b, near_c, near_ready, mine,
            flops=pass_flops,
        )
        col = spread(joined(mine, moved).reshape(half // 128, 128))
        top = jnp.max(col, axis=0)
        col = (top + jnp.log(jnp.sum(jnp.exp(col - top), axis=0))).reshape(1, half)
        far_col = swapped(col, "src", 1)
    part = rows // 2
    sums_like = (f32(part, 128), f32(part, EMB))
    sums = call(
        near_plan_kernel, sums_like, (right_like,), "near_plan",
        left, *near, col,
        flops=pass_flops,
    )
    grad = call(
        first_plan_kernel, bf16(EMB, part), (right_like, *sums_like), "first_plan",
        src_emb, left, *far, far_col, *sums,
        flops=pass_flops,
    )
    grads = [exchanged(grad, rounded_sum)]
    grad, g_own = call(
        last_plan_kernel, (bf16(EMB, part), f32(1, piece)), (right_like, *sums_like), "last_plan",
        src_emb, left, *near, col, *far, far_col,
        flops=2 * pass_flops,
    )
    grads.append(exchanged(grad, rounded_sum))
    first, second = (jnp.concatenate(part, axis=1).astype(jnp.float32) for part in zip(*grads))
    return f.reshape(rows), g_own[0], first + second


def solution(mesh):
    placed = (
        P(None, "src"),
        P(None, "src"),
        P("src"),
        P(None, ("src", "tgt")),
        P(None, ("src", "tgt")),
        P(("src", "tgt")),
    )
    return jax.shard_map(
        per_device,
        mesh=mesh,
        in_specs=placed,
        out_specs=(P("src"), P(("src", "tgt")), P(None, "src")),
        check_vma=False,
    )
```
